32 devices in a mesh: leaf: 2 (over core), row: 4 (over y, x), col: 4 (over z).
Axes of the slice: x: 2, y: 2, z: 4, core: 2. Of those that a mesh axis runs over, the one named last changes fastest.
Arguments:
- rhs: bfloat16 [7680, 512], P(('leaf', 'row'), 'col'), may hold values from -6 to 6
- pivot_inverse: bfloat16 [7680, 2560], P('leaf', 'row'), may hold values from -0.125 to 0.125
- panel: bfloat16 [3072, 2560], P('leaf', 'row'), may hold values from -0.0625 to 0.0625
- live: int32 [3], replicated, may hold values from 10 to 20, as said below
- parent_map: int32 [2, 12], replicated, may hold values from 0 to 19, as said below
Outputs:
- forward_solution: bfloat16 [7680, 512], P(('leaf', 'row'), 'col')
- solution: bfloat16 [7680, 512], P(('leaf', 'row'), 'col')
The draws below stay inside these ranges and needn't reach their ends.
Inputs may be any that keep to these rules, and one draw needn't show every extreme that they name: `live`: the root front (last index) is full, 20 blocks. `parent_map`: within one front's row the parent blocks are distinct.
All inputs are finite; a program needn't handle non-finite values.
Results may differ from the reference program's by a relative error of at most 0.012.
Values may be sent and summed in bfloat16 or wider, within the bound.
No kernel may reach another device: no remote copies, remote signals or barrier semaphores. Data moves between devices by JAX's collectives and lax.ppermute only.
A program may use at most 64 MiB of HBM per device.

```python
import jax
import jax.numpy as jnp

F = 2560
E = 1536
R = 512
DEPTH = 1
FRONTS = 3
CHILDREN = 2
DPIECE = 3840
WPIECE = 1536
VPIECE = 960
N_LEAF = 2
N_ROW = 4


def draw_live(key, part):
    counts = jax.random.randint(key, (FRONTS,), F // 256, F // 128 + 1)
    return counts.at[FRONTS - 1].set(F // 128).astype(jnp.int32)


def draw_parent_map(key, part):
    row_keys = jax.random.split(key, CHILDREN)

    def one_row(sub_key):
        return jax.random.permutation(sub_key, F // 128)[:E // 128]
    return jax.vmap(one_row)(row_keys).astype(jnp.int32)


def levels(stream_key, dims, shards, low, largest):
    def one(position, parts):
        heights = jax.random.uniform(jax.random.fold_in(jax.random.fold_in(stream_key, 6), position), (parts,), jnp.float32, low / len(shards), largest / len(shards))
        return jnp.repeat(jnp.exp(heights), dims[position] // parts).reshape((-1,) + (1,) * (len(dims) - position - 1))

    factor_of = one(*shards[0])
    for cut in shards[1:]:
        factor_of = factor_of * one(*cut)
    return factor_of


def bell_draw(rng, dims, spread, reach, cuts=(), kind=jnp.bfloat16):
    array = jax.random.normal(rng, dims, jnp.float32) * spread
    if len(cuts) > 0:
        array = levels(rng, dims, cuts, -0.22, 0.18) * array
    return jnp.clip(array, min=-reach, max=reach).astype(kind)


def setup_inputs(seed: int = 0) -> dict:
    arg_keys = jax.random.split(jax.random.key(seed), 6)
    return {
        "rhs": bell_draw(arg_keys[0], (N_LEAF * N_ROW * VPIECE, R), 1.0, 6.0, ((0, 8), (1, 4))),
        "pivot_inverse": bell_draw(arg_keys[1], (N_LEAF * DPIECE, F), F ** -0.5, 0.125, ((0, 2), (1, 4))),
        "panel": bell_draw(arg_keys[2], (N_LEAF * WPIECE, F), (4 * F) ** -0.5, 0.0625, ((0, 2), (1, 4))),
        "live": draw_live(jax.random.fold_in(arg_keys[5], 71), 0),
        "parent_map": draw_parent_map(jax.random.fold_in(arg_keys[5], 71), 0),
    }


def to_front(group_block):
    count_g, total_rows, row_width = group_block.shape
    piece_rows = total_rows // N_ROW
    return group_block.reshape(count_g, N_ROW, piece_rows, row_width).transpose(1, 0, 2, 3).reshape(count_g * total_rows, row_width)


def from_front(full_block, groups):
    total_rows, row_width = full_block.shape
    piece_rows = total_rows // (N_ROW * groups)
    return full_block.reshape(N_ROW, groups, piece_rows, row_width).transpose(1, 0, 2, 3)


def block_onehot(mapping):
    return (jnp.arange(F // 128, dtype=jnp.int32)[:, None] == mapping[None, :]).astype(jnp.float32)


def reference(rhs, pivot_inverse, panel, live, parent_map):
    vectors = rhs.reshape(N_LEAF, N_ROW, VPIECE, R)
    pivots = pivot_inverse.reshape(N_LEAF, DPIECE, F)
    panels = panel.reshape(N_LEAF, WPIECE, F)
    forward_out = jnp.zeros((N_LEAF, N_ROW, VPIECE, R), jnp.bfloat16)
    backward_out = jnp.zeros((N_LEAF, N_ROW, VPIECE, R), jnp.bfloat16)
    layout = []
    vec_off, piv_off, pan_off, front_base = 0, 0, 0, 0
    for level_no in range(DEPTH + 1):
        groups = 2 ** level_no
        layout.append((groups, vec_off, piv_off, pan_off, front_base))
        vec_off += F // (N_ROW * groups)
        piv_off += F // groups
        pan_off += E // groups
        front_base += N_LEAF // groups
    updates = {}
    forward_values = {}
    masks = {}
    for level_no in range(DEPTH + 1):
        groups, vec_off, piv_off, pan_off, front_base = layout[level_no]
        piece_rows = F // (N_ROW * groups)
        for front_no in range(N_LEAF // groups):
            lower_g = front_no * groups
            upper_g = lower_g + groups
            right_side = to_front(vectors[lower_g:upper_g, :, vec_off:vec_off + piece_rows].reshape(groups, N_ROW * piece_rows, R))
            if level_no > 0:
                child_base = layout[level_no - 1][4]
                incoming = jnp.zeros((F, R), jnp.float32)
                for side_no in range(2):
                    child_no = 2 * front_no + side_no
                    onehot = block_onehot(parent_map[child_base + child_no])
                    child_update = updates[(level_no - 1, child_no)].astype(jnp.float32).reshape(E // 128, 128, R)
                    incoming = incoming + jnp.einsum("ke,eab->kab", onehot, child_update).reshape(F, R)
                right_side = (right_side.astype(jnp.float32) - incoming).astype(jnp.bfloat16)
            live_mask = (jnp.arange(F, dtype=jnp.int32) < live[front_base + front_no] * 128)[:, None]
            masks[(level_no, front_no)] = live_mask
            masked = jnp.where(live_mask, right_side, jnp.zeros_like(right_side))
            diag_block = to_front(pivots[lower_g:upper_g, piv_off:piv_off + F // groups])
            product = jnp.dot(diag_block, masked, preferred_element_type=jnp.float32)
            forward_value = jnp.where(live_mask, product, 0.0).astype(jnp.bfloat16)
            forward_values[(level_no, front_no)] = forward_value
            if level_no < DEPTH:
                off_block = to_front(panels[lower_g:upper_g, pan_off:pan_off + E // groups])
                updates[(level_no, front_no)] = jnp.dot(off_block, masked, preferred_element_type=jnp.float32).astype(jnp.bfloat16)
            forward_out = forward_out.at[lower_g:upper_g, :, vec_off:vec_off + piece_rows].set(from_front(forward_value, groups))
    solved = {}
    for level_no in reversed(range(DEPTH + 1)):
        groups, vec_off, piv_off, pan_off, front_base = layout[level_no]
        piece_rows = F // (N_ROW * groups)
        for front_no in range(N_LEAF // groups):
            lower_g = front_no * groups
            upper_g = lower_g + groups
            diag_block = to_front(pivots[lower_g:upper_g, piv_off:piv_off + F // groups])
            value = jnp.dot(diag_block.T, forward_values[(level_no, front_no)], preferred_element_type=jnp.float32)
            if level_no < DEPTH:
                parent_value = solved[(level_no + 1, front_no // 2)].astype(jnp.float32).reshape(F // 128, 128, R)
                onehot = block_onehot(parent_map[front_base + front_no])
                taken_rows = jnp.einsum("ke,kab->eab", onehot, parent_value).reshape(E, R).astype(jnp.bfloat16)
                off_block = to_front(panels[lower_g:upper_g, pan_off:pan_off + E // groups])
                value = value - jnp.dot(off_block.T, taken_rows, preferred_element_type=jnp.float32)
            result = jnp.where(masks[(level_no, front_no)], value, 0.0).astype(jnp.bfloat16)
            solved[(level_no, front_no)] = result
            backward_out = backward_out.at[lower_g:upper_g, :, vec_off:vec_off + piece_rows].set(from_front(result, groups))
    return forward_out.reshape(N_LEAF * N_ROW * VPIECE, R), backward_out.reshape(N_LEAF * N_ROW * VPIECE, R)
```

```python
import functools

import jax
import jax.numpy as jnp
from jax import lax
from jax.experimental import pallas as pl
from jax.experimental.pallas import tpu as pltpu
from jax.sharding import PartitionSpec as P

F = 2560
E = 1536


def from_partner(block, axis, apart):
    count = lax.axis_size(axis)
    route = []
    for low in range(count):
        high = low | 1 << apart
        if high != low and high < count:
            route += [(low, high), (high, low)]
    return lax.ppermute(block, axis, route)


def doubling(stacked, bit_count, leaf_pos, swapper):
    for bit_no in range(bit_count):
        partner = swapper(stacked, bit_no)
        upper_half = jnp.right_shift(leaf_pos, bit_no) % 2 == 1
        stacked = jnp.where(
            upper_half,
            jnp.concatenate([partner, stacked], 0),
            jnp.concatenate([stacked, partner], 0),
        )
    return stacked


def halving(partial_value, bit_count, leaf_pos, swapper):
    for bit_no in reversed(range(bit_count)):
        halves = partial_value.reshape((2, partial_value.shape[0] // 2) + partial_value.shape[1:])
        upper_half = jnp.right_shift(leaf_pos, bit_no) % 2 == 1
        kept_half = jnp.where(upper_half, halves[1], halves[0])
        sent_half = jnp.where(upper_half, halves[0], halves[1])
        partial_value = kept_half + swapper(sent_half, bit_no)
    return partial_value[0]


def to_front(group_block, row_count):
    count_g, total_rows, row_width = group_block.shape
    piece_rows = total_rows // row_count
    return (
        group_block.reshape(count_g, row_count, piece_rows, row_width)
        .transpose(1, 0, 2, 3)
        .reshape(count_g * total_rows, row_width)
    )


def block_onehot(mapping):
    return (jnp.arange(F // 128, dtype=jnp.int32)[:, None] == mapping[None, :]).astype(jnp.bfloat16)


def pivot_sum(diag_block, quarter_rows):
    return lax.psum_scatter(
        jnp.dot(diag_block, quarter_rows, preferred_element_type=jnp.float32).astype(jnp.bfloat16),
        "row",
        scatter_dimension=0,
        tiled=True,
    ).astype(jnp.float32)


def quarter_swap(values, bit_no):
    return from_partner(values, "leaf", bit_no)


def update_swap(values, bit_no):
    return from_partner(values, "leaf", bit_no)


def parent_swap(values, bit_no):
    return from_partner(values, "leaf", bit_no)


def reduce_swap(values, bit_no):
    return from_partner(values.astype(jnp.bfloat16), "leaf", bit_no).astype(values.dtype)


def deep_tree(rhs, pivot_inverse, panel, live, parent_map):
    leaves = lax.axis_size("leaf")
    row_count = lax.axis_size("row")
    tree_depth = leaves.bit_length() - 1
    leaf_pos = lax.axis_index("leaf")
    row_pos = lax.axis_index("row")
    columns = rhs.shape[1]
    quarter = F // row_count
    parent_blocks = F // 128
    child_blocks = E // 128
    layout = []
    vec_off, piv_off, pan_off, front_base = (0, 0, 0, 0)
    for level_no in range(tree_depth + 1):
        groups = 2**level_no
        layout.append((groups, vec_off, piv_off, pan_off, front_base))
        vec_off += F // (row_count * groups)
        piv_off += F // groups
        pan_off += E // groups
        front_base += leaves // groups
    forward_parts = []
    live_masks = []
    incoming = None
    for level_no in range(tree_depth + 1):
        groups, vec_off, piv_off, pan_off, front_base = layout[level_no]
        piece_rows = F // (row_count * groups)
        panel_rows = E // (row_count * groups)
        inner_pos = leaf_pos % groups
        front_no = jnp.right_shift(leaf_pos, level_no)
        live_rows = lax.dynamic_index_in_dim(live, front_base + front_no, 0, keepdims=False) * 128
        first_row = (row_pos * groups + inner_pos) * piece_rows
        live_mask = (first_row + jnp.arange(piece_rows, dtype=jnp.int32) < live_rows)[:, None]
        live_masks.append(live_mask)
        right_side = rhs[vec_off : vec_off + piece_rows]
        if incoming is not None:
            right_side = (right_side.astype(jnp.float32) - incoming).astype(jnp.bfloat16)
        masked = jnp.where(live_mask, right_side, jnp.zeros_like(right_side))
        quarter_rows = doubling(masked[None], level_no, leaf_pos, quarter_swap).reshape(
            quarter, columns
        )
        diag_block = pivot_inverse[piv_off : piv_off + F // groups]
        if level_no < tree_depth:
            off_block = panel[pan_off : pan_off + E // groups]
            forward_value = pivot_sum(diag_block, quarter_rows)
            update_rows = lax.psum(
                jnp.dot(off_block, quarter_rows, preferred_element_type=jnp.float32), "row"
            ).astype(jnp.bfloat16)
        else:
            forward_value = pivot_sum(diag_block, quarter_rows)
        forward_parts.append(jnp.where(live_mask, forward_value, 0.0).astype(jnp.bfloat16))
        if level_no < tree_depth:
            gathered = doubling(update_rows[None], level_no + 1, leaf_pos, update_swap)
            parent_front = jnp.right_shift(leaf_pos, level_no + 1)
            assembled = jnp.zeros((parent_blocks, 128, columns), jnp.float32)
            for side_no in range(2):
                child_update = to_front(
                    gathered[side_no * groups : (side_no + 1) * groups], row_count
                )
                mapping = lax.dynamic_index_in_dim(
                    parent_map, front_base + 2 * parent_front + side_no, 0, keepdims=False
                )
                assembled = assembled + jnp.einsum(
                    "ke,eab->kab",
                    block_onehot(mapping),
                    child_update.reshape(child_blocks, 128, columns),
                    preferred_element_type=jnp.float32,
                )
            parent_groups = 2 * groups
            parent_rows = F // (row_count * parent_groups)
            parent_first = (row_pos * parent_groups + leaf_pos % parent_groups) * parent_rows
            incoming = lax.dynamic_slice_in_dim(
                assembled.reshape(F, columns), parent_first, parent_rows, 0
            )
    backward_parts = [None] * (tree_depth + 1)
    parent_value = None
    for level_no in reversed(range(tree_depth + 1)):
        groups, vec_off, piv_off, pan_off, front_base = layout[level_no]
        piece_rows = F // (row_count * groups)
        panel_rows = E // (row_count * groups)
        inner_pos = leaf_pos % groups
        front_no = jnp.right_shift(leaf_pos, level_no)
        diag_block = pivot_inverse[piv_off : piv_off + F // groups]
        own_piece = forward_parts[level_no]
        if level_no == tree_depth:
            own_rows = lax.all_gather(own_piece, "row", axis=0, tiled=True)
            partial_value = jnp.einsum(
                "ik,ia->ka", diag_block, own_rows, preferred_element_type=jnp.float32
            )
        else:
            own_rows, parent_gathered = (
                lax.all_gather(own_piece, "row", axis=0, tiled=True),
                lax.all_gather(parent_value, "row", axis=0, tiled=True),
            )
            whole_parent = doubling(parent_gathered[None], level_no + 1, leaf_pos, parent_swap)
            parent_full = to_front(whole_parent, row_count)
            mapping = lax.dynamic_index_in_dim(parent_map, front_base + front_no, 0, keepdims=False)
            taken_rows = jnp.einsum(
                "ke,kab->eab",
                block_onehot(mapping),
                parent_full.reshape(parent_blocks, 128, columns),
                preferred_element_type=jnp.float32,
            ).astype(jnp.bfloat16)
            taken_rows = lax.dynamic_index_in_dim(
                taken_rows.reshape(row_count, groups, panel_rows, columns),
                inner_pos,
                1,
                keepdims=False,
            ).reshape(row_count * panel_rows, columns)
            off_block = panel[pan_off : pan_off + E // groups]
            partial_value = jnp.einsum(
                "ik,ia->ka", diag_block, own_rows, preferred_element_type=jnp.float32
            ) - jnp.einsum("ik,ia->ka", off_block, taken_rows, preferred_element_type=jnp.float32)
        if level_no == 0:
            reduced = partial_value
        else:
            reduced = halving(
                partial_value.reshape(groups, piece_rows, columns), level_no, leaf_pos, reduce_swap
            )
        parent_value = jnp.where(live_masks[level_no], reduced, 0.0).astype(jnp.bfloat16)
        backward_parts[level_no] = parent_value
    return (jnp.concatenate(forward_parts, 0), jnp.concatenate(backward_parts, 0))


B = 128
VMEM = pl.BlockSpec(memory_space=pltpu.VMEM)
SMEM = pl.BlockSpec(memory_space=pltpu.SMEM)
ANY = pl.BlockSpec(memory_space=pl.ANY)
BF = jnp.bfloat16
F32 = jnp.float32


def bf16(rows, columns):
    return jax.ShapeDtypeStruct((rows, columns), BF)


def call(body, out_shape, in_specs, scratch, flops, bytes_moved):
    return pl.pallas_call(
        body,
        out_shape=out_shape,
        in_specs=in_specs,
        out_specs=jax.tree.map(lambda _: VMEM, out_shape),
        scratch_shapes=scratch,
        compiler_params=pltpu.CompilerParams(vmem_limit_bytes=24 * 1024 * 1024),
        cost_estimate=pl.CostEstimate(flops=flops, bytes_accessed=bytes_moved, transcendentals=0),
    )


def masked_rows(value, first_row, live_blocks):
    row = first_row + lax.broadcasted_iota(jnp.int32, value.shape, 0)
    return jnp.where(row < live_blocks * B, value, jnp.zeros_like(value))


def rows_at(start, size):
    return pl.ds(pl.multiple_of(start, 16), size)


def mm(left, right):
    return jnp.dot(left, right, preferred_element_type=F32)


def panel_kernel(sizes, live, pmap, rhs, panel, send, keep, b_v, w_v, c_v, sems):
    quarter, half, parts, update_rows = sizes
    leaf_pos = lax.axis_index("leaf")
    row_pos = lax.axis_index("row")
    get_b = pltpu.make_async_copy(rhs.at[pl.ds(0, quarter)], b_v, sems.at[0])
    get_b.start()
    step = update_rows // parts
    copies = []
    for i in range(parts):
        rows = pl.ds(i * step, step)
        copies.append(pltpu.make_async_copy(panel.at[rows], w_v.at[rows], sems.at[1 + i]))
        copies[-1].start()
    c_v[...] = jnp.zeros_like(c_v)
    get_b.wait()
    masked = masked_rows(b_v[...], row_pos * quarter, live[leaf_pos])
    for i in range(parts):
        copies[i].wait()
        product = mm(w_v[pl.ds(i * step, step)], masked).astype(BF)
        for e in range(step // B):
            block = pmap[leaf_pos, i * (step // B) + e]
            c_v[pl.ds(pl.multiple_of(block * B, B), B)] = product[e * B : (e + 1) * B]
    for k in range(4):
        base = (row_pos ^ k) * quarter
        keep[pl.ds(k * half, half)] = c_v[rows_at(base + leaf_pos * half, half)]
        send[pl.ds(k * half, half)] = c_v[rows_at(base + (1 - leaf_pos) * half, half)]


def leaf_pivot_kernel(
    sizes, live, rhs, pivot, send_x, send_y, keep_x, keep_y, b_v, d_v, sems
):
    quarter, half = sizes
    leaf_pos = lax.axis_index("leaf")
    row_pos = lax.axis_index("row")
    get_b = pltpu.make_async_copy(rhs.at[pl.ds(0, quarter)], b_v, sems.at[4])
    get_b.start()
    order = (3, 1, 2, 0)
    copies = {}
    for k in order:
        rows = rows_at((row_pos ^ k) * quarter, quarter)
        copies[k] = pltpu.make_async_copy(pivot.at[rows], d_v.at[k], sems.at[k])
        copies[k].start()
    get_b.wait()
    masked = masked_rows(b_v[...], row_pos * quarter, live[leaf_pos])
    first, second = pl.ds(0, half), pl.ds(half, half)
    low = {1: (send_x, first), 3: (send_x, second), 0: (keep_x, first), 2: (keep_x, second)}
    high = {2: (send_y, first), 3: (send_y, second), 0: (keep_y, first), 1: (keep_y, second)}
    for k in order:
        copies[k].wait()
        product = mm(d_v[k], masked).astype(BF)
        ref, rows = low[k]
        ref[rows] = product[:half]
        ref, rows = high[k]
        ref[rows] = product[half:]


def root_pivot_kernel(sizes, own, other, pivot, out0, out1, out2, out3, q_v, d_v, sems):
    quarter, half, base = sizes
    leaf_pos = lax.axis_index("leaf")
    row_pos = lax.axis_index("row")
    outs = (out0, out1, out2, out3)
    order = (3, 1, 2, 0)
    copies = {}
    for k in order:
        rows = rows_at(base + (row_pos ^ k) * half, half)
        copies[k] = pltpu.make_async_copy(pivot.at[rows], d_v.at[k], sems.at[k])
        copies[k].start()
    q_v[rows_at(leaf_pos * half, half)] = own[...]
    q_v[rows_at((1 - leaf_pos) * half, half)] = other[...]
    right = q_v[...]
    for k in order:
        copies[k].wait()
        outs[k][...] = mm(d_v[k], right).astype(BF)


def root_transposed_kernel(sizes, y0, y1, y2, y3, pivot, keep, send, y_v, d_v, s_v, sem):
    quarter, half, base = sizes
    leaf_pos = lax.axis_index("leaf")
    row_pos = lax.axis_index("row")
    get_d = pltpu.make_async_copy(pivot.at[pl.ds(base, 4 * half)], d_v, sem)
    get_d.start()
    for k, piece in enumerate((y0, y1, y2, y3)):
        y_v[rows_at((row_pos ^ k) * half, half)] = piece[...]
    turned = y_v[...].T
    get_d.wait()
    s_v[...] = mm(turned, d_v[...]).T
    keep[...] = s_v[rows_at(leaf_pos * half, half)]
    send[...] = s_v[rows_at((1 - leaf_pos) * half, half)].astype(BF)


def leaf_transposed_kernel(
    sizes, f0, f1, f2, f3a, f3b, root_piece, pivot, total, forward, y_v, d_v, sem
):
    quarter, half = sizes
    row_pos = lax.axis_index("row")
    get_d = pltpu.make_async_copy(pivot.at[pl.ds(0, 4 * quarter)], d_v, sem)
    get_d.start()
    for k, piece in enumerate((f0, f1, f2)):
        y_v[rows_at((row_pos ^ k) * quarter, quarter)] = piece[...]
    y_v[rows_at((row_pos ^ 3) * quarter, half)] = f3a[...]
    y_v[rows_at((row_pos ^ 3) * quarter + half, half)] = f3b[...]
    forward[pl.ds(0, quarter)] = f0[...]
    forward[pl.ds(quarter, half)] = root_piece[...]
    turned = y_v[...].T
    get_d.wait()
    total[...] = mm(turned, d_v[...])


def last_kernel(
    sizes, live, pmap, s0, s1, s2, s3, t0, t1, t2, t3, total, panel, out, s_v, w_v, p_v, sem
):
    quarter, half, update_rows = sizes
    leaf_pos = lax.axis_index("leaf")
    row_pos = lax.axis_index("row")
    get_p = pltpu.make_async_copy(panel.at[pl.ds(0, update_rows)], p_v, sem)
    get_p.start()
    for k, (mine, theirs) in enumerate(((s0, t0), (s1, t1), (s2, t2), (s3, t3))):
        base = (row_pos ^ k) * quarter
        s_v[rows_at(base + leaf_pos * half, half)] = mine[...]
        s_v[rows_at(base + (1 - leaf_pos) * half, half)] = theirs[...]
    for e in range(update_rows // B):
        block = pmap[leaf_pos, e]
        w_v[pl.ds(e * B, B)] = s_v[pl.ds(pl.multiple_of(block * B, B), B)]
    turned = w_v[...].T
    get_p.wait()
    value = (total[...] - mm(turned, p_v[...])).T
    out[pl.ds(0, quarter)] = masked_rows(value, row_pos * quarter, live[leaf_pos]).astype(BF)
    out[pl.ds(quarter, half)] = s0[...]


def row_swap(value, apart):
    count = lax.axis_size("row")
    return lax.ppermute(value, "row", [(r, r ^ apart) for r in range(count)])


def leaf_swap(value):
    return lax.ppermute(value, "leaf", [(0, 1), (1, 0)])


def two_levels(rhs, pivot_inverse, panel, live, parent_map):
    columns = rhs.shape[1]
    quarter = pivot_inverse.shape[1]
    half = quarter // 2
    front = 4 * quarter
    updates = parent_map.shape[1] * B
    leaf_pos = lax.axis_index("leaf")
    row_pos = lax.axis_index("row")

    def live_rows(value, first_row, front_no):
        row = first_row + lax.broadcasted_iota(jnp.int32, value.shape, 0)
        count = lax.dynamic_index_in_dim(live, front_no, 0, keepdims=False) * B
        return jnp.where(row < count, value, 0.0)

    root_first = (2 * row_pos + leaf_pos) * half

    parts = 4 if updates % (4 * B) == 0 else 1
    sent, kept = call(
        functools.partial(panel_kernel, (quarter, half, parts, updates)),
        (bf16(4 * half, columns), bf16(4 * half, columns)),
        [SMEM, SMEM, ANY, ANY],
        [
            pltpu.VMEM((quarter, columns), BF),
            pltpu.VMEM((updates, quarter), BF),
            pltpu.VMEM((front, columns), BF),
            pltpu.SemaphoreType.DMA((1 + parts,)),
        ],
        2 * updates * quarter * columns,
        2 * updates * quarter,
    )(live, parent_map, rhs, panel)
    partner = leaf_swap(sent)

    def summed(k):
        rows = slice(k * half, (k + 1) * half)
        return kept[rows].astype(F32) + partner[rows].astype(F32)

    arrived = [row_swap(summed(k).astype(BF), k) for k in (3, 1, 2)]
    incoming = summed(0)
    for value in arrived:
        incoming = incoming + value.astype(F32)
    right_side = (rhs[quarter:].astype(F32) - incoming).astype(BF)
    right_side = live_rows(right_side, root_first, 2).astype(BF)
    right_other = leaf_swap(right_side)

    send_x, send_y, keep_x, keep_y = call(
        functools.partial(leaf_pivot_kernel, (quarter, half)),
        (bf16(quarter, columns),) * 4,
        [SMEM, ANY, ANY],
        [
            pltpu.VMEM((quarter, columns), BF),
            pltpu.VMEM((4, quarter, quarter), BF),
            pltpu.SemaphoreType.DMA((5,)),
        ],
        2 * front * quarter * columns,
        2 * front * quarter,
    )(live, rhs, pivot_inverse)
    sum_x = keep_x.astype(F32) + row_swap(send_x, 1).astype(F32)
    sum_y = keep_y.astype(F32) + row_swap(send_y, 2).astype(F32)
    low = sum_x[:half] + row_swap(sum_x[half:].astype(BF), 2).astype(F32)
    high = sum_y[:half] + row_swap(sum_y[half:].astype(BF), 1).astype(F32)
    leaf_forward = live_rows(
        jnp.concatenate([low, high], 0), row_pos * quarter, leaf_pos
    ).astype(BF)

    outs = call(
        functools.partial(root_pivot_kernel, (quarter, half, front)),
        (bf16(half, columns),) * 4,
        [VMEM, VMEM, ANY],
        [
            pltpu.VMEM((quarter, columns), BF),
            pltpu.VMEM((4, half, quarter), BF),
            pltpu.SemaphoreType.DMA((4,)),
        ],
        front * quarter * columns,
        front * quarter,
    )(right_side, right_other, pivot_inverse)
    root_forward = outs[0].astype(F32)
    for k in (3, 1, 2):
        root_forward = root_forward + row_swap(outs[k], k).astype(F32)
    root_forward = live_rows(root_forward, root_first, 2).astype(BF)

    root_rows = [root_forward] + [row_swap(root_forward, k) for k in (1, 2, 3)]
    root_keep, root_send = call(
        functools.partial(root_transposed_kernel, (quarter, half, front)),
        (jax.ShapeDtypeStruct((half, columns), F32), bf16(half, columns)),
        [VMEM, VMEM, VMEM, VMEM, ANY],
        [
            pltpu.VMEM((4 * half, columns), BF),
            pltpu.VMEM((4 * half, quarter), BF),
            pltpu.VMEM((quarter, columns), F32),
            pltpu.SemaphoreType.DMA,
        ],
        front * quarter * columns,
        front * quarter,
    )(*root_rows, pivot_inverse)
    root_value = root_keep + leaf_swap(root_send).astype(F32)
    root_value = live_rows(root_value, root_first, 2).astype(BF)
    mine = [root_value] + [row_swap(root_value, k) for k in (1, 2, 3)]
    theirs = [leaf_swap(value) for value in mine]

    from_x = row_swap(leaf_forward, 1)
    from_y = row_swap(leaf_forward, 2)
    third_low = row_swap(from_x[:half], 2)
    third_high = row_swap(from_y[half:], 1)
    total, forward = call(
        functools.partial(leaf_transposed_kernel, (quarter, half)),
        (jax.ShapeDtypeStruct((columns, quarter), F32), bf16(quarter + half, columns)),
        [VMEM] * 6 + [ANY],
        [
            pltpu.VMEM((front, columns), BF),
            pltpu.VMEM((front, quarter), BF),
            pltpu.SemaphoreType.DMA,
        ],
        2 * front * quarter * columns,
        2 * front * quarter,
    )(leaf_forward, from_x, from_y, third_low, third_high, root_forward, pivot_inverse)

    backward = call(
        functools.partial(last_kernel, (quarter, half, updates)),
        bf16(quarter + half, columns),
        [SMEM, SMEM] + [VMEM] * 9 + [ANY],
        [
            pltpu.VMEM((front, columns), BF),
            pltpu.VMEM((updates, columns), BF),
            pltpu.VMEM((updates, quarter), BF),
            pltpu.SemaphoreType.DMA,
        ],
        2 * updates * quarter * columns,
        2 * updates * quarter,
    )(live, parent_map, *mine, *theirs, total, panel)
    return forward, backward


def on_device(rhs, pivot_inverse, panel, live, parent_map):
    if lax.axis_size("leaf") == 2 and lax.axis_size("row") == 4:
        return two_levels(rhs, pivot_inverse, panel, live, parent_map)
    return deep_tree(rhs, pivot_inverse, panel, live, parent_map)


def solution(mesh):
    in_specs = (P(("leaf", "row"), "col"), P("leaf", "row"), P("leaf", "row"), P(), P())
    out_specs = (P(("leaf", "row"), "col"), P(("leaf", "row"), "col"))
    return jax.shard_map(
        on_device, mesh=mesh, in_specs=in_specs, out_specs=out_specs, check_vma=False
    )
```

```python
import functools

import jax
import jax.numpy as jnp
from jax import lax
from jax.experimental import pallas as pl
from jax.experimental.pallas import tpu as pltpu
from jax.sharding import PartitionSpec as P

F = 2560
E = 1536


def from_partner(block, axis, apart):
    count = lax.axis_size(axis)
    route = []
    for low in range(count):
        high = low | 1 << apart
        if high != low and high < count:
            route += [(low, high), (high, low)]
    return lax.ppermute(block, axis, route)


def doubling(stacked, bit_count, leaf_pos, swapper):
    for bit_no in range(bit_count):
        partner = swapper(stacked, bit_no)
        upper_half = jnp.right_shift(leaf_pos, bit_no) % 2 == 1
        stacked = jnp.where(
            upper_half,
            jnp.concatenate([partner, stacked], 0),
            jnp.concatenate([stacked, partner], 0),
        )
    return stacked


def halving(partial_value, bit_count, leaf_pos, swapper):
    for bit_no in reversed(range(bit_count)):
        halves = partial_value.reshape((2, partial_value.shape[0] // 2) + partial_value.shape[1:])
        upper_half = jnp.right_shift(leaf_pos, bit_no) % 2 == 1
        kept_half = jnp.where(upper_half, halves[1], halves[0])
        sent_half = jnp.where(upper_half, halves[0], halves[1])
        partial_value = kept_half + swapper(sent_half, bit_no)
    return partial_value[0]


def to_front(group_block, row_count):
    count_g, total_rows, row_width = group_block.shape
    piece_rows = total_rows // row_count
    return (
        group_block.reshape(count_g, row_count, piece_rows, row_width)
        .transpose(1, 0, 2, 3)
        .reshape(count_g * total_rows, row_width)
    )


def block_onehot(mapping):
    return (jnp.arange(F // 128, dtype=jnp.int32)[:, None] == mapping[None, :]).astype(jnp.bfloat16)


def pivot_sum(diag_block, quarter_rows):
    return lax.psum_scatter(
        jnp.dot(diag_block, quarter_rows, preferred_element_type=jnp.float32).astype(jnp.bfloat16),
        "row",
        scatter_dimension=0,
        tiled=True,
    ).astype(jnp.float32)


def quarter_swap(values, bit_no):
    return from_partner(values, "leaf", bit_no)


def update_swap(values, bit_no):
    return from_partner(values, "leaf", bit_no)


def parent_swap(values, bit_no):
    return from_partner(values, "leaf", bit_no)


def reduce_swap(values, bit_no):
    return from_partner(values.astype(jnp.bfloat16), "leaf", bit_no).astype(values.dtype)


def deep_tree(rhs, pivot_inverse, panel, live, parent_map):
    leaves = lax.axis_size("leaf")
    row_count = lax.axis_size("row")
    tree_depth = leaves.bit_length() - 1
    leaf_pos = lax.axis_index("leaf")
    row_pos = lax.axis_index("row")
    columns = rhs.shape[1]
    quarter = F // row_count
    parent_blocks = F // 128
    child_blocks = E // 128
    layout = []
    vec_off, piv_off, pan_off, front_base = (0, 0, 0, 0)
    for level_no in range(tree_depth + 1):
        groups = 2**level_no
        layout.append((groups, vec_off, piv_off, pan_off, front_base))
        vec_off += F // (row_count * groups)
        piv_off += F // groups
        pan_off += E // groups
        front_base += leaves // groups
    forward_parts = []
    live_masks = []
    incoming = None
    for level_no in range(tree_depth + 1):
        groups, vec_off, piv_off, pan_off, front_base = layout[level_no]
        piece_rows = F // (row_count * groups)
        panel_rows = E // (row_count * groups)
        inner_pos = leaf_pos % groups
        front_no = jnp.right_shift(leaf_pos, level_no)
        live_rows = lax.dynamic_index_in_dim(live, front_base + front_no, 0, keepdims=False) * 128
        first_row = (row_pos * groups + inner_pos) * piece_rows
        live_mask = (first_row + jnp.arange(piece_rows, dtype=jnp.int32) < live_rows)[:, None]
        live_masks.append(live_mask)
        right_side = rhs[vec_off : vec_off + piece_rows]
        if incoming is not None:
            right_side = (right_side.astype(jnp.float32) - incoming).astype(jnp.bfloat16)
        masked = jnp.where(live_mask, right_side, jnp.zeros_like(right_side))
        quarter_rows = doubling(masked[None], level_no, leaf_pos, quarter_swap).reshape(
            quarter, columns
        )
        diag_block = pivot_inverse[piv_off : piv_off + F // groups]
        if level_no < tree_depth:
            off_block = panel[pan_off : pan_off + E // groups]
            forward_value = pivot_sum(diag_block, quarter_rows)
            update_rows = lax.psum(
                jnp.dot(off_block, quarter_rows, preferred_element_type=jnp.float32), "row"
            ).astype(jnp.bfloat16)
        else:
            forward_value = pivot_sum(diag_block, quarter_rows)
        forward_parts.append(jnp.where(live_mask, forward_value, 0.0).astype(jnp.bfloat16))
        if level_no < tree_depth:
            gathered = doubling(update_rows[None], level_no + 1, leaf_pos, update_swap)
            parent_front = jnp.right_shift(leaf_pos, level_no + 1)
            assembled = jnp.zeros((parent_blocks, 128, columns), jnp.float32)
            for side_no in range(2):
                child_update = to_front(
                    gathered[side_no * groups : (side_no + 1) * groups], row_count
                )
                mapping = lax.dynamic_index_in_dim(
                    parent_map, front_base + 2 * parent_front + side_no, 0, keepdims=False
                )
                assembled = assembled + jnp.einsum(
                    "ke,eab->kab",
                    block_onehot(mapping),
                    child_update.reshape(child_blocks, 128, columns),
                    preferred_element_type=jnp.float32,
                )
            parent_groups = 2 * groups
            parent_rows = F // (row_count * parent_groups)
            parent_first = (row_pos * parent_groups + leaf_pos % parent_groups) * parent_rows
            incoming = lax.dynamic_slice_in_dim(
                assembled.reshape(F, columns), parent_first, parent_rows, 0
            )
    backward_parts = [None] * (tree_depth + 1)
    parent_value = None
    for level_no in reversed(range(tree_depth + 1)):
        groups, vec_off, piv_off, pan_off, front_base = layout[level_no]
        piece_rows = F // (row_count * groups)
        panel_rows = E // (row_count * groups)
        inner_pos = leaf_pos % groups
        front_no = jnp.right_shift(leaf_pos, level_no)
        diag_block = pivot_inverse[piv_off : piv_off + F // groups]
        own_piece = forward_parts[level_no]
        if level_no == tree_depth:
            own_rows = lax.all_gather(own_piece, "row", axis=0, tiled=True)
            partial_value = jnp.einsum(
                "ik,ia->ka", diag_block, own_rows, preferred_element_type=jnp.float32
            )
        else:
            own_rows, parent_gathered = (
                lax.all_gather(own_piece, "row", axis=0, tiled=True),
                lax.all_gather(parent_value, "row", axis=0, tiled=True),
            )
            whole_parent = doubling(parent_gathered[None], level_no + 1, leaf_pos, parent_swap)
            parent_full = to_front(whole_parent, row_count)
            mapping = lax.dynamic_index_in_dim(parent_map, front_base + front_no, 0, keepdims=False)
            taken_rows = jnp.einsum(
                "ke,kab->eab",
                block_onehot(mapping),
                parent_full.reshape(parent_blocks, 128, columns),
                preferred_element_type=jnp.float32,
            ).astype(jnp.bfloat16)
            taken_rows = lax.dynamic_index_in_dim(
                taken_rows.reshape(row_count, groups, panel_rows, columns),
                inner_pos,
                1,
                keepdims=False,
            ).reshape(row_count * panel_rows, columns)
            off_block = panel[pan_off : pan_off + E // groups]
            partial_value = jnp.einsum(
                "ik,ia->ka", diag_block, own_rows, preferred_element_type=jnp.float32
            ) - jnp.einsum("ik,ia->ka", off_block, taken_rows, preferred_element_type=jnp.float32)
        if level_no == 0:
            reduced = partial_value
        else:
            reduced = halving(
                partial_value.reshape(groups, piece_rows, columns), level_no, leaf_pos, reduce_swap
            )
        parent_value = jnp.where(live_masks[level_no], reduced, 0.0).astype(jnp.bfloat16)
        backward_parts[level_no] = parent_value
    return (jnp.concatenate(forward_parts, 0), jnp.concatenate(backward_parts, 0))


B = 128
VMEM = pl.BlockSpec(memory_space=pltpu.VMEM)
SMEM = pl.BlockSpec(memory_space=pltpu.SMEM)
ANY = pl.BlockSpec(memory_space=pl.ANY)
BF = jnp.bfloat16
F32 = jnp.float32
MIB = 1024 * 1024


def shaped(rows, columns, dtype=BF):
    return jax.ShapeDtypeStruct((rows, columns), dtype)


def kept(rows, columns, dtype=BF):
    return pltpu.VMEM((rows, columns), dtype)


def call(body, out_shape, in_specs, scratch, limit, flops, bytes_moved):
    return pl.pallas_call(
        body,
        out_shape=out_shape,
        in_specs=in_specs,
        out_specs=jax.tree.map(lambda _: VMEM, out_shape, is_leaf=lambda s: hasattr(s, "shape")),
        scratch_shapes=scratch,
        compiler_params=pltpu.CompilerParams(vmem_limit_bytes=limit * MIB),
        cost_estimate=pl.CostEstimate(flops=flops, bytes_accessed=bytes_moved, transcendentals=0),
    )


def masked_rows(value, first_row, live_blocks):
    row = first_row + lax.broadcasted_iota(jnp.int32, value.shape, 0)
    return jnp.where(row < live_blocks * B, value, jnp.zeros_like(value))


def rows_at(start, size):
    return pl.ds(pl.multiple_of(start, 16), size)


def mm(left, right):
    return jnp.dot(left, right, preferred_element_type=F32)


def panel_kernel(sizes, live, pmap, rhs, panel, send, keep, w_v, b_v, c_v, sems):
    quarter, half, parts, update_rows = sizes
    leaf_pos = lax.axis_index("leaf")
    row_pos = lax.axis_index("row")
    get_b = pltpu.make_async_copy(rhs.at[pl.ds(0, quarter)], b_v, sems.at[0])
    get_b.start()
    step = update_rows // parts
    copies = []
    for i in range(parts):
        rows = pl.ds(i * step, step)
        copies.append(pltpu.make_async_copy(panel.at[rows], w_v.at[rows], sems.at[1 + i]))
        copies[-1].start()
    c_v[...] = jnp.zeros_like(c_v)
    get_b.wait()
    masked = masked_rows(b_v[...], row_pos * quarter, live[leaf_pos])
    for i in range(parts):
        copies[i].wait()
        product = mm(w_v[pl.ds(i * step, step)], masked).astype(BF)
        for e in range(step // B):
            block = pmap[leaf_pos, i * (step // B) + e]
            c_v[pl.ds(pl.multiple_of(block * B, B), B)] = product[e * B : (e + 1) * B]
    for r in range(4):
        base = r * quarter
        keep[pl.ds(r * half, half)] = c_v[rows_at(base + leaf_pos * half, half)]
        send[pl.ds(r * half, half)] = c_v[rows_at(base + (1 - leaf_pos) * half, half)]


def leaf_pivot_kernel(sizes, live, rhs, pivot, after, partial, d_v, b_v, sems):
    quarter, half = sizes
    leaf_pos = lax.axis_index("leaf")
    row_pos = lax.axis_index("row")
    get_b = pltpu.make_async_copy(rhs.at[pl.ds(0, quarter)], b_v, sems.at[6])
    get_b.start()
    copies = []
    for k in range(6):
        rows = pl.ds(k * quarter, quarter)
        copies.append(pltpu.make_async_copy(pivot.at[rows], d_v.at[rows], sems.at[k]))
        copies[-1].start()
    get_b.wait()
    masked = masked_rows(b_v[...], row_pos * quarter, live[leaf_pos])
    for k in range(4):
        copies[k].wait()
        rows = pl.ds(k * quarter, quarter)
        partial[rows] = mm(d_v[rows], masked).astype(BF)
    copies[4].wait()
    copies[5].wait()


def root_pivot_kernel(sizes, own, other, pivot, partial, q_v):
    quarter, half, base = sizes
    leaf_pos = lax.axis_index("leaf")
    q_v[rows_at(leaf_pos * half, half)] = own[...]
    q_v[rows_at((1 - leaf_pos) * half, half)] = other[...]
    partial[...] = mm(pivot[pl.ds(base, 4 * half)], q_v[...]).astype(BF)


def root_transposed_kernel(sizes, y, pivot, keep, send, s_v):
    quarter, half, base = sizes
    leaf_pos = lax.axis_index("leaf")
    s_v[...] = mm(y[...].T, pivot[pl.ds(base, 4 * half)]).T
    keep[...] = s_v[rows_at(leaf_pos * half, half)]
    send[...] = s_v[rows_at((1 - leaf_pos) * half, half)].astype(BF)


def leaf_transposed_kernel(sizes, y, own, root_piece, pivot, total, forward):
    quarter, half = sizes
    forward[pl.ds(0, quarter)] = own[...]
    forward[pl.ds(quarter, half)] = root_piece[...]
    total[...] = mm(y[...].T, pivot[pl.ds(0, 4 * quarter)])


def last_kernel(sizes, live, pmap, mine, theirs, own, total, w_v, out, s_v, p_v):
    quarter, half, update_rows = sizes
    leaf_pos = lax.axis_index("leaf")
    row_pos = lax.axis_index("row")
    for r in range(4):
        rows = pl.ds(r * half, half)
        s_v[rows_at(r * quarter + leaf_pos * half, half)] = mine[rows]
        s_v[rows_at(r * quarter + (1 - leaf_pos) * half, half)] = theirs[rows]
    for e in range(update_rows // B):
        block = pmap[leaf_pos, e]
        p_v[pl.ds(e * B, B)] = s_v[pl.ds(pl.multiple_of(block * B, B), B)]
    value = (total[...] - mm(p_v[...].T, w_v[...])).T
    out[pl.ds(0, quarter)] = masked_rows(value, row_pos * quarter, live[leaf_pos]).astype(BF)
    out[pl.ds(quarter, half)] = own[...]


def leaf_swap(value):
    return lax.ppermute(value, "leaf", [(0, 1), (1, 0)])


def row_trade(value):
    return lax.all_to_all(value, "row", 0, 0, tiled=True)


def row_sum(value):
    parts = row_trade(value).reshape(4, value.shape[0] // 4, value.shape[1])
    return parts.astype(F32).sum(0)


def row_gather(value):
    return row_trade(jnp.concatenate([value] * 4, 0))


def two_levels(rhs, pivot_inverse, panel, live, parent_map):
    columns = rhs.shape[1]
    quarter = pivot_inverse.shape[1]
    half = quarter // 2
    front = 4 * quarter
    updates = parent_map.shape[1] * B
    leaf_pos = lax.axis_index("leaf")
    row_pos = lax.axis_index("row")

    def live_rows(value, first_row, front_no):
        row = first_row + lax.broadcasted_iota(jnp.int32, value.shape, 0)
        count = lax.dynamic_index_in_dim(live, front_no, 0, keepdims=False) * B
        return jnp.where(row < count, value, 0.0).astype(BF)

    root_first = (2 * row_pos + leaf_pos) * half
    root = live.shape[0] - 1

    parts = 4 if updates % (4 * B) == 0 else 1
    sent, keep, w_v = call(
        functools.partial(panel_kernel, (quarter, half, parts, updates)),
        (shaped(4 * half, columns), shaped(4 * half, columns), kept(updates, quarter)),
        [SMEM, SMEM, ANY, ANY],
        [
            pltpu.VMEM((quarter, columns), BF),
            pltpu.VMEM((front, columns), BF),
            pltpu.SemaphoreType.DMA((1 + parts,)),
        ],
        56,
        2 * updates * quarter * columns,
        2 * updates * quarter,
    )(live, parent_map, rhs, panel)
    update = keep.astype(F32) + leaf_swap(sent).astype(F32)
    incoming = row_sum(update.astype(BF))
    right_side = (rhs[quarter:].astype(F32) - incoming).astype(BF)
    right_side = live_rows(right_side, root_first, root)
    partial, d_v = call(
        functools.partial(leaf_pivot_kernel, (quarter, half)),
        (shaped(front, columns), kept(6 * quarter, quarter)),
        [SMEM, ANY, ANY, ANY],
        [pltpu.VMEM((quarter, columns), BF), pltpu.SemaphoreType.DMA((7,))],
        50,
        2 * front * quarter * columns,
        2 * front * quarter,
    )(live, rhs, pivot_inverse, sent)
    right_other = leaf_swap(right_side)
    partial, right_other = lax.optimization_barrier((partial, right_other))
    leaf_forward = live_rows(row_sum(partial), row_pos * quarter, leaf_pos)

    root_partial = call(
        functools.partial(root_pivot_kernel, (quarter, half, front)),
        shaped(4 * half, columns),
        [VMEM, VMEM, VMEM],
        [pltpu.VMEM((quarter, columns), BF)],
        16,
        front * quarter * columns,
        front * quarter,
    )(right_side, right_other, d_v)
    root_forward = live_rows(row_sum(root_partial), root_first, root)

    root_keep, root_send = call(
        functools.partial(root_transposed_kernel, (quarter, half, front)),
        (shaped(half, columns, F32), shaped(half, columns)),
        [VMEM, VMEM],
        [pltpu.VMEM((quarter, columns), F32)],
        16,
        front * quarter * columns,
        front * quarter,
    )(row_gather(root_forward), d_v)
    root_value = root_keep + leaf_swap(root_send).astype(F32)
    root_value = live_rows(root_value, root_first, root)
    mine = row_gather(root_value)
    theirs = leaf_swap(mine)

    total, forward = call(
        functools.partial(leaf_transposed_kernel, (quarter, half)),
        (shaped(columns, quarter, F32), shaped(quarter + half, columns)),
        [VMEM] * 4,
        [],
        16,
        2 * front * quarter * columns,
        2 * front * quarter,
    )(row_gather(leaf_forward), leaf_forward, root_forward, d_v)

    backward = call(
        functools.partial(last_kernel, (quarter, half, updates)),
        shaped(quarter + half, columns),
        [SMEM, SMEM] + [VMEM] * 5,
        [pltpu.VMEM((front, columns), BF), pltpu.VMEM((updates, columns), BF)],
        16,
        2 * updates * quarter * columns,
        2 * updates * quarter,
    )(live, parent_map, mine, theirs, root_value, total, w_v)
    return forward, backward


def on_device(rhs, pivot_inverse, panel, live, parent_map):
    if lax.axis_size("leaf") == 2 and lax.axis_size("row") == 4:
        return two_levels(rhs, pivot_inverse, panel, live, parent_map)
    return deep_tree(rhs, pivot_inverse, panel, live, parent_map)


def solution(mesh):
    in_specs = (P(("leaf", "row"), "col"), P("leaf", "row"), P("leaf", "row"), P(), P())
    out_specs = (P(("leaf", "row"), "col"), P(("leaf", "row"), "col"))
    return jax.shard_map(
        on_device, mesh=mesh, in_specs=in_specs, out_specs=out_specs, check_vma=False
    )
```

```python
import functools

import jax
import jax.numpy as jnp
from jax import lax
from jax.experimental import pallas as pl
from jax.experimental.pallas import tpu as pltpu
from jax.sharding import PartitionSpec as P

F = 2560
E = 1536


def from_partner(block, axis, apart):
    count = lax.axis_size(axis)
    route = []
    for low in range(count):
        high = low | 1 << apart
        if high != low and high < count:
            route += [(low, high), (high, low)]
    return lax.ppermute(block, axis, route)


def doubling(stacked, bit_count, leaf_pos, swapper):
    for bit_no in range(bit_count):
        partner = swapper(stacked, bit_no)
        upper_half = jnp.right_shift(leaf_pos, bit_no) % 2 == 1
        stacked = jnp.where(
            upper_half,
            jnp.concatenate([partner, stacked], 0),
            jnp.concatenate([stacked, partner], 0),
        )
    return stacked


def halving(partial_value, bit_count, leaf_pos, swapper):
    for bit_no in reversed(range(bit_count)):
        halves = partial_value.reshape((2, partial_value.shape[0] // 2) + partial_value.shape[1:])
        upper_half = jnp.right_shift(leaf_pos, bit_no) % 2 == 1
        kept_half = jnp.where(upper_half, halves[1], halves[0])
        sent_half = jnp.where(upper_half, halves[0], halves[1])
        partial_value = kept_half + swapper(sent_half, bit_no)
    return partial_value[0]


def to_front(group_block, row_count):
    count_g, total_rows, row_width = group_block.shape
    piece_rows = total_rows // row_count
    return (
        group_block.reshape(count_g, row_count, piece_rows, row_width)
        .transpose(1, 0, 2, 3)
        .reshape(count_g * total_rows, row_width)
    )


def block_onehot(mapping):
    return (jnp.arange(F // 128, dtype=jnp.int32)[:, None] == mapping[None, :]).astype(jnp.bfloat16)


def pivot_sum(diag_block, quarter_rows):
    return lax.psum_scatter(
        jnp.dot(diag_block, quarter_rows, preferred_element_type=jnp.float32).astype(jnp.bfloat16),
        "row",
        scatter_dimension=0,
        tiled=True,
    ).astype(jnp.float32)


def quarter_swap(values, bit_no):
    return from_partner(values, "leaf", bit_no)


def update_swap(values, bit_no):
    return from_partner(values, "leaf", bit_no)


def parent_swap(values, bit_no):
    return from_partner(values, "leaf", bit_no)


def reduce_swap(values, bit_no):
    return from_partner(values.astype(jnp.bfloat16), "leaf", bit_no).astype(values.dtype)


def deep_tree(rhs, pivot_inverse, panel, live, parent_map):
    leaves = lax.axis_size("leaf")
    row_count = lax.axis_size("row")
    tree_depth = leaves.bit_length() - 1
    leaf_pos = lax.axis_index("leaf")
    row_pos = lax.axis_index("row")
    columns = rhs.shape[1]
    quarter = F // row_count
    parent_blocks = F // 128
    child_blocks = E // 128
    layout = []
    vec_off, piv_off, pan_off, front_base = (0, 0, 0, 0)
    for level_no in range(tree_depth + 1):
        groups = 2**level_no
        layout.append((groups, vec_off, piv_off, pan_off, front_base))
        vec_off += F // (row_count * groups)
        piv_off += F // groups
        pan_off += E // groups
        front_base += leaves // groups
    forward_parts = []
    live_masks = []
    incoming = None
    for level_no in range(tree_depth + 1):
        groups, vec_off, piv_off, pan_off, front_base = layout[level_no]
        piece_rows = F // (row_count * groups)
        panel_rows = E // (row_count * groups)
        inner_pos = leaf_pos % groups
        front_no = jnp.right_shift(leaf_pos, level_no)
        live_rows = lax.dynamic_index_in_dim(live, front_base + front_no, 0, keepdims=False) * 128
        first_row = (row_pos * groups + inner_pos) * piece_rows
        live_mask = (first_row + jnp.arange(piece_rows, dtype=jnp.int32) < live_rows)[:, None]
        live_masks.append(live_mask)
        right_side = rhs[vec_off : vec_off + piece_rows]
        if incoming is not None:
            right_side = (right_side.astype(jnp.float32) - incoming).astype(jnp.bfloat16)
        masked = jnp.where(live_mask, right_side, jnp.zeros_like(right_side))
        quarter_rows = doubling(masked[None], level_no, leaf_pos, quarter_swap).reshape(
            quarter, columns
        )
        diag_block = pivot_inverse[piv_off : piv_off + F // groups]
        if level_no < tree_depth:
            off_block = panel[pan_off : pan_off + E // groups]
            forward_value = pivot_sum(diag_block, quarter_rows)
            update_rows = lax.psum(
                jnp.dot(off_block, quarter_rows, preferred_element_type=jnp.float32), "row"
            ).astype(jnp.bfloat16)
        else:
            forward_value = pivot_sum(diag_block, quarter_rows)
        forward_parts.append(jnp.where(live_mask, forward_value, 0.0).astype(jnp.bfloat16))
        if level_no < tree_depth:
            gathered = doubling(update_rows[None], level_no + 1, leaf_pos, update_swap)
            parent_front = jnp.right_shift(leaf_pos, level_no + 1)
            assembled = jnp.zeros((parent_blocks, 128, columns), jnp.float32)
            for side_no in range(2):
                child_update = to_front(
                    gathered[side_no * groups : (side_no + 1) * groups], row_count
                )
                mapping = lax.dynamic_index_in_dim(
                    parent_map, front_base + 2 * parent_front + side_no, 0, keepdims=False
                )
                assembled = assembled + jnp.einsum(
                    "ke,eab->kab",
                    block_onehot(mapping),
                    child_update.reshape(child_blocks, 128, columns),
                    preferred_element_type=jnp.float32,
                )
            parent_groups = 2 * groups
            parent_rows = F // (row_count * parent_groups)
            parent_first = (row_pos * parent_groups + leaf_pos % parent_groups) * parent_rows
            incoming = lax.dynamic_slice_in_dim(
                assembled.reshape(F, columns), parent_first, parent_rows, 0
            )
    backward_parts = [None] * (tree_depth + 1)
    parent_value = None
    for level_no in reversed(range(tree_depth + 1)):
        groups, vec_off, piv_off, pan_off, front_base = layout[level_no]
        piece_rows = F // (row_count * groups)
        panel_rows = E // (row_count * groups)
        inner_pos = leaf_pos % groups
        front_no = jnp.right_shift(leaf_pos, level_no)
        diag_block = pivot_inverse[piv_off : piv_off + F // groups]
        own_piece = forward_parts[level_no]
        if level_no == tree_depth:
            own_rows = lax.all_gather(own_piece, "row", axis=0, tiled=True)
            partial_value = jnp.einsum(
                "ik,ia->ka", diag_block, own_rows, preferred_element_type=jnp.float32
            )
        else:
            own_rows, parent_gathered = (
                lax.all_gather(own_piece, "row", axis=0, tiled=True),
                lax.all_gather(parent_value, "row", axis=0, tiled=True),
            )
            whole_parent = doubling(parent_gathered[None], level_no + 1, leaf_pos, parent_swap)
            parent_full = to_front(whole_parent, row_count)
            mapping = lax.dynamic_index_in_dim(parent_map, front_base + front_no, 0, keepdims=False)
            taken_rows = jnp.einsum(
                "ke,kab->eab",
                block_onehot(mapping),
                parent_full.reshape(parent_blocks, 128, columns),
                preferred_element_type=jnp.float32,
            ).astype(jnp.bfloat16)
            taken_rows = lax.dynamic_index_in_dim(
                taken_rows.reshape(row_count, groups, panel_rows, columns),
                inner_pos,
                1,
                keepdims=False,
            ).reshape(row_count * panel_rows, columns)
            off_block = panel[pan_off : pan_off + E // groups]
            partial_value = jnp.einsum(
                "ik,ia->ka", diag_block, own_rows, preferred_element_type=jnp.float32
            ) - jnp.einsum("ik,ia->ka", off_block, taken_rows, preferred_element_type=jnp.float32)
        if level_no == 0:
            reduced = partial_value
        else:
            reduced = halving(
                partial_value.reshape(groups, piece_rows, columns), level_no, leaf_pos, reduce_swap
            )
        parent_value = jnp.where(live_masks[level_no], reduced, 0.0).astype(jnp.bfloat16)
        backward_parts[level_no] = parent_value
    return (jnp.concatenate(forward_parts, 0), jnp.concatenate(backward_parts, 0))


B = 128
VMEM = pl.BlockSpec(memory_space=pltpu.VMEM)
ANY = pl.BlockSpec(memory_space=pl.ANY)
BF = jnp.bfloat16
F32 = jnp.float32
MIB = 1024 * 1024


def stored(rows, columns, dtype=BF):
    return jax.ShapeDtypeStruct((rows, columns), dtype)


def kept(rows, columns, dtype=BF):
    return pltpu.VMEM((rows, columns), dtype)


def call(body, out_shape, in_specs, scratch, limit, flops, bytes_moved):
    return pl.pallas_call(
        body,
        out_shape=out_shape,
        in_specs=in_specs,
        out_specs=jax.tree.map(lambda _: VMEM, out_shape, is_leaf=lambda s: hasattr(s, "shape")),
        scratch_shapes=scratch,
        compiler_params=pltpu.CompilerParams(vmem_limit_bytes=limit),
        cost_estimate=pl.CostEstimate(flops=flops, bytes_accessed=bytes_moved, transcendentals=0),
    )


def rows_at(start, size):
    return pl.ds(pl.multiple_of(start, 16), size)


def mm(left, right):
    return jnp.dot(left, right, preferred_element_type=F32)


def row_order(row_pos, leaf_pos):
    first = 1 + leaf_pos
    return (row_pos, row_pos ^ (3 - first), row_pos ^ first, row_pos ^ 3)


def panel_kernel(
    sizes, live, pmap, rhs, panel, send, keep, b_v, masked, mask, w_v, c_v, live_s, pmap_s, sems
):
    quarter, half, parts, update_rows = sizes
    leaf_pos = lax.axis_index("leaf")
    row_pos = lax.axis_index("row")
    gets = [
        pltpu.make_async_copy(live, live_s, sems.at[0]),
        pltpu.make_async_copy(rhs, b_v, sems.at[1]),
        pltpu.make_async_copy(pmap, pmap_s, sems.at[2]),
    ]
    step = update_rows // parts
    for i in range(parts):
        rows = pl.ds(i * step, step)
        gets.append(pltpu.make_async_copy(panel.at[rows], w_v.at[rows], sems.at[3 + i]))
    for get in gets:
        get.start()
    c_v[...] = jnp.zeros_like(c_v)
    gets[0].wait()
    gets[1].wait()
    value = b_v[pl.ds(0, quarter)]
    row = row_pos * quarter + lax.broadcasted_iota(jnp.int32, value.shape, 0)
    alive = row < live_s[leaf_pos] * B
    mask[...] = jnp.where(alive, 1.0, 0.0).astype(BF)
    masked[...] = jnp.where(alive, value, jnp.zeros_like(value))
    right = masked[...]
    gets[2].wait()
    for i in range(parts):
        gets[3 + i].wait()
        product = mm(w_v[pl.ds(i * step, step)], right).astype(BF)
        for e in range(step // B):
            block = pmap_s[leaf_pos, i * (step // B) + e]
            c_v[pl.ds(pl.multiple_of(block * B, B), B)] = product[e * B : (e + 1) * B]
    for k, r in enumerate(row_order(row_pos, leaf_pos)):
        keep[pl.ds(k * half, half)] = c_v[rows_at(r * quarter + leaf_pos * half, half)]
    for k, r in enumerate(row_order(row_pos, 1 - leaf_pos)):
        send[pl.ds(k * half, half)] = c_v[rows_at(r * quarter + (1 - leaf_pos) * half, half)]


def leaf_pivot_kernel(sizes, masked, pivot, after, send, keep, d_v, sems):
    quarter, half = sizes
    order = row_order(lax.axis_index("row"), lax.axis_index("leaf"))
    gets = []
    for k in (2, 3, 0, 1):
        rows = rows_at(order[k] * quarter, quarter)
        gets.append(pltpu.make_async_copy(pivot.at[rows], d_v.at[rows], sems.at[k]))
    rows = pl.ds(4 * quarter, 4 * half)
    gets.append(pltpu.make_async_copy(pivot.at[rows], d_v.at[rows], sems.at[4]))
    for get in gets:
        get.start()
    right = masked[...]
    for get, k in zip(gets, (2, 3, 0, 1)):
        get.wait()
        out = keep if k < 2 else send
        product = mm(d_v[rows_at(order[k] * quarter, quarter)], right)
        out[pl.ds((k % 2) * quarter, quarter)] = product.astype(BF)
    gets[-1].wait()


def scatter_kernel(sizes, live, pmap, w_v, after, out, live_s, pmap_s, sems):
    quarter, update_rows = sizes
    leaf_pos = lax.axis_index("leaf")
    row_pos = lax.axis_index("row")
    gets = [
        pltpu.make_async_copy(live, live_s, sems.at[0]),
        pltpu.make_async_copy(pmap, pmap_s, sems.at[1]),
    ]
    for get in gets:
        get.start()
    out[...] = jnp.zeros_like(out)
    for get in gets:
        get.wait()
    column = row_pos * quarter + lax.broadcasted_iota(jnp.int32, (B, quarter), 1)
    alive = column < live_s[leaf_pos] * B
    for e in range(update_rows // B):
        value = w_v[pl.ds(e * B, B)]
        block = pmap_s[leaf_pos, e]
        out[pl.ds(pl.multiple_of(block * B, B), B)] = jnp.where(alive, value, jnp.zeros_like(value))


def root_pivot_kernel(sizes, own, other, d_v, send, keep, q_v):
    quarter, half, base = sizes
    leaf_pos = lax.axis_index("leaf")
    order = row_order(lax.axis_index("row"), leaf_pos)
    q_v[rows_at(leaf_pos * half, half)] = own[...]
    q_v[rows_at((1 - leaf_pos) * half, half)] = other[...]
    right = q_v[...]
    for k in range(4):
        out = keep if k < 2 else send
        product = mm(d_v[rows_at(base + order[k] * half, half)], right)
        out[pl.ds((k % 2) * half, half)] = product.astype(BF)


def root_transposed_kernel(sizes, near, far, d_v, keep, send, y_v, s_v):
    quarter, half, base = sizes
    leaf_pos = lax.axis_index("leaf")
    order = row_order(lax.axis_index("row"), leaf_pos)
    for k in range(4):
        part = (near if k < 2 else far)[pl.ds((k % 2) * half, half)]
        y_v[rows_at(order[k] * half, half)] = part
    s_v[...] = mm(y_v[...].T, d_v[pl.ds(base, 4 * half)]).T
    keep[...] = s_v[rows_at(leaf_pos * half, half)]
    send[...] = s_v[rows_at((1 - leaf_pos) * half, half)].astype(BF)


def leaf_transposed_kernel(sizes, near, far, d_v, mask, total, y_v):
    quarter, half = sizes
    order = row_order(lax.axis_index("row"), lax.axis_index("leaf"))
    for k in range(4):
        part = (near if k < 2 else far)[pl.ds((k % 2) * quarter, quarter)]
        y_v[rows_at(order[k] * quarter, quarter)] = part
    value = mm(y_v[...].T, d_v[pl.ds(0, 4 * quarter)])
    total[...] = jnp.where(mask[...].astype(F32).T > 0.0, value, 0.0)


def place(sizes, which, mine, theirs, s_v, w_v, panel_rows):
    quarter, half = sizes
    leaf_pos = lax.axis_index("leaf")
    row_pos = lax.axis_index("row")
    at = 0
    for source, side in ((mine, leaf_pos), (theirs, 1 - leaf_pos)):
        order = row_order(row_pos, side)
        for k in range(2):
            rows = pl.ds(at, half)
            s_v[rows] = source[pl.ds(k * half, half)]
            w_v[rows] = panel_rows[rows_at(order[which + k] * quarter + side * half, half)]
            at += half


def early_kernel(sizes, mine, theirs, total, panel_rows, out, s_v, w_v):
    place(sizes, 0, mine, theirs, s_v, w_v, panel_rows)
    out[...] = total[...] - mm(s_v[...].T, w_v[...])


def last_kernel(sizes, mine, theirs, total, panel_rows, near, out, s_v, w_v):
    quarter, half = sizes
    place(sizes, 2, mine, theirs, s_v, w_v, panel_rows)
    value = total[...] - mm(s_v[...].T, w_v[...])
    out[pl.ds(0, quarter)] = value.T.astype(BF)
    out[pl.ds(quarter, half)] = near[pl.ds(0, half)]


def leaf_swap(value):
    return lax.ppermute(value, "leaf", [(0, 1), (1, 0)])


def row_swap(value, phase):
    route = []
    for leaf in range(2):
        apart = (1 + leaf) if phase == 0 else (2 - leaf)
        route += [(4 * leaf + r, 4 * leaf + (r ^ apart)) for r in range(4)]
    return lax.ppermute(value, ("leaf", "row"), route)


def added(left, right):
    return left.astype(F32) + right.astype(F32)


def two_levels(rhs, pivot_inverse, panel, live, parent_map):
    columns = rhs.shape[1]
    quarter = pivot_inverse.shape[1]
    half = quarter // 2
    front = 4 * quarter
    updates = parent_map.shape[1] * B
    barrier = lax.optimization_barrier
    smem = [pltpu.SMEM(live.shape, jnp.int32), pltpu.SMEM(parent_map.shape, jnp.int32)]

    parts = 4 if updates % (4 * B) == 0 else 1
    sent, keep, b_v, masked, mask, w_v = call(
        functools.partial(panel_kernel, (quarter, half, parts, updates)),
        (
            kept(4 * half, columns),
            kept(4 * half, columns),
            kept(quarter + half, columns),
            kept(quarter, columns),
            kept(quarter, columns),
            kept(updates, quarter),
        ),
        [ANY] * 4,
        [pltpu.VMEM((front, columns), BF), *smem, pltpu.SemaphoreType.DMA((3 + parts,))],
        62_100_000,
        2 * updates * quarter * columns,
        2 * updates * quarter,
    )(live, parent_map, rhs, panel)
    got = leaf_swap(sent)
    away = added(keep[quarter:], got[quarter:]).astype(BF)
    home = added(keep[:quarter], got[:quarter])
    home = home + row_swap(away, 0).astype(F32)
    incoming = home[:half] + row_swap(home[half:].astype(BF), 1).astype(F32)
    right_side = (b_v[quarter:].astype(F32) - incoming).astype(BF)
    right_other = leaf_swap(right_side)

    send_e, keep_e, d_v = call(
        functools.partial(leaf_pivot_kernel, (quarter, half)),
        (kept(2 * quarter, columns), kept(2 * quarter, columns), kept(front + 4 * half, quarter)),
        [VMEM, ANY, ANY],
        [pltpu.SemaphoreType.DMA((5,))],
        48 * MIB,
        2 * front * quarter * columns,
        2 * front * quarter,
    )(masked, pivot_inverse, away)

    send_e, home = barrier((send_e, home))
    send_e = barrier((send_e, incoming))[0]
    home_e = keep_e.astype(F32) + row_swap(send_e, 0).astype(F32)

    send, keep = call(
        functools.partial(root_pivot_kernel, (quarter, half, front)),
        (kept(quarter, columns), kept(quarter, columns)),
        [VMEM, VMEM, VMEM],
        [pltpu.VMEM((quarter, columns), BF)],
        16 * MIB,
        front * quarter * columns,
        front * quarter,
    )(right_side, right_other, d_v)
    home = keep.astype(F32) + row_swap(send, 0).astype(F32)
    root_forward = (home[:half] + row_swap(home[half:].astype(BF), 1).astype(F32)).astype(BF)

    away_e = barrier((home_e[quarter:].astype(BF), home))[0]
    leaf_forward = home_e[:quarter] + row_swap(away_e, 1).astype(F32)
    leaf_forward = jnp.where(mask > 0, leaf_forward, 0.0).astype(BF)

    near = jnp.concatenate([root_forward, row_swap(root_forward, 1)], 0)
    far = row_swap(near, 0)
    root_keep, root_send = call(
        functools.partial(root_transposed_kernel, (quarter, half, front)),
        (kept(half, columns, F32), kept(half, columns)),
        [VMEM, VMEM, VMEM],
        [pltpu.VMEM((4 * half, columns), BF), pltpu.VMEM((quarter, columns), F32)],
        16 * MIB,
        front * quarter * columns,
        front * quarter,
    )(near, far, d_v)
    root_value = (root_keep + leaf_swap(root_send).astype(F32)).astype(BF)

    near_e = jnp.concatenate([leaf_forward, row_swap(leaf_forward, 1)], 0)
    far_e = row_swap(near_e, 0)
    panel_rows = call(
        functools.partial(scatter_kernel, (quarter, updates)),
        kept(front, quarter),
        [ANY, ANY, VMEM, ANY],
        [*smem, pltpu.SemaphoreType.DMA((2,))],
        16 * MIB,
        0,
        4 * front * quarter,
    )(live, parent_map, w_v, right_side)
    total = call(
        functools.partial(leaf_transposed_kernel, (quarter, half)),
        kept(columns, quarter, F32),
        [VMEM] * 4,
        [pltpu.VMEM((front, columns), BF)],
        16 * MIB,
        2 * front * quarter * columns,
        2 * front * quarter,
    )(near_e, far_e, d_v, mask)
    forward = jnp.concatenate([leaf_forward, root_forward], 0)

    near = jnp.concatenate([root_value, row_swap(root_value, 1)], 0)
    far = row_swap(near, 0)
    near_other = leaf_swap(near)
    scratch = [pltpu.VMEM((4 * half, columns), BF), pltpu.VMEM((4 * half, quarter), BF)]
    total = call(
        functools.partial(early_kernel, (quarter, half)),
        kept(columns, quarter, F32),
        [VMEM] * 4,
        scratch,
        16 * MIB,
        front * quarter * columns,
        front * quarter,
    )(near, near_other, total, panel_rows)
    far_other = leaf_swap(far)
    backward = call(
        functools.partial(last_kernel, (quarter, half)),
        stored(quarter + half, columns),
        [VMEM] * 5,
        scratch,
        16 * MIB,
        front * quarter * columns,
        front * quarter,
    )(far, far_other, total, panel_rows, near)
    return forward, backward


def on_device(rhs, pivot_inverse, panel, live, parent_map):
    if lax.axis_size("leaf") == 2 and lax.axis_size("row") == 4:
        return two_levels(rhs, pivot_inverse, panel, live, parent_map)
    return deep_tree(rhs, pivot_inverse, panel, live, parent_map)


def solution(mesh):
    in_specs = (P(("leaf", "row"), "col"), P("leaf", "row"), P("leaf", "row"), P(), P())
    out_specs = (P(("leaf", "row"), "col"), P(("leaf", "row"), "col"))
    return jax.shard_map(
        on_device, mesh=mesh, in_specs=in_specs, out_specs=out_specs, check_vma=False
    )
```

```python
import functools

import jax
import jax.numpy as jnp
from jax import lax
from jax.experimental import pallas as pl
from jax.experimental.pallas import tpu as pltpu
from jax.sharding import PartitionSpec as P

F = 2560
E = 1536


def from_partner(block, axis, apart):
    count = lax.axis_size(axis)
    route = []
    for low in range(count):
        high = low | 1 << apart
        if high != low and high < count:
            route += [(low, high), (high, low)]
    return lax.ppermute(block, axis, route)


def doubling(stacked, bit_count, leaf_pos, swapper):
    for bit_no in range(bit_count):
        partner = swapper(stacked, bit_no)
        upper_half = jnp.right_shift(leaf_pos, bit_no) % 2 == 1
        stacked = jnp.where(
            upper_half,
            jnp.concatenate([partner, stacked], 0),
            jnp.concatenate([stacked, partner], 0),
        )
    return stacked


def halving(partial_value, bit_count, leaf_pos, swapper):
    for bit_no in reversed(range(bit_count)):
        halves = partial_value.reshape((2, partial_value.shape[0] // 2) + partial_value.shape[1:])
        upper_half = jnp.right_shift(leaf_pos, bit_no) % 2 == 1
        kept_half = jnp.where(upper_half, halves[1], halves[0])
        sent_half = jnp.where(upper_half, halves[0], halves[1])
        partial_value = kept_half + swapper(sent_half, bit_no)
    return partial_value[0]


def to_front(group_block, row_count):
    count_g, total_rows, row_width = group_block.shape
    piece_rows = total_rows // row_count
    return (
        group_block.reshape(count_g, row_count, piece_rows, row_width)
        .transpose(1, 0, 2, 3)
        .reshape(count_g * total_rows, row_width)
    )


def block_onehot(mapping):
    return (jnp.arange(F // 128, dtype=jnp.int32)[:, None] == mapping[None, :]).astype(jnp.bfloat16)


def pivot_sum(diag_block, quarter_rows):
    return lax.psum_scatter(
        jnp.dot(diag_block, quarter_rows, preferred_element_type=jnp.float32).astype(jnp.bfloat16),
        "row",
        scatter_dimension=0,
        tiled=True,
    ).astype(jnp.float32)


def quarter_swap(values, bit_no):
    return from_partner(values, "leaf", bit_no)


def update_swap(values, bit_no):
    return from_partner(values, "leaf", bit_no)


def parent_swap(values, bit_no):
    return from_partner(values, "leaf", bit_no)


def reduce_swap(values, bit_no):
    return from_partner(values.astype(jnp.bfloat16), "leaf", bit_no).astype(values.dtype)


def deep_tree(rhs, pivot_inverse, panel, live, parent_map):
    leaves = lax.axis_size("leaf")
    row_count = lax.axis_size("row")
    tree_depth = leaves.bit_length() - 1
    leaf_pos = lax.axis_index("leaf")
    row_pos = lax.axis_index("row")
    columns = rhs.shape[1]
    quarter = F // row_count
    parent_blocks = F // 128
    child_blocks = E // 128
    layout = []
    vec_off, piv_off, pan_off, front_base = (0, 0, 0, 0)
    for level_no in range(tree_depth + 1):
        groups = 2**level_no
        layout.append((groups, vec_off, piv_off, pan_off, front_base))
        vec_off += F // (row_count * groups)
        piv_off += F // groups
        pan_off += E // groups
        front_base += leaves // groups
    forward_parts = []
    live_masks = []
    incoming = None
    for level_no in range(tree_depth + 1):
        groups, vec_off, piv_off, pan_off, front_base = layout[level_no]
        piece_rows = F // (row_count * groups)
        panel_rows = E // (row_count * groups)
        inner_pos = leaf_pos % groups
        front_no = jnp.right_shift(leaf_pos, level_no)
        live_rows = lax.dynamic_index_in_dim(live, front_base + front_no, 0, keepdims=False) * 128
        first_row = (row_pos * groups + inner_pos) * piece_rows
        live_mask = (first_row + jnp.arange(piece_rows, dtype=jnp.int32) < live_rows)[:, None]
        live_masks.append(live_mask)
        right_side = rhs[vec_off : vec_off + piece_rows]
        if incoming is not None:
            right_side = (right_side.astype(jnp.float32) - incoming).astype(jnp.bfloat16)
        masked = jnp.where(live_mask, right_side, jnp.zeros_like(right_side))
        quarter_rows = doubling(masked[None], level_no, leaf_pos, quarter_swap).reshape(
            quarter, columns
        )
        diag_block = pivot_inverse[piv_off : piv_off + F // groups]
        if level_no < tree_depth:
            off_block = panel[pan_off : pan_off + E // groups]
            forward_value = pivot_sum(diag_block, quarter_rows)
            update_rows = lax.psum(
                jnp.dot(off_block, quarter_rows, preferred_element_type=jnp.float32), "row"
            ).astype(jnp.bfloat16)
        else:
            forward_value = pivot_sum(diag_block, quarter_rows)
        forward_parts.append(jnp.where(live_mask, forward_value, 0.0).astype(jnp.bfloat16))
        if level_no < tree_depth:
            gathered = doubling(update_rows[None], level_no + 1, leaf_pos, update_swap)
            parent_front = jnp.right_shift(leaf_pos, level_no + 1)
            assembled = jnp.zeros((parent_blocks, 128, columns), jnp.float32)
            for side_no in range(2):
                child_update = to_front(
                    gathered[side_no * groups : (side_no + 1) * groups], row_count
                )
                mapping = lax.dynamic_index_in_dim(
                    parent_map, front_base + 2 * parent_front + side_no, 0, keepdims=False
                )
                assembled = assembled + jnp.einsum(
                    "ke,eab->kab",
                    block_onehot(mapping),
                    child_update.reshape(child_blocks, 128, columns),
                    preferred_element_type=jnp.float32,
                )
            parent_groups = 2 * groups
            parent_rows = F // (row_count * parent_groups)
            parent_first = (row_pos * parent_groups + leaf_pos % parent_groups) * parent_rows
            incoming = lax.dynamic_slice_in_dim(
                assembled.reshape(F, columns), parent_first, parent_rows, 0
            )
    backward_parts = [None] * (tree_depth + 1)
    parent_value = None
    for level_no in reversed(range(tree_depth + 1)):
        groups, vec_off, piv_off, pan_off, front_base = layout[level_no]
        piece_rows = F // (row_count * groups)
        panel_rows = E // (row_count * groups)
        inner_pos = leaf_pos % groups
        front_no = jnp.right_shift(leaf_pos, level_no)
        diag_block = pivot_inverse[piv_off : piv_off + F // groups]
        own_piece = forward_parts[level_no]
        if level_no == tree_depth:
            own_rows = lax.all_gather(own_piece, "row", axis=0, tiled=True)
            partial_value = jnp.einsum(
                "ik,ia->ka", diag_block, own_rows, preferred_element_type=jnp.float32
            )
        else:
            own_rows, parent_gathered = (
                lax.all_gather(own_piece, "row", axis=0, tiled=True),
                lax.all_gather(parent_value, "row", axis=0, tiled=True),
            )
            whole_parent = doubling(parent_gathered[None], level_no + 1, leaf_pos, parent_swap)
            parent_full = to_front(whole_parent, row_count)
            mapping = lax.dynamic_index_in_dim(parent_map, front_base + front_no, 0, keepdims=False)
            taken_rows = jnp.einsum(
                "ke,kab->eab",
                block_onehot(mapping),
                parent_full.reshape(parent_blocks, 128, columns),
                preferred_element_type=jnp.float32,
            ).astype(jnp.bfloat16)
            taken_rows = lax.dynamic_index_in_dim(
                taken_rows.reshape(row_count, groups, panel_rows, columns),
                inner_pos,
                1,
                keepdims=False,
            ).reshape(row_count * panel_rows, columns)
            off_block = panel[pan_off : pan_off + E // groups]
            partial_value = jnp.einsum(
                "ik,ia->ka", diag_block, own_rows, preferred_element_type=jnp.float32
            ) - jnp.einsum("ik,ia->ka", off_block, taken_rows, preferred_element_type=jnp.float32)
        if level_no == 0:
            reduced = partial_value
        else:
            reduced = halving(
                partial_value.reshape(groups, piece_rows, columns), level_no, leaf_pos, reduce_swap
            )
        parent_value = jnp.where(live_masks[level_no], reduced, 0.0).astype(jnp.bfloat16)
        backward_parts[level_no] = parent_value
    return (jnp.concatenate(forward_parts, 0), jnp.concatenate(backward_parts, 0))


B = 128
VMEM = pl.BlockSpec(memory_space=pltpu.VMEM)
ANY = pl.BlockSpec(memory_space=pl.ANY)
BF = jnp.bfloat16
F32 = jnp.float32
MIB = 1024 * 1024


def stored(rows, columns, dtype=BF):
    return jax.ShapeDtypeStruct((rows, columns), dtype)


def kept(rows, columns, dtype=BF):
    return pltpu.VMEM((rows, columns), dtype)


def call(body, out_shape, in_specs, scratch, limit, flops, bytes_moved):
    return pl.pallas_call(
        body,
        out_shape=out_shape,
        in_specs=in_specs,
        out_specs=jax.tree.map(lambda _: VMEM, out_shape, is_leaf=lambda s: hasattr(s, "shape")),
        scratch_shapes=scratch,
        compiler_params=pltpu.CompilerParams(vmem_limit_bytes=limit),
        cost_estimate=pl.CostEstimate(flops=flops, bytes_accessed=bytes_moved, transcendentals=0),
    )


def rows_at(start, size):
    return pl.ds(pl.multiple_of(start, 16), size)


def mm(left, right):
    return jnp.dot(left, right, preferred_element_type=F32)


def row_order(row_pos, leaf_pos):
    first = 1 + leaf_pos
    return (row_pos, row_pos ^ (3 - first), row_pos ^ first, row_pos ^ 3)


def panel_kernel(
    sizes,
    live,
    pmap,
    rhs,
    panel,
    pivot,
    send,
    keep,
    b_v,
    masked,
    mask,
    w_v,
    d_v,
    c_v,
    live_s,
    pmap_s,
    sems,
):
    quarter, half, parts, update_rows = sizes
    leaf_pos = lax.axis_index("leaf")
    row_pos = lax.axis_index("row")
    gets = [
        pltpu.make_async_copy(live, live_s, sems.at[0]),
        pltpu.make_async_copy(rhs, b_v, sems.at[1]),
        pltpu.make_async_copy(pmap, pmap_s, sems.at[2]),
    ]
    step = update_rows // parts
    for i in range(parts):
        rows = pl.ds(i * step, step)
        gets.append(pltpu.make_async_copy(panel.at[rows], w_v.at[rows], sems.at[3 + i]))
    gets.append(pltpu.make_async_copy(pivot, d_v, sems.at[3 + parts]))
    for get in gets:
        get.start()
    c_v[...] = jnp.zeros_like(c_v)
    gets[0].wait()
    gets[1].wait()
    value = b_v[pl.ds(0, quarter)]
    row = row_pos * quarter + lax.broadcasted_iota(jnp.int32, value.shape, 0)
    alive = row < live_s[leaf_pos] * B
    mask[...] = jnp.where(alive, 1.0, 0.0).astype(BF)
    masked[...] = jnp.where(alive, value, jnp.zeros_like(value))
    right = masked[...]
    gets[2].wait()
    for i in range(parts):
        gets[3 + i].wait()
        product = mm(w_v[pl.ds(i * step, step)], right).astype(BF)
        for e in range(step // B):
            block = pmap_s[leaf_pos, i * (step // B) + e]
            c_v[pl.ds(pl.multiple_of(block * B, B), B)] = product[e * B : (e + 1) * B]
    for out, side in ((keep, leaf_pos), (send, 1 - leaf_pos)):
        near = (row_pos ^ (1 + side)) * quarter
        out[pl.ds(0, quarter)] = c_v[rows_at(near, quarter)]
        at = side * half
        out[pl.ds(quarter, half)] = c_v[rows_at((row_pos ^ 3) * quarter + at, half)]
        out[pl.ds(quarter + half, half)] = c_v[rows_at(row_pos * quarter + at, half)]
    gets[3 + parts].wait()


def leaf_pivot_kernel(sizes, masked, d_v, after, send, keep):
    quarter, half = sizes
    order = row_order(lax.axis_index("row"), lax.axis_index("leaf"))
    right = masked[...]
    for k in (2, 3, 0, 1):
        out = keep if k < 2 else send
        product = mm(d_v[rows_at(order[k] * quarter, quarter)], right)
        out[pl.ds((k % 2) * quarter, quarter)] = product.astype(BF)


def scatter_kernel(sizes, live, pmap, w_v, after, out, live_s, pmap_s, sems):
    quarter, update_rows = sizes
    leaf_pos = lax.axis_index("leaf")
    row_pos = lax.axis_index("row")
    gets = [
        pltpu.make_async_copy(live, live_s, sems.at[0]),
        pltpu.make_async_copy(pmap, pmap_s, sems.at[1]),
    ]
    for get in gets:
        get.start()
    out[...] = jnp.zeros_like(out)
    for get in gets:
        get.wait()
    column = row_pos * quarter + lax.broadcasted_iota(jnp.int32, (B, quarter), 1)
    alive = column < live_s[leaf_pos] * B
    for e in range(update_rows // B):
        value = w_v[pl.ds(e * B, B)]
        block = pmap_s[leaf_pos, e]
        out[pl.ds(pl.multiple_of(block * B, B), B)] = jnp.where(alive, value, jnp.zeros_like(value))


def root_pivot_kernel(sizes, own, other, d_v, out):
    base, rows = sizes
    right = -(own[...].astype(F32) + other[...].astype(F32))
    out[...] = mm(d_v[pl.ds(base, rows)], right.astype(BF)).astype(BF)


def root_transposed_kernel(sizes, y, d_v, out):
    base, rows = sizes
    out[...] = mm(y[...].T, d_v[pl.ds(base, rows)]).T.astype(BF)


def leaf_transposed_kernel(sizes, near, far, d_v, mask, root_rows, panel_rows, total, y_v):
    quarter, half = sizes
    row_pos = lax.axis_index("row")
    order = row_order(row_pos, lax.axis_index("leaf"))
    for k in range(4):
        part = (near if k < 2 else far)[pl.ds((k % 2) * quarter, quarter)]
        y_v[rows_at(order[k] * quarter, quarter)] = part
    value = mm(y_v[...].T, d_v[pl.ds(0, 4 * quarter)])
    value = jnp.where(mask[...].astype(F32).T > 0.0, value, 0.0)
    own = panel_rows[rows_at(row_pos * quarter, quarter)]
    total[...] = value - mm(root_rows[...].T, own)


def last_kernel(sizes, mine, theirs, mine_far, theirs_far, total, panel_rows, root_rows, out):
    quarter, half = sizes
    leaf_pos = lax.axis_index("leaf")
    row_pos = lax.axis_index("row")
    value = total[...]
    for near, far, side in ((mine, mine_far, leaf_pos), (theirs, theirs_far, 1 - leaf_pos)):
        rows = rows_at((row_pos ^ (1 + side)) * quarter, quarter)
        value = value - mm(near[...].T, panel_rows[rows])
        rows = rows_at((row_pos ^ 3) * quarter + side * half, half)
        value = value - mm(far[...].T, panel_rows[rows])
    out[pl.ds(0, quarter)] = value.T.astype(BF)
    out[pl.ds(quarter, half)] = root_rows[rows_at(leaf_pos * half, half)]


def leaf_swap(value):
    return lax.ppermute(value, "leaf", [(0, 1), (1, 0)])


def row_swap(value, phase):
    route = []
    for leaf in range(2):
        apart = (1 + leaf, 2 - leaf, 3)[phase]
        route += [(4 * leaf + r, 4 * leaf + (r ^ apart)) for r in range(4)]
    return lax.ppermute(value, ("leaf", "row"), route)


def added(left, right):
    return left.astype(F32) + right.astype(F32)


def two_levels(rhs, pivot_inverse, panel, live, parent_map):
    columns = rhs.shape[1]
    quarter = pivot_inverse.shape[1]
    half = quarter // 2
    front = 4 * quarter
    updates = parent_map.shape[1] * B
    leaf_pos = lax.axis_index("leaf")
    row_pos = lax.axis_index("row")
    after = lambda value, other: lax.optimization_barrier((value, other))[0]
    smem = [pltpu.SMEM(live.shape, jnp.int32), pltpu.SMEM(parent_map.shape, jnp.int32)]

    parts = 4 if updates % (4 * B) == 0 else 1
    sent, keep, b_v, masked, mask, w_v, d_v = call(
        functools.partial(panel_kernel, (quarter, half, parts, updates)),
        (
            kept(4 * half, columns),
            kept(4 * half, columns),
            kept(quarter + half, columns),
            kept(quarter, columns),
            kept(quarter, columns),
            kept(updates, quarter),
            kept(front + 4 * half, quarter),
        ),
        [ANY] * 5,
        [pltpu.VMEM((front, columns), BF), *smem, pltpu.SemaphoreType.DMA((4 + parts,))],
        57_100_000,
        2 * updates * quarter * columns,
        2 * updates * quarter,
    )(live, parent_map, rhs, panel, pivot_inverse)
    got = leaf_swap(sent)
    update = added(keep, got)
    away_far = update[quarter : quarter + half].astype(BF)
    away_near = update[:quarter].astype(BF)
    from_far = row_swap(away_far, 2)
    from_near = row_swap(away_near, 0)

    send_e, keep_e = call(
        functools.partial(leaf_pivot_kernel, (quarter, half)),
        (kept(2 * quarter, columns), kept(2 * quarter, columns)),
        [VMEM, VMEM, ANY],
        [],
        16 * MIB,
        2 * front * quarter * columns,
        2 * front * quarter,
    )(masked, d_v, away_near)
    got_e = row_swap(send_e, 0)
    from_near = after(from_near, send_e)

    term = update[quarter + half :] + from_far.astype(F32) - b_v[quarter:].astype(F32)
    lower = jnp.where(leaf_pos == 0, term, 0.0)
    upper = jnp.where(leaf_pos == 0, 0.0, term)
    negated = (from_near.astype(F32) + jnp.concatenate([lower, upper], 0)).astype(BF)
    negated_other = leaf_swap(negated)

    partial = call(
        functools.partial(root_pivot_kernel, (front, 4 * half)),
        kept(4 * half, columns),
        [VMEM, VMEM, VMEM],
        [],
        16 * MIB,
        front * quarter * columns,
        front * quarter,
    )(negated, negated_other, d_v)
    home_e = added(keep_e, got_e)
    away_e = home_e[quarter:].astype(BF)
    got_e = row_swap(away_e, 1)
    panel_rows = call(
        functools.partial(scatter_kernel, (quarter, updates)),
        kept(front, quarter),
        [ANY, ANY, VMEM, ANY],
        [*smem, pltpu.SemaphoreType.DMA((2,))],
        16 * MIB,
        0,
        4 * front * quarter,
    )(live, parent_map, w_v, away_e)
    partial = added(partial, after(row_swap(partial, 0), panel_rows))
    root_forward = (partial + row_swap(partial.astype(BF), 1).astype(F32)).astype(BF)
    leaf_forward = home_e[:quarter] + got_e.astype(F32)
    leaf_forward = jnp.where(mask > 0, leaf_forward, 0.0).astype(BF)

    part = call(
        functools.partial(root_transposed_kernel, (front, 4 * half)),
        kept(quarter, columns),
        [VMEM, VMEM],
        [],
        16 * MIB,
        front * quarter * columns,
        front * quarter,
    )(root_forward, d_v)
    root_rows = added(part, leaf_swap(part)).astype(BF)

    near_e = jnp.concatenate([leaf_forward, row_swap(leaf_forward, 1)], 0)
    far_e = row_swap(near_e, 0)
    root_piece = lax.dynamic_slice_in_dim(root_forward, row_pos * half, half, 0)
    forward = jnp.concatenate([leaf_forward, root_piece], 0)

    near = row_swap(root_rows, 0)
    far = row_swap(lax.dynamic_slice_in_dim(root_rows, leaf_pos * half, half, 0), 2)
    total = call(
        functools.partial(leaf_transposed_kernel, (quarter, half)),
        kept(columns, quarter, F32),
        [VMEM] * 6,
        [pltpu.VMEM((front, columns), BF)],
        16 * MIB,
        2 * front * quarter * columns,
        2 * front * quarter,
    )(near_e, far_e, d_v, mask, root_rows, panel_rows)
    near_other = leaf_swap(near)
    far_other = leaf_swap(far)
    backward = call(
        functools.partial(last_kernel, (quarter, half)),
        stored(quarter + half, columns),
        [VMEM] * 7,
        [],
        16 * MIB,
        front * quarter * columns,
        front * quarter,
    )(near, near_other, far, far_other, total, panel_rows, root_rows)
    return forward, backward


def on_device(rhs, pivot_inverse, panel, live, parent_map):
    if lax.axis_size("leaf") == 2 and lax.axis_size("row") == 4:
        return two_levels(rhs, pivot_inverse, panel, live, parent_map)
    return deep_tree(rhs, pivot_inverse, panel, live, parent_map)


def solution(mesh):
    in_specs = (P(("leaf", "row"), "col"), P("leaf", "row"), P("leaf", "row"), P(), P())
    out_specs = (P(("leaf", "row"), "col"), P(("leaf", "row"), "col"))
    return jax.shard_map(
        on_device, mesh=mesh, in_specs=in_specs, out_specs=out_specs, check_vma=False
    )
```

```python
import functools

import jax
import jax.numpy as jnp
from jax import lax
from jax.experimental import pallas as pl
from jax.experimental.pallas import tpu as pltpu
from jax.sharding import PartitionSpec as P

F = 2560
E = 1536


def from_partner(block, axis, apart):
    count = lax.axis_size(axis)
    route = []
    for low in range(count):
        high = low | 1 << apart
        if high != low and high < count:
            route += [(low, high), (high, low)]
    return lax.ppermute(block, axis, route)


def doubling(stacked, bit_count, leaf_pos, swapper):
    for bit_no in range(bit_count):
        partner = swapper(stacked, bit_no)
        upper_half = jnp.right_shift(leaf_pos, bit_no) % 2 == 1
        stacked = jnp.where(
            upper_half,
            jnp.concatenate([partner, stacked], 0),
            jnp.concatenate([stacked, partner], 0),
        )
    return stacked


def halving(partial_value, bit_count, leaf_pos, swapper):
    for bit_no in reversed(range(bit_count)):
        halves = partial_value.reshape((2, partial_value.shape[0] // 2) + partial_value.shape[1:])
        upper_half = jnp.right_shift(leaf_pos, bit_no) % 2 == 1
        kept_half = jnp.where(upper_half, halves[1], halves[0])
        sent_half = jnp.where(upper_half, halves[0], halves[1])
        partial_value = kept_half + swapper(sent_half, bit_no)
    return partial_value[0]


def to_front(group_block, row_count):
    count_g, total_rows, row_width = group_block.shape
    piece_rows = total_rows // row_count
    return (
        group_block.reshape(count_g, row_count, piece_rows, row_width)
        .transpose(1, 0, 2, 3)
        .reshape(count_g * total_rows, row_width)
    )


def block_onehot(mapping):
    return (jnp.arange(F // 128, dtype=jnp.int32)[:, None] == mapping[None, :]).astype(jnp.bfloat16)


def pivot_sum(diag_block, quarter_rows):
    return lax.psum_scatter(
        jnp.dot(diag_block, quarter_rows, preferred_element_type=jnp.float32).astype(jnp.bfloat16),
        "row",
        scatter_dimension=0,
        tiled=True,
    ).astype(jnp.float32)


def quarter_swap(values, bit_no):
    return from_partner(values, "leaf", bit_no)


def update_swap(values, bit_no):
    return from_partner(values, "leaf", bit_no)


def parent_swap(values, bit_no):
    return from_partner(values, "leaf", bit_no)


def reduce_swap(values, bit_no):
    return from_partner(values.astype(jnp.bfloat16), "leaf", bit_no).astype(values.dtype)


def deep_tree(rhs, pivot_inverse, panel, live, parent_map):
    leaves = lax.axis_size("leaf")
    row_count = lax.axis_size("row")
    tree_depth = leaves.bit_length() - 1
    leaf_pos = lax.axis_index("leaf")
    row_pos = lax.axis_index("row")
    columns = rhs.shape[1]
    quarter = F // row_count
    parent_blocks = F // 128
    child_blocks = E // 128
    layout = []
    vec_off, piv_off, pan_off, front_base = (0, 0, 0, 0)
    for level_no in range(tree_depth + 1):
        groups = 2**level_no
        layout.append((groups, vec_off, piv_off, pan_off, front_base))
        vec_off += F // (row_count * groups)
        piv_off += F // groups
        pan_off += E // groups
        front_base += leaves // groups
    forward_parts = []
    live_masks = []
    incoming = None
    for level_no in range(tree_depth + 1):
        groups, vec_off, piv_off, pan_off, front_base = layout[level_no]
        piece_rows = F // (row_count * groups)
        panel_rows = E // (row_count * groups)
        inner_pos = leaf_pos % groups
        front_no = jnp.right_shift(leaf_pos, level_no)
        live_rows = lax.dynamic_index_in_dim(live, front_base + front_no, 0, keepdims=False) * 128
        first_row = (row_pos * groups + inner_pos) * piece_rows
        live_mask = (first_row + jnp.arange(piece_rows, dtype=jnp.int32) < live_rows)[:, None]
        live_masks.append(live_mask)
        right_side = rhs[vec_off : vec_off + piece_rows]
        if incoming is not None:
            right_side = (right_side.astype(jnp.float32) - incoming).astype(jnp.bfloat16)
        masked = jnp.where(live_mask, right_side, jnp.zeros_like(right_side))
        quarter_rows = doubling(masked[None], level_no, leaf_pos, quarter_swap).reshape(
            quarter, columns
        )
        diag_block = pivot_inverse[piv_off : piv_off + F // groups]
        if level_no < tree_depth:
            off_block = panel[pan_off : pan_off + E // groups]
            forward_value = pivot_sum(diag_block, quarter_rows)
            update_rows = lax.psum(
                jnp.dot(off_block, quarter_rows, preferred_element_type=jnp.float32), "row"
            ).astype(jnp.bfloat16)
        else:
            forward_value = pivot_sum(diag_block, quarter_rows)
        forward_parts.append(jnp.where(live_mask, forward_value, 0.0).astype(jnp.bfloat16))
        if level_no < tree_depth:
            gathered = doubling(update_rows[None], level_no + 1, leaf_pos, update_swap)
            parent_front = jnp.right_shift(leaf_pos, level_no + 1)
            assembled = jnp.zeros((parent_blocks, 128, columns), jnp.float32)
            for side_no in range(2):
                child_update = to_front(
                    gathered[side_no * groups : (side_no + 1) * groups], row_count
                )
                mapping = lax.dynamic_index_in_dim(
                    parent_map, front_base + 2 * parent_front + side_no, 0, keepdims=False
                )
                assembled = assembled + jnp.einsum(
                    "ke,eab->kab",
                    block_onehot(mapping),
                    child_update.reshape(child_blocks, 128, columns),
                    preferred_element_type=jnp.float32,
                )
            parent_groups = 2 * groups
            parent_rows = F // (row_count * parent_groups)
            parent_first = (row_pos * parent_groups + leaf_pos % parent_groups) * parent_rows
            incoming = lax.dynamic_slice_in_dim(
                assembled.reshape(F, columns), parent_first, parent_rows, 0
            )
    backward_parts = [None] * (tree_depth + 1)
    parent_value = None
    for level_no in reversed(range(tree_depth + 1)):
        groups, vec_off, piv_off, pan_off, front_base = layout[level_no]
        piece_rows = F // (row_count * groups)
        panel_rows = E // (row_count * groups)
        inner_pos = leaf_pos % groups
        front_no = jnp.right_shift(leaf_pos, level_no)
        diag_block = pivot_inverse[piv_off : piv_off + F // groups]
        own_piece = forward_parts[level_no]
        if level_no == tree_depth:
            own_rows = lax.all_gather(own_piece, "row", axis=0, tiled=True)
            partial_value = jnp.einsum(
                "ik,ia->ka", diag_block, own_rows, preferred_element_type=jnp.float32
            )
        else:
            own_rows, parent_gathered = (
                lax.all_gather(own_piece, "row", axis=0, tiled=True),
                lax.all_gather(parent_value, "row", axis=0, tiled=True),
            )
            whole_parent = doubling(parent_gathered[None], level_no + 1, leaf_pos, parent_swap)
            parent_full = to_front(whole_parent, row_count)
            mapping = lax.dynamic_index_in_dim(parent_map, front_base + front_no, 0, keepdims=False)
            taken_rows = jnp.einsum(
                "ke,kab->eab",
                block_onehot(mapping),
                parent_full.reshape(parent_blocks, 128, columns),
                preferred_element_type=jnp.float32,
            ).astype(jnp.bfloat16)
            taken_rows = lax.dynamic_index_in_dim(
                taken_rows.reshape(row_count, groups, panel_rows, columns),
                inner_pos,
                1,
                keepdims=False,
            ).reshape(row_count * panel_rows, columns)
            off_block = panel[pan_off : pan_off + E // groups]
            partial_value = jnp.einsum(
                "ik,ia->ka", diag_block, own_rows, preferred_element_type=jnp.float32
            ) - jnp.einsum("ik,ia->ka", off_block, taken_rows, preferred_element_type=jnp.float32)
        if level_no == 0:
            reduced = partial_value
        else:
            reduced = halving(
                partial_value.reshape(groups, piece_rows, columns), level_no, leaf_pos, reduce_swap
            )
        parent_value = jnp.where(live_masks[level_no], reduced, 0.0).astype(jnp.bfloat16)
        backward_parts[level_no] = parent_value
    return (jnp.concatenate(forward_parts, 0), jnp.concatenate(backward_parts, 0))


B = 128
VMEM = pl.BlockSpec(memory_space=pltpu.VMEM)
ANY = pl.BlockSpec(memory_space=pl.ANY)
BF = jnp.bfloat16
F32 = jnp.float32
MIB = 1024 * 1024


def stored(rows, columns, dtype=BF):
    return jax.ShapeDtypeStruct((rows, columns), dtype)


def kept(rows, columns, dtype=BF):
    return pltpu.VMEM((rows, columns), dtype)


def call(body, out_shape, in_specs, scratch, limit, flops, bytes_moved):
    return pl.pallas_call(
        body,
        out_shape=out_shape,
        in_specs=in_specs,
        out_specs=jax.tree.map(lambda _: VMEM, out_shape, is_leaf=lambda s: hasattr(s, "shape")),
        scratch_shapes=scratch,
        compiler_params=pltpu.CompilerParams(vmem_limit_bytes=limit),
        cost_estimate=pl.CostEstimate(flops=flops, bytes_accessed=bytes_moved, transcendentals=0),
    )


def rows_at(start, size):
    return pl.ds(pl.multiple_of(start, 16), size)


def mm(left, right):
    return jnp.dot(left, right, preferred_element_type=F32)


def row_order(row_pos, leaf_pos):
    first = 1 + leaf_pos
    return (row_pos, row_pos ^ (3 - first), row_pos ^ first, row_pos ^ 3)


def panel_kernel(
    sizes,
    live,
    pmap,
    rhs,
    panel,
    pivot,
    send,
    keep,
    b_v,
    masked,
    mask,
    w_v,
    d_v,
    c_v,
    live_s,
    pmap_s,
    sems,
):
    quarter, half, parts, update_rows = sizes
    leaf_pos = lax.axis_index("leaf")
    row_pos = lax.axis_index("row")
    gets = [
        pltpu.make_async_copy(live, live_s, sems.at[0]),
        pltpu.make_async_copy(rhs, b_v, sems.at[1]),
        pltpu.make_async_copy(pmap, pmap_s, sems.at[2]),
    ]
    step = update_rows // parts
    for i in range(parts):
        rows = pl.ds(i * step, step)
        gets.append(pltpu.make_async_copy(panel.at[rows], w_v.at[rows], sems.at[3 + i]))
    gets.append(pltpu.make_async_copy(pivot, d_v, sems.at[3 + parts]))
    for get in gets:
        get.start()
    c_v[...] = jnp.zeros_like(c_v)
    gets[0].wait()
    gets[1].wait()
    value = b_v[pl.ds(0, quarter)]
    row = row_pos * quarter + lax.broadcasted_iota(jnp.int32, value.shape, 0)
    alive = row < live_s[leaf_pos] * B
    mask[...] = jnp.where(alive, 1.0, 0.0).astype(BF)
    masked[...] = jnp.where(alive, value, jnp.zeros_like(value))
    right = masked[...]
    gets[2].wait()
    for i in range(parts):
        gets[3 + i].wait()
        product = mm(w_v[pl.ds(i * step, step)], right).astype(BF)
        for e in range(step // B):
            block = pmap_s[leaf_pos, i * (step // B) + e]
            c_v[pl.ds(pl.multiple_of(block * B, B), B)] = product[e * B : (e + 1) * B]
    for out, side in ((keep, leaf_pos), (send, 1 - leaf_pos)):
        near = (row_pos ^ (1 + side)) * quarter
        mine, other = side * half, (1 - side) * half
        out[pl.ds(0, half)] = c_v[rows_at(near + mine, half)]
        out[pl.ds(half, half)] = c_v[rows_at(near + other, half)]
        out[pl.ds(quarter, half)] = c_v[rows_at((row_pos ^ 3) * quarter + mine, half)]
        out[pl.ds(quarter + half, half)] = c_v[rows_at(row_pos * quarter + mine, half)]
    gets[3 + parts].wait()


def leaf_pivot_kernel(sizes, masked, d_v, after, send, keep):
    quarter, half = sizes
    order = row_order(lax.axis_index("row"), lax.axis_index("leaf"))
    right = masked[...]
    for k in (2, 3, 0, 1):
        out = keep if k < 2 else send
        product = mm(d_v[rows_at(order[k] * quarter, quarter)], right)
        out[pl.ds((k % 2) * quarter, quarter)] = product.astype(BF)


def scatter_kernel(sizes, live, pmap, w_v, after, out, live_s, pmap_s, sems):
    quarter, update_rows = sizes
    leaf_pos = lax.axis_index("leaf")
    row_pos = lax.axis_index("row")
    gets = [
        pltpu.make_async_copy(live, live_s, sems.at[0]),
        pltpu.make_async_copy(pmap, pmap_s, sems.at[1]),
    ]
    for get in gets:
        get.start()
    out[...] = jnp.zeros_like(out)
    for get in gets:
        get.wait()
    column = row_pos * quarter + lax.broadcasted_iota(jnp.int32, (B, quarter), 1)
    alive = column < live_s[leaf_pos] * B
    for e in range(update_rows // B):
        value = w_v[pl.ds(e * B, B)]
        block = pmap_s[leaf_pos, e]
        out[pl.ds(pl.multiple_of(block * B, B), B)] = jnp.where(alive, value, jnp.zeros_like(value))


def root_pivot_kernel(sizes, own, other, d_v, out, q_v):
    half, base = sizes
    leaf_pos = lax.axis_index("leaf")
    first, second = pl.ds(0, half), pl.ds(half, half)
    for mine, theirs, at in ((first, second, leaf_pos), (second, first, 1 - leaf_pos)):
        value = own[mine].astype(F32) + other[theirs].astype(F32)
        q_v[rows_at(at * half, half)] = (-value).astype(BF)
    out[...] = mm(d_v[pl.ds(base, 4 * half)], q_v[...]).astype(BF)


def root_transposed_kernel(sizes, y, d_v, out, piece, s_v):
    half, base = sizes
    leaf_pos = lax.axis_index("leaf")
    row_pos = lax.axis_index("row")
    piece[...] = y[rows_at(row_pos * half, half)]
    s_v[...] = mm(y[...].T, d_v[pl.ds(base, 4 * half)]).T
    out[pl.ds(0, half)] = s_v[rows_at(leaf_pos * half, half)].astype(BF)
    out[pl.ds(half, half)] = s_v[rows_at((1 - leaf_pos) * half, half)].astype(BF)


def near_product(rows, row, side, panel_rows, half):
    value = 0.0
    for k, at in enumerate((side, 1 - side)):
        part = rows[pl.ds(k * half, half)].T
        value = value + mm(part, panel_rows[rows_at((2 * row + at) * half, half)])
    return value


def leaf_transposed_kernel(sizes, near, far, d_v, mask, root_rows, panel_rows, total, y_v):
    quarter, half = sizes
    row_pos = lax.axis_index("row")
    leaf_pos = lax.axis_index("leaf")
    order = row_order(row_pos, leaf_pos)
    for k in range(4):
        part = (near if k < 2 else far)[pl.ds((k % 2) * quarter, quarter)]
        y_v[rows_at(order[k] * quarter, quarter)] = part
    value = mm(y_v[...].T, d_v[pl.ds(0, 4 * quarter)])
    value = jnp.where(mask[...].astype(F32).T > 0.0, value, 0.0)
    total[...] = value - near_product(root_rows, row_pos, leaf_pos, panel_rows, half)


def last_kernel(sizes, mine, theirs, mine_far, theirs_far, total, panel_rows, root_rows, out):
    quarter, half = sizes
    leaf_pos = lax.axis_index("leaf")
    row_pos = lax.axis_index("row")
    value = total[...]
    for near, far, side in ((mine, mine_far, leaf_pos), (theirs, theirs_far, 1 - leaf_pos)):
        value = value - near_product(near, row_pos ^ (1 + side), side, panel_rows, half)
        rows = rows_at((row_pos ^ 3) * quarter + side * half, half)
        value = value - mm(far[...].T, panel_rows[rows])
    out[pl.ds(0, quarter)] = value.T.astype(BF)
    out[pl.ds(quarter, half)] = root_rows[pl.ds(0, half)]


def leaf_swap(value):
    return lax.ppermute(value, "leaf", [(0, 1), (1, 0)])


def row_swap(value, phase):
    route = []
    for leaf in range(2):
        apart = (1 + leaf, 2 - leaf, 3)[phase]
        route += [(4 * leaf + r, 4 * leaf + (r ^ apart)) for r in range(4)]
    return lax.ppermute(value, ("leaf", "row"), route)


def added(left, right):
    return left.astype(F32) + right.astype(F32)


def two_levels(rhs, pivot_inverse, panel, live, parent_map):
    columns = rhs.shape[1]
    quarter = pivot_inverse.shape[1]
    half = quarter // 2
    front = 4 * quarter
    updates = parent_map.shape[1] * B
    after = lambda value, other: lax.optimization_barrier((value, other))[0]
    smem = [pltpu.SMEM(live.shape, jnp.int32), pltpu.SMEM(parent_map.shape, jnp.int32)]

    parts = 4 if updates % (4 * B) == 0 else 1
    sent, keep, b_v, masked, mask, w_v, d_v = call(
        functools.partial(panel_kernel, (quarter, half, parts, updates)),
        (
            kept(4 * half, columns),
            kept(4 * half, columns),
            kept(quarter + half, columns),
            kept(quarter, columns),
            kept(quarter, columns),
            kept(updates, quarter),
            kept(front + 4 * half, quarter),
        ),
        [ANY] * 5,
        [pltpu.VMEM((front, columns), BF), *smem, pltpu.SemaphoreType.DMA((4 + parts,))],
        57_100_000,
        2 * updates * quarter * columns,
        2 * updates * quarter,
    )(live, parent_map, rhs, panel, pivot_inverse)
    got = leaf_swap(sent)
    update = added(keep, got)
    away_far = update[quarter : quarter + half].astype(BF)
    away_near = update[:quarter].astype(BF)
    from_far = row_swap(away_far, 2)
    from_near = row_swap(away_near, 0)

    send_e, keep_e = call(
        functools.partial(leaf_pivot_kernel, (quarter, half)),
        (kept(2 * quarter, columns), kept(2 * quarter, columns)),
        [VMEM, VMEM, ANY],
        [],
        16 * MIB,
        2 * front * quarter * columns,
        2 * front * quarter,
    )(masked, d_v, away_near)
    got_e = row_swap(send_e, 0)
    from_near = after(from_near, send_e)

    term = update[quarter + half :] + from_far.astype(F32) - b_v[quarter:].astype(F32)
    from_near = from_near.astype(F32)
    negated = jnp.concatenate([from_near[:half] + term, from_near[half:]], 0).astype(BF)
    negated_other = leaf_swap(negated)

    partial = call(
        functools.partial(root_pivot_kernel, (half, front)),
        kept(4 * half, columns),
        [VMEM, VMEM, VMEM],
        [pltpu.VMEM((quarter, columns), BF)],
        16 * MIB,
        front * quarter * columns,
        front * quarter,
    )(negated, negated_other, d_v)
    home_e = added(keep_e, got_e)
    away_e = home_e[quarter:].astype(BF)
    got_e = row_swap(away_e, 1)
    panel_rows = call(
        functools.partial(scatter_kernel, (quarter, updates)),
        kept(front, quarter),
        [ANY, ANY, VMEM, ANY],
        [*smem, pltpu.SemaphoreType.DMA((2,))],
        16 * MIB,
        0,
        4 * front * quarter,
    )(live, parent_map, w_v, away_e)
    partial = added(partial, after(row_swap(partial, 0), panel_rows))
    root_forward = (partial + row_swap(partial.astype(BF), 1).astype(F32)).astype(BF)
    leaf_forward = home_e[:quarter] + got_e.astype(F32)
    leaf_forward = jnp.where(mask > 0, leaf_forward, 0.0).astype(BF)

    part, root_piece = call(
        functools.partial(root_transposed_kernel, (half, front)),
        (kept(quarter, columns), kept(half, columns)),
        [VMEM, VMEM],
        [pltpu.VMEM((quarter, columns), F32)],
        16 * MIB,
        front * quarter * columns,
        front * quarter,
    )(root_forward, d_v)
    got = leaf_swap(part)
    root_mine = added(part[:half], got[half:]).astype(BF)
    root_other = added(part[half:], got[:half]).astype(BF)
    root_rows = jnp.concatenate([root_mine, root_other], 0)

    near_e = jnp.concatenate([leaf_forward, row_swap(leaf_forward, 1)], 0)
    far_e = row_swap(near_e, 0)
    forward = jnp.concatenate([leaf_forward, root_piece], 0)

    near = row_swap(root_rows, 0)
    far = row_swap(root_mine, 2)
    total = call(
        functools.partial(leaf_transposed_kernel, (quarter, half)),
        kept(columns, quarter, F32),
        [VMEM] * 6,
        [pltpu.VMEM((front, columns), BF)],
        16 * MIB,
        2 * front * quarter * columns,
        2 * front * quarter,
    )(near_e, far_e, d_v, mask, root_rows, panel_rows)
    near_other = leaf_swap(near)
    far_other = leaf_swap(far)
    backward = call(
        functools.partial(last_kernel, (quarter, half)),
        stored(quarter + half, columns),
        [VMEM] * 7,
        [],
        16 * MIB,
        front * quarter * columns,
        front * quarter,
    )(near, near_other, far, far_other, total, panel_rows, root_rows)
    return forward, backward


def on_device(rhs, pivot_inverse, panel, live, parent_map):
    if lax.axis_size("leaf") == 2 and lax.axis_size("row") == 4:
        return two_levels(rhs, pivot_inverse, panel, live, parent_map)
    return deep_tree(rhs, pivot_inverse, panel, live, parent_map)


def solution(mesh):
    in_specs = (P(("leaf", "row"), "col"), P("leaf", "row"), P("leaf", "row"), P(), P())
    out_specs = (P(("leaf", "row"), "col"), P(("leaf", "row"), "col"))
    return jax.shard_map(
        on_device, mesh=mesh, in_specs=in_specs, out_specs=out_specs, check_vma=False
    )
```

```python
import functools

import jax
import jax.numpy as jnp
from jax import lax
from jax.experimental import pallas as pl
from jax.experimental.pallas import tpu as pltpu
from jax.sharding import PartitionSpec as P

F = 2560
E = 1536


def from_partner(block, axis, apart):
    count = lax.axis_size(axis)
    route = []
    for low in range(count):
        high = low | 1 << apart
        if high != low and high < count:
            route += [(low, high), (high, low)]
    return lax.ppermute(block, axis, route)


def doubling(stacked, bit_count, leaf_pos, swapper):
    for bit_no in range(bit_count):
        partner = swapper(stacked, bit_no)
        upper_half = jnp.right_shift(leaf_pos, bit_no) % 2 == 1
        stacked = jnp.where(
            upper_half,
            jnp.concatenate([partner, stacked], 0),
            jnp.concatenate([stacked, partner], 0),
        )
    return stacked


def halving(partial_value, bit_count, leaf_pos, swapper):
    for bit_no in reversed(range(bit_count)):
        halves = partial_value.reshape((2, partial_value.shape[0] // 2) + partial_value.shape[1:])
        upper_half = jnp.right_shift(leaf_pos, bit_no) % 2 == 1
        kept_half = jnp.where(upper_half, halves[1], halves[0])
        sent_half = jnp.where(upper_half, halves[0], halves[1])
        partial_value = kept_half + swapper(sent_half, bit_no)
    return partial_value[0]


def to_front(group_block, row_count):
    count_g, total_rows, row_width = group_block.shape
    piece_rows = total_rows // row_count
    return (
        group_block.reshape(count_g, row_count, piece_rows, row_width)
        .transpose(1, 0, 2, 3)
        .reshape(count_g * total_rows, row_width)
    )


def block_onehot(mapping):
    return (jnp.arange(F // 128, dtype=jnp.int32)[:, None] == mapping[None, :]).astype(jnp.bfloat16)


def pivot_sum(diag_block, quarter_rows):
    return lax.psum_scatter(
        jnp.dot(diag_block, quarter_rows, preferred_element_type=jnp.float32).astype(jnp.bfloat16),
        "row",
        scatter_dimension=0,
        tiled=True,
    ).astype(jnp.float32)


def quarter_swap(values, bit_no):
    return from_partner(values, "leaf", bit_no)


def update_swap(values, bit_no):
    return from_partner(values, "leaf", bit_no)


def parent_swap(values, bit_no):
    return from_partner(values, "leaf", bit_no)


def reduce_swap(values, bit_no):
    return from_partner(values.astype(jnp.bfloat16), "leaf", bit_no).astype(values.dtype)


def deep_tree(rhs, pivot_inverse, panel, live, parent_map):
    leaves = lax.axis_size("leaf")
    row_count = lax.axis_size("row")
    tree_depth = leaves.bit_length() - 1
    leaf_pos = lax.axis_index("leaf")
    row_pos = lax.axis_index("row")
    columns = rhs.shape[1]
    quarter = F // row_count
    parent_blocks = F // 128
    child_blocks = E // 128
    layout = []
    vec_off, piv_off, pan_off, front_base = (0, 0, 0, 0)
    for level_no in range(tree_depth + 1):
        groups = 2**level_no
        layout.append((groups, vec_off, piv_off, pan_off, front_base))
        vec_off += F // (row_count * groups)
        piv_off += F // groups
        pan_off += E // groups
        front_base += leaves // groups
    forward_parts = []
    live_masks = []
    incoming = None
    for level_no in range(tree_depth + 1):
        groups, vec_off, piv_off, pan_off, front_base = layout[level_no]
        piece_rows = F // (row_count * groups)
        panel_rows = E // (row_count * groups)
        inner_pos = leaf_pos % groups
        front_no = jnp.right_shift(leaf_pos, level_no)
        live_rows = lax.dynamic_index_in_dim(live, front_base + front_no, 0, keepdims=False) * 128
        first_row = (row_pos * groups + inner_pos) * piece_rows
        live_mask = (first_row + jnp.arange(piece_rows, dtype=jnp.int32) < live_rows)[:, None]
        live_masks.append(live_mask)
        right_side = rhs[vec_off : vec_off + piece_rows]
        if incoming is not None:
            right_side = (right_side.astype(jnp.float32) - incoming).astype(jnp.bfloat16)
        masked = jnp.where(live_mask, right_side, jnp.zeros_like(right_side))
        quarter_rows = doubling(masked[None], level_no, leaf_pos, quarter_swap).reshape(
            quarter, columns
        )
        diag_block = pivot_inverse[piv_off : piv_off + F // groups]
        if level_no < tree_depth:
            off_block = panel[pan_off : pan_off + E // groups]
            forward_value = pivot_sum(diag_block, quarter_rows)
            update_rows = lax.psum(
                jnp.dot(off_block, quarter_rows, preferred_element_type=jnp.float32), "row"
            ).astype(jnp.bfloat16)
        else:
            forward_value = pivot_sum(diag_block, quarter_rows)
        forward_parts.append(jnp.where(live_mask, forward_value, 0.0).astype(jnp.bfloat16))
        if level_no < tree_depth:
            gathered = doubling(update_rows[None], level_no + 1, leaf_pos, update_swap)
            parent_front = jnp.right_shift(leaf_pos, level_no + 1)
            assembled = jnp.zeros((parent_blocks, 128, columns), jnp.float32)
            for side_no in range(2):
                child_update = to_front(
                    gathered[side_no * groups : (side_no + 1) * groups], row_count
                )
                mapping = lax.dynamic_index_in_dim(
                    parent_map, front_base + 2 * parent_front + side_no, 0, keepdims=False
                )
                assembled = assembled + jnp.einsum(
                    "ke,eab->kab",
                    block_onehot(mapping),
                    child_update.reshape(child_blocks, 128, columns),
                    preferred_element_type=jnp.float32,
                )
            parent_groups = 2 * groups
            parent_rows = F // (row_count * parent_groups)
            parent_first = (row_pos * parent_groups + leaf_pos % parent_groups) * parent_rows
            incoming = lax.dynamic_slice_in_dim(
                assembled.reshape(F, columns), parent_first, parent_rows, 0
            )
    backward_parts = [None] * (tree_depth + 1)
    parent_value = None
    for level_no in reversed(range(tree_depth + 1)):
        groups, vec_off, piv_off, pan_off, front_base = layout[level_no]
        piece_rows = F // (row_count * groups)
        panel_rows = E // (row_count * groups)
        inner_pos = leaf_pos % groups
        front_no = jnp.right_shift(leaf_pos, level_no)
        diag_block = pivot_inverse[piv_off : piv_off + F // groups]
        own_piece = forward_parts[level_no]
        if level_no == tree_depth:
            own_rows = lax.all_gather(own_piece, "row", axis=0, tiled=True)
            partial_value = jnp.einsum(
                "ik,ia->ka", diag_block, own_rows, preferred_element_type=jnp.float32
            )
        else:
            own_rows, parent_gathered = (
                lax.all_gather(own_piece, "row", axis=0, tiled=True),
                lax.all_gather(parent_value, "row", axis=0, tiled=True),
            )
            whole_parent = doubling(parent_gathered[None], level_no + 1, leaf_pos, parent_swap)
            parent_full = to_front(whole_parent, row_count)
            mapping = lax.dynamic_index_in_dim(parent_map, front_base + front_no, 0, keepdims=False)
            taken_rows = jnp.einsum(
                "ke,kab->eab",
                block_onehot(mapping),
                parent_full.reshape(parent_blocks, 128, columns),
                preferred_element_type=jnp.float32,
            ).astype(jnp.bfloat16)
            taken_rows = lax.dynamic_index_in_dim(
                taken_rows.reshape(row_count, groups, panel_rows, columns),
                inner_pos,
                1,
                keepdims=False,
            ).reshape(row_count * panel_rows, columns)
            off_block = panel[pan_off : pan_off + E // groups]
            partial_value = jnp.einsum(
                "ik,ia->ka", diag_block, own_rows, preferred_element_type=jnp.float32
            ) - jnp.einsum("ik,ia->ka", off_block, taken_rows, preferred_element_type=jnp.float32)
        if level_no == 0:
            reduced = partial_value
        else:
            reduced = halving(
                partial_value.reshape(groups, piece_rows, columns), level_no, leaf_pos, reduce_swap
            )
        parent_value = jnp.where(live_masks[level_no], reduced, 0.0).astype(jnp.bfloat16)
        backward_parts[level_no] = parent_value
    return (jnp.concatenate(forward_parts, 0), jnp.concatenate(backward_parts, 0))


B = 128
VMEM = pl.BlockSpec(memory_space=pltpu.VMEM)
ANY = pl.BlockSpec(memory_space=pl.ANY)
BF = jnp.bfloat16
F32 = jnp.float32
MIB = 1024 * 1024


def stored(rows, columns, dtype=BF):
    return jax.ShapeDtypeStruct((rows, columns), dtype)


def kept(rows, columns, dtype=BF):
    return pltpu.VMEM((rows, columns), dtype)


def call(body, out_shape, in_specs, scratch, limit, flops, bytes_moved):
    return pl.pallas_call(
        body,
        out_shape=out_shape,
        in_specs=in_specs,
        out_specs=jax.tree.map(lambda _: VMEM, out_shape, is_leaf=lambda s: hasattr(s, "shape")),
        scratch_shapes=scratch,
        compiler_params=pltpu.CompilerParams(vmem_limit_bytes=limit),
        cost_estimate=pl.CostEstimate(flops=flops, bytes_accessed=bytes_moved, transcendentals=0),
    )


def rows_at(start, size):
    return pl.ds(pl.multiple_of(start, 16), size)


def mm(left, right):
    return jnp.dot(left, right, preferred_element_type=F32)


def row_order(row_pos, leaf_pos):
    return (row_pos, row_pos ^ (1 + leaf_pos), row_pos ^ (2 - leaf_pos), row_pos ^ 3)


def panel_kernel(
    sizes,
    live,
    pmap,
    rhs,
    panel,
    pivot,
    send,
    keep,
    b_v,
    masked,
    mask,
    w_v,
    d_v,
    c_v,
    live_s,
    pmap_s,
    sems,
):
    quarter, half, parts, update_rows = sizes
    leaf_pos = lax.axis_index("leaf")
    row_pos = lax.axis_index("row")
    gets = [
        pltpu.make_async_copy(live, live_s, sems.at[0]),
        pltpu.make_async_copy(rhs, b_v, sems.at[1]),
        pltpu.make_async_copy(pmap, pmap_s, sems.at[2]),
    ]
    step = update_rows // parts
    for i in range(parts):
        rows = pl.ds(i * step, step)
        gets.append(pltpu.make_async_copy(panel.at[rows], w_v.at[rows], sems.at[3 + i]))
    gets.append(pltpu.make_async_copy(pivot, d_v, sems.at[3 + parts]))
    for get in gets:
        get.start()
    c_v[...] = jnp.zeros_like(c_v)
    gets[0].wait()
    gets[1].wait()
    value = b_v[pl.ds(0, quarter)]
    row = row_pos * quarter + lax.broadcasted_iota(jnp.int32, value.shape, 0)
    alive = row < live_s[leaf_pos] * B
    mask[...] = jnp.where(alive, 1.0, 0.0).astype(BF)
    masked[...] = jnp.where(alive, value, jnp.zeros_like(value))
    right = masked[...]
    gets[2].wait()
    for i in range(parts):
        gets[3 + i].wait()
        product = mm(w_v[pl.ds(i * step, step)], right).astype(BF)
        for e in range(step // B):
            block = pmap_s[leaf_pos, i * (step // B) + e]
            c_v[pl.ds(pl.multiple_of(block * B, B), B)] = product[e * B : (e + 1) * B]
    for out, side in ((keep, leaf_pos), (send, 1 - leaf_pos)):
        near = (row_pos ^ (1 + side)) * quarter
        mine, other = side * half, (1 - side) * half
        out[pl.ds(0, half)] = c_v[rows_at(near + mine, half)]
        out[pl.ds(half, half)] = c_v[rows_at(near + other, half)]
        out[pl.ds(quarter, half)] = c_v[rows_at((row_pos ^ 3) * quarter + mine, half)]
        out[pl.ds(quarter + half, half)] = c_v[rows_at(row_pos * quarter + mine, half)]
    gets[3 + parts].wait()


def leaf_pivot_kernel(sizes, masked, d_v, after, *outs):
    quarter = sizes
    order = row_order(lax.axis_index("row"), lax.axis_index("leaf"))
    right = masked[...]
    for k in (3, 1, 2, 0):
        product = mm(d_v[rows_at(order[k] * quarter, quarter)], right)
        outs[k][...] = product.astype(BF)


def scatter_kernel(sizes, live, pmap, w_v, after, out, live_s, pmap_s, sems):
    quarter, update_rows = sizes
    leaf_pos = lax.axis_index("leaf")
    row_pos = lax.axis_index("row")
    gets = [
        pltpu.make_async_copy(live, live_s, sems.at[0]),
        pltpu.make_async_copy(pmap, pmap_s, sems.at[1]),
    ]
    for get in gets:
        get.start()
    per_row = quarter // B
    out[...] = jnp.zeros_like(out)
    for get in gets:
        get.wait()
    column = row_pos * quarter + lax.broadcasted_iota(jnp.int32, (B, quarter), 1)
    alive = column < live_s[leaf_pos] * B
    for e in range(update_rows // B):
        value = w_v[pl.ds(e * B, B)]
        block = pmap_s[leaf_pos, e]
        away = (block // per_row) ^ row_pos
        slot = jnp.where(away == 1 + leaf_pos, 1, jnp.where(away == 2 - leaf_pos, 2, away))
        at = (slot * per_row + block % per_row) * B
        out[pl.ds(pl.multiple_of(at, B), B)] = jnp.where(alive, value, jnp.zeros_like(value))


def root_pivot_kernel(sizes, mine, yours, other_mine, other_yours, d_v, out, q_v):
    half, base = sizes
    leaf_pos = lax.axis_index("leaf")
    for own, other, at in ((mine, other_yours, leaf_pos), (yours, other_mine, 1 - leaf_pos)):
        value = own[...].astype(F32) + other[...].astype(F32)
        q_v[rows_at(at * half, half)] = (-value).astype(BF)
    out[...] = mm(d_v[pl.ds(base, 4 * half)], q_v[...]).astype(BF)


def root_transposed_kernel(sizes, y, d_v, out, piece, s_v):
    half, base = sizes
    leaf_pos = lax.axis_index("leaf")
    row_pos = lax.axis_index("row")
    piece[...] = y[rows_at(row_pos * half, half)]
    s_v[...] = mm(y[...].T, d_v[pl.ds(base, 4 * half)]).T
    out[pl.ds(0, half)] = s_v[rows_at(leaf_pos * half, half)].astype(BF)
    out[pl.ds(half, half)] = s_v[rows_at((1 - leaf_pos) * half, half)].astype(BF)


def put(target, slot, half, source, order):
    for k, side in enumerate(order):
        at = 2 * slot * half + side * half
        target[rows_at(at, half)] = source[pl.ds(k * half, half)]


def leaf_transposed_kernel(
    sizes, near, far, d_v, mask, root_rows, panel_rows, root_piece, total, forward, y_v, s_v
):
    quarter, half = sizes
    row_pos = lax.axis_index("row")
    leaf_pos = lax.axis_index("leaf")
    order = row_order(row_pos, leaf_pos)
    own = near[pl.ds(0, quarter)]
    forward[pl.ds(0, quarter)] = own
    forward[pl.ds(quarter, half)] = root_piece[...]
    for k, part in enumerate(
        (own, near[pl.ds(quarter, quarter)], far[pl.ds(0, quarter)], far[pl.ds(quarter, quarter)])
    ):
        y_v[rows_at(order[(0, 2, 1, 3)[k]] * quarter, quarter)] = part
    value = mm(y_v[...].T, d_v[pl.ds(0, 4 * quarter)])
    value = jnp.where(mask[...].astype(F32).T > 0.0, value, 0.0)
    put(s_v, 0, half, root_rows, (leaf_pos, 1 - leaf_pos))
    total[...] = value - mm(s_v[...].T, panel_rows[pl.ds(0, quarter)])


def last_kernel(sizes, mine, theirs, mine_far, theirs_far, total, panel_rows, root_rows, out, s_v):
    quarter, half = sizes
    leaf_pos = lax.axis_index("leaf")
    put(s_v, 1, half, mine, (leaf_pos, 1 - leaf_pos))
    put(s_v, 0, half, theirs, (1 - leaf_pos, leaf_pos))
    put(s_v, 2, half, mine_far, (leaf_pos,))
    put(s_v, 2, half, theirs_far, (1 - leaf_pos,))
    value = total[...] - mm(s_v[...].T, panel_rows[pl.ds(quarter, 3 * quarter)])
    out[pl.ds(0, quarter)] = value.T.astype(BF)
    out[pl.ds(quarter, half)] = root_rows[pl.ds(0, half)]


def leaf_swap(value):
    return lax.ppermute(value, "leaf", [(0, 1), (1, 0)])


def row_swap(value, phase):
    route = []
    for leaf in range(2):
        apart = (1 + leaf, 2 - leaf, 3)[phase]
        route += [(4 * leaf + r, 4 * leaf + (r ^ apart)) for r in range(4)]
    return lax.ppermute(value, ("leaf", "row"), route)


def added(left, right):
    return left.astype(F32) + right.astype(F32)


def two_levels(rhs, pivot_inverse, panel, live, parent_map):
    columns = rhs.shape[1]
    quarter = pivot_inverse.shape[1]
    half = quarter // 2
    front = 4 * quarter
    updates = parent_map.shape[1] * B
    after = lambda value, other: lax.optimization_barrier((value, other))[0]
    smem = [pltpu.SMEM(live.shape, jnp.int32), pltpu.SMEM(parent_map.shape, jnp.int32)]

    parts = 4 if updates % (4 * B) == 0 else 1
    sent, keep, b_v, masked, mask, w_v, d_v = call(
        functools.partial(panel_kernel, (quarter, half, parts, updates)),
        (
            kept(4 * half, columns),
            kept(4 * half, columns),
            kept(quarter + half, columns),
            kept(quarter, columns),
            kept(quarter, columns),
            kept(updates, quarter),
            kept(front + 4 * half, quarter),
        ),
        [ANY] * 5,
        [pltpu.VMEM((front, columns), BF), *smem, pltpu.SemaphoreType.DMA((4 + parts,))],
        57_100_000,
        2 * updates * quarter * columns,
        2 * updates * quarter,
    )(live, parent_map, rhs, panel, pivot_inverse)
    got = leaf_swap(sent)
    update = added(keep, got)
    away_far = update[quarter : quarter + half].astype(BF)
    away_near = update[:quarter].astype(BF)
    from_far = row_swap(away_far, 2)
    from_near = row_swap(away_near, 0)

    pieces = call(
        functools.partial(leaf_pivot_kernel, quarter),
        (kept(quarter, columns),) * 4,
        [VMEM, VMEM, ANY],
        [],
        16 * MIB,
        2 * front * quarter * columns,
        2 * front * quarter,
    )(masked, d_v, away_near)
    from_near = after(from_near, pieces[0])
    leaf_forward = pieces[0].astype(F32)
    for phase in (2, 0, 1):
        leaf_forward = leaf_forward + row_swap(pieces[1 + phase], phase).astype(F32)
    leaf_forward = jnp.where(mask > 0, leaf_forward, 0.0).astype(BF)
    near_e = jnp.concatenate([leaf_forward, row_swap(leaf_forward, 1)], 0)
    far_e = row_swap(near_e, 0)

    term = update[quarter + half :] + from_far.astype(F32) - b_v[quarter:].astype(F32)
    from_near = from_near.astype(F32)
    negated_mine = (from_near[:half] + term).astype(BF)
    negated_yours = from_near[half:].astype(BF)
    other_yours = leaf_swap(negated_yours)
    other_mine = leaf_swap(negated_mine)

    partial = call(
        functools.partial(root_pivot_kernel, (half, front)),
        kept(4 * half, columns),
        [VMEM] * 5,
        [pltpu.VMEM((quarter, columns), BF)],
        16 * MIB,
        0,
        0,
    )(negated_mine, negated_yours, other_mine, other_yours, d_v)
    panel_rows = call(
        functools.partial(scatter_kernel, (quarter, updates)),
        kept(front, quarter),
        [ANY, ANY, VMEM, ANY],
        [*smem, pltpu.SemaphoreType.DMA((2,))],
        16 * MIB,
        0,
        0,
    )(live, parent_map, w_v, leaf_forward)
    partial = added(partial, after(row_swap(partial, 1), panel_rows))
    got = after(row_swap(partial.astype(BF), 0), near_e)
    root_forward = (partial + got.astype(F32)).astype(BF)

    part, root_piece = call(
        functools.partial(root_transposed_kernel, (half, front)),
        (kept(quarter, columns), kept(half, columns)),
        [VMEM, VMEM],
        [pltpu.VMEM((quarter, columns), F32)],
        16 * MIB,
        0,
        0,
    )(root_forward, d_v)
    got = leaf_swap(part)
    root_mine = added(part[:half], got[half:]).astype(BF)
    root_other = added(part[half:], got[:half]).astype(BF)
    root_rows = jnp.concatenate([root_mine, root_other], 0)

    near = row_swap(root_rows, 1)
    far = row_swap(root_mine, 2)
    total, forward = call(
        functools.partial(leaf_transposed_kernel, (quarter, half)),
        (kept(columns, quarter, F32), stored(quarter + half, columns)),
        [VMEM] * 7,
        [pltpu.VMEM((front, columns), BF), pltpu.VMEM((quarter, columns), BF)],
        16 * MIB,
        2 * front * quarter * columns,
        2 * front * quarter,
    )(near_e, far_e, d_v, mask, root_rows, panel_rows, root_piece)
    near = after(near, total)
    near_other = leaf_swap(near)
    far_other = leaf_swap(far)
    backward = call(
        functools.partial(last_kernel, (quarter, half)),
        stored(quarter + half, columns),
        [VMEM] * 7,
        [pltpu.VMEM((3 * quarter, columns), BF)],
        16 * MIB,
        front * quarter * columns,
        front * quarter,
    )(near, near_other, far, far_other, total, panel_rows, root_rows)
    return forward, backward


def on_device(rhs, pivot_inverse, panel, live, parent_map):
    if lax.axis_size("leaf") == 2 and lax.axis_size("row") == 4:
        return two_levels(rhs, pivot_inverse, panel, live, parent_map)
    return deep_tree(rhs, pivot_inverse, panel, live, parent_map)


def solution(mesh):
    in_specs = (P(("leaf", "row"), "col"), P("leaf", "row"), P("leaf", "row"), P(), P())
    out_specs = (P(("leaf", "row"), "col"), P(("leaf", "row"), "col"))
    return jax.shard_map(
        on_device, mesh=mesh, in_specs=in_specs, out_specs=out_specs, check_vma=False
    )
```

```python
import functools

import jax
import jax.numpy as jnp
from jax import lax
from jax.experimental import pallas as pl
from jax.experimental.pallas import tpu as pltpu
from jax.sharding import PartitionSpec as P

F = 2560
E = 1536


def from_partner(block, axis, apart):
    count = lax.axis_size(axis)
    route = []
    for low in range(count):
        high = low | 1 << apart
        if high != low and high < count:
            route += [(low, high), (high, low)]
    return lax.ppermute(block, axis, route)


def doubling(stacked, bit_count, leaf_pos, swapper):
    for bit_no in range(bit_count):
        partner = swapper(stacked, bit_no)
        upper_half = jnp.right_shift(leaf_pos, bit_no) % 2 == 1
        stacked = jnp.where(
            upper_half,
            jnp.concatenate([partner, stacked], 0),
            jnp.concatenate([stacked, partner], 0),
        )
    return stacked


def halving(partial_value, bit_count, leaf_pos, swapper):
    for bit_no in reversed(range(bit_count)):
        halves = partial_value.reshape((2, partial_value.shape[0] // 2) + partial_value.shape[1:])
        upper_half = jnp.right_shift(leaf_pos, bit_no) % 2 == 1
        kept_half = jnp.where(upper_half, halves[1], halves[0])
        sent_half = jnp.where(upper_half, halves[0], halves[1])
        partial_value = kept_half + swapper(sent_half, bit_no)
    return partial_value[0]


def to_front(group_block, row_count):
    count_g, total_rows, row_width = group_block.shape
    piece_rows = total_rows // row_count
    return (
        group_block.reshape(count_g, row_count, piece_rows, row_width)
        .transpose(1, 0, 2, 3)
        .reshape(count_g * total_rows, row_width)
    )


def block_onehot(mapping):
    return (jnp.arange(F // 128, dtype=jnp.int32)[:, None] == mapping[None, :]).astype(jnp.bfloat16)


def pivot_sum(diag_block, quarter_rows):
    return lax.psum_scatter(
        jnp.dot(diag_block, quarter_rows, preferred_element_type=jnp.float32).astype(jnp.bfloat16),
        "row",
        scatter_dimension=0,
        tiled=True,
    ).astype(jnp.float32)


def quarter_swap(values, bit_no):
    return from_partner(values, "leaf", bit_no)


def update_swap(values, bit_no):
    return from_partner(values, "leaf", bit_no)


def parent_swap(values, bit_no):
    return from_partner(values, "leaf", bit_no)


def reduce_swap(values, bit_no):
    return from_partner(values.astype(jnp.bfloat16), "leaf", bit_no).astype(values.dtype)


def deep_tree(rhs, pivot_inverse, panel, live, parent_map):
    leaves = lax.axis_size("leaf")
    row_count = lax.axis_size("row")
    tree_depth = leaves.bit_length() - 1
    leaf_pos = lax.axis_index("leaf")
    row_pos = lax.axis_index("row")
    columns = rhs.shape[1]
    quarter = F // row_count
    parent_blocks = F // 128
    child_blocks = E // 128
    layout = []
    vec_off, piv_off, pan_off, front_base = (0, 0, 0, 0)
    for level_no in range(tree_depth + 1):
        groups = 2**level_no
        layout.append((groups, vec_off, piv_off, pan_off, front_base))
        vec_off += F // (row_count * groups)
        piv_off += F // groups
        pan_off += E // groups
        front_base += leaves // groups
    forward_parts = []
    live_masks = []
    incoming = None
    for level_no in range(tree_depth + 1):
        groups, vec_off, piv_off, pan_off, front_base = layout[level_no]
        piece_rows = F // (row_count * groups)
        panel_rows = E // (row_count * groups)
        inner_pos = leaf_pos % groups
        front_no = jnp.right_shift(leaf_pos, level_no)
        live_rows = lax.dynamic_index_in_dim(live, front_base + front_no, 0, keepdims=False) * 128
        first_row = (row_pos * groups + inner_pos) * piece_rows
        live_mask = (first_row + jnp.arange(piece_rows, dtype=jnp.int32) < live_rows)[:, None]
        live_masks.append(live_mask)
        right_side = rhs[vec_off : vec_off + piece_rows]
        if incoming is not None:
            right_side = (right_side.astype(jnp.float32) - incoming).astype(jnp.bfloat16)
        masked = jnp.where(live_mask, right_side, jnp.zeros_like(right_side))
        quarter_rows = doubling(masked[None], level_no, leaf_pos, quarter_swap).reshape(
            quarter, columns
        )
        diag_block = pivot_inverse[piv_off : piv_off + F // groups]
        if level_no < tree_depth:
            off_block = panel[pan_off : pan_off + E // groups]
            forward_value = pivot_sum(diag_block, quarter_rows)
            update_rows = lax.psum(
                jnp.dot(off_block, quarter_rows, preferred_element_type=jnp.float32), "row"
            ).astype(jnp.bfloat16)
        else:
            forward_value = pivot_sum(diag_block, quarter_rows)
        forward_parts.append(jnp.where(live_mask, forward_value, 0.0).astype(jnp.bfloat16))
        if level_no < tree_depth:
            gathered = doubling(update_rows[None], level_no + 1, leaf_pos, update_swap)
            parent_front = jnp.right_shift(leaf_pos, level_no + 1)
            assembled = jnp.zeros((parent_blocks, 128, columns), jnp.float32)
            for side_no in range(2):
                child_update = to_front(
                    gathered[side_no * groups : (side_no + 1) * groups], row_count
                )
                mapping = lax.dynamic_index_in_dim(
                    parent_map, front_base + 2 * parent_front + side_no, 0, keepdims=False
                )
                assembled = assembled + jnp.einsum(
                    "ke,eab->kab",
                    block_onehot(mapping),
                    child_update.reshape(child_blocks, 128, columns),
                    preferred_element_type=jnp.float32,
                )
            parent_groups = 2 * groups
            parent_rows = F // (row_count * parent_groups)
            parent_first = (row_pos * parent_groups + leaf_pos % parent_groups) * parent_rows
            incoming = lax.dynamic_slice_in_dim(
                assembled.reshape(F, columns), parent_first, parent_rows, 0
            )
    backward_parts = [None] * (tree_depth + 1)
    parent_value = None
    for level_no in reversed(range(tree_depth + 1)):
        groups, vec_off, piv_off, pan_off, front_base = layout[level_no]
        piece_rows = F // (row_count * groups)
        panel_rows = E // (row_count * groups)
        inner_pos = leaf_pos % groups
        front_no = jnp.right_shift(leaf_pos, level_no)
        diag_block = pivot_inverse[piv_off : piv_off + F // groups]
        own_piece = forward_parts[level_no]
        if level_no == tree_depth:
            own_rows = lax.all_gather(own_piece, "row", axis=0, tiled=True)
            partial_value = jnp.einsum(
                "ik,ia->ka", diag_block, own_rows, preferred_element_type=jnp.float32
            )
        else:
            own_rows, parent_gathered = (
                lax.all_gather(own_piece, "row", axis=0, tiled=True),
                lax.all_gather(parent_value, "row", axis=0, tiled=True),
            )
            whole_parent = doubling(parent_gathered[None], level_no + 1, leaf_pos, parent_swap)
            parent_full = to_front(whole_parent, row_count)
            mapping = lax.dynamic_index_in_dim(parent_map, front_base + front_no, 0, keepdims=False)
            taken_rows = jnp.einsum(
                "ke,kab->eab",
                block_onehot(mapping),
                parent_full.reshape(parent_blocks, 128, columns),
                preferred_element_type=jnp.float32,
            ).astype(jnp.bfloat16)
            taken_rows = lax.dynamic_index_in_dim(
                taken_rows.reshape(row_count, groups, panel_rows, columns),
                inner_pos,
                1,
                keepdims=False,
            ).reshape(row_count * panel_rows, columns)
            off_block = panel[pan_off : pan_off + E // groups]
            partial_value = jnp.einsum(
                "ik,ia->ka", diag_block, own_rows, preferred_element_type=jnp.float32
            ) - jnp.einsum("ik,ia->ka", off_block, taken_rows, preferred_element_type=jnp.float32)
        if level_no == 0:
            reduced = partial_value
        else:
            reduced = halving(
                partial_value.reshape(groups, piece_rows, columns), level_no, leaf_pos, reduce_swap
            )
        parent_value = jnp.where(live_masks[level_no], reduced, 0.0).astype(jnp.bfloat16)
        backward_parts[level_no] = parent_value
    return (jnp.concatenate(forward_parts, 0), jnp.concatenate(backward_parts, 0))


B = 128
VMEM = pl.BlockSpec(memory_space=pltpu.VMEM)
ANY = pl.BlockSpec(memory_space=pl.ANY)
BF = jnp.bfloat16
F32 = jnp.float32
MIB = 1024 * 1024


def stored(rows, columns, dtype=BF):
    return jax.ShapeDtypeStruct((rows, columns), dtype)


def kept(rows, columns, dtype=BF):
    return pltpu.VMEM((rows, columns), dtype)


def call(body, out_shape, in_specs, scratch, limit, flops, bytes_moved):
    return pl.pallas_call(
        body,
        out_shape=out_shape,
        in_specs=in_specs,
        out_specs=jax.tree.map(lambda _: VMEM, out_shape, is_leaf=lambda s: hasattr(s, "shape")),
        scratch_shapes=scratch,
        compiler_params=pltpu.CompilerParams(vmem_limit_bytes=limit),
        cost_estimate=pl.CostEstimate(flops=flops, bytes_accessed=bytes_moved, transcendentals=0),
    )


def rows_at(start, size):
    return pl.ds(pl.multiple_of(start, 16), size)


def mm(left, right):
    return jnp.dot(left, right, preferred_element_type=F32)


def row_order(row_pos, leaf_pos):
    return (row_pos, row_pos ^ (1 + leaf_pos), row_pos ^ (2 - leaf_pos), row_pos ^ 3)


def panel_kernel(
    sizes,
    live,
    pmap,
    rhs,
    panel,
    pivot,
    send,
    keep,
    b_v,
    masked,
    mask,
    w_v,
    d_v,
    c_v,
    live_s,
    pmap_s,
    sems,
):
    quarter, half, parts, update_rows = sizes
    leaf_pos = lax.axis_index("leaf")
    row_pos = lax.axis_index("row")
    gets = [
        pltpu.make_async_copy(live, live_s, sems.at[0]),
        pltpu.make_async_copy(rhs, b_v, sems.at[1]),
        pltpu.make_async_copy(pmap, pmap_s, sems.at[2]),
    ]
    step = update_rows // parts
    for i in range(parts):
        rows = pl.ds(i * step, step)
        gets.append(pltpu.make_async_copy(panel.at[rows], w_v.at[rows], sems.at[3 + i]))
    gets.append(pltpu.make_async_copy(pivot, d_v, sems.at[3 + parts]))
    for get in gets:
        get.start()
    c_v[...] = jnp.zeros_like(c_v)
    gets[0].wait()
    gets[1].wait()
    value = b_v[pl.ds(0, quarter)]
    row = row_pos * quarter + lax.broadcasted_iota(jnp.int32, value.shape, 0)
    alive = row < live_s[leaf_pos] * B
    mask[...] = jnp.where(alive, 1.0, 0.0).astype(BF)
    masked[...] = jnp.where(alive, value, jnp.zeros_like(value))
    right = masked[...]
    gets[2].wait()
    for i in range(parts):
        gets[3 + i].wait()
        product = mm(w_v[pl.ds(i * step, step)], right).astype(BF)
        for e in range(step // B):
            block = pmap_s[leaf_pos, i * (step // B) + e]
            c_v[pl.ds(pl.multiple_of(block * B, B), B)] = product[e * B : (e + 1) * B]
    for out, side in ((keep, leaf_pos), (send, 1 - leaf_pos)):
        near = (row_pos ^ (1 + side)) * quarter
        mine, other = side * half, (1 - side) * half
        out[pl.ds(0, half)] = c_v[rows_at(near + mine, half)]
        out[pl.ds(half, half)] = c_v[rows_at(near + other, half)]
        out[pl.ds(quarter, half)] = c_v[rows_at((row_pos ^ 3) * quarter + mine, half)]
        out[pl.ds(quarter + half, half)] = c_v[rows_at(row_pos * quarter + mine, half)]
    gets[3 + parts].wait()


def leaf_pivot_kernel(sizes, masked, d_v, after, *outs):
    quarter = sizes
    order = row_order(lax.axis_index("row"), lax.axis_index("leaf"))
    right = masked[...]
    for k in (3, 1, 2, 0):
        product = mm(d_v[rows_at(order[k] * quarter, quarter)], right)
        outs[k][...] = product.astype(BF)


def scatter_kernel(sizes, live, pmap, w_v, after, out, live_s, pmap_s, sems):
    quarter, update_rows = sizes
    leaf_pos = lax.axis_index("leaf")
    row_pos = lax.axis_index("row")
    gets = [
        pltpu.make_async_copy(live, live_s, sems.at[0]),
        pltpu.make_async_copy(pmap, pmap_s, sems.at[1]),
    ]
    for get in gets:
        get.start()
    per_row = quarter // B
    out[...] = jnp.zeros_like(out)
    for get in gets:
        get.wait()
    column = row_pos * quarter + lax.broadcasted_iota(jnp.int32, (B, quarter), 1)
    alive = column < live_s[leaf_pos] * B
    for e in range(update_rows // B):
        value = w_v[pl.ds(e * B, B)]
        block = pmap_s[leaf_pos, e]
        away = (block // per_row) ^ row_pos
        slot = jnp.where(away == 1 + leaf_pos, 1, jnp.where(away == 2 - leaf_pos, 2, away))
        at = (slot * per_row + block % per_row) * B
        out[pl.ds(pl.multiple_of(at, B), B)] = jnp.where(alive, value, jnp.zeros_like(value))


def root_pivot_kernel(sizes, mine, yours, other_mine, other_yours, d_v, out, q_v):
    half, base = sizes
    leaf_pos = lax.axis_index("leaf")
    for own, other, at in ((mine, other_yours, leaf_pos), (yours, other_mine, 1 - leaf_pos)):
        value = own[...].astype(F32) + other[...].astype(F32)
        q_v[rows_at(at * half, half)] = (-value).astype(BF)
    out[...] = mm(d_v[pl.ds(base, 4 * half)], q_v[...]).astype(BF)


def root_transposed_kernel(sizes, y, d_v, out, piece, s_v):
    half, base = sizes
    leaf_pos = lax.axis_index("leaf")
    row_pos = lax.axis_index("row")
    piece[...] = y[rows_at(row_pos * half, half)]
    s_v[...] = mm(y[...].T, d_v[pl.ds(base, 4 * half)]).T
    out[pl.ds(0, half)] = s_v[rows_at(leaf_pos * half, half)].astype(BF)
    out[pl.ds(half, half)] = s_v[rows_at((1 - leaf_pos) * half, half)].astype(BF)


def put(target, slot, half, source, order):
    for k, side in enumerate(order):
        at = 2 * slot * half + side * half
        target[rows_at(at, half)] = source[pl.ds(k * half, half)]


def leaf_transposed_kernel(
    sizes,
    own,
    rows_x,
    rows_y,
    rows_d,
    d_v,
    mask,
    root_rows,
    panel_rows,
    root_piece,
    total,
    forward,
    y_v,
    s_v,
):
    quarter, half = sizes
    row_pos = lax.axis_index("row")
    leaf_pos = lax.axis_index("leaf")
    order = row_order(row_pos, leaf_pos)
    forward[pl.ds(0, quarter)] = own[...]
    forward[pl.ds(quarter, half)] = root_piece[...]
    for k, part in enumerate((own, rows_x, rows_y, rows_d)):
        y_v[rows_at(order[k] * quarter, quarter)] = part[...]
    value = mm(y_v[...].T, d_v[pl.ds(0, 4 * quarter)])
    value = jnp.where(mask[...].astype(F32).T > 0.0, value, 0.0)
    put(s_v, 0, half, root_rows, (leaf_pos, 1 - leaf_pos))
    total[...] = value - mm(s_v[...].T, panel_rows[pl.ds(0, quarter)])


def last_kernel(sizes, mine, theirs, mine_far, theirs_far, total, panel_rows, root_rows, out, s_v):
    quarter, half = sizes
    leaf_pos = lax.axis_index("leaf")
    put(s_v, 1, half, mine, (leaf_pos, 1 - leaf_pos))
    put(s_v, 0, half, theirs, (1 - leaf_pos, leaf_pos))
    put(s_v, 2, half, mine_far, (leaf_pos,))
    put(s_v, 2, half, theirs_far, (1 - leaf_pos,))
    value = total[...] - mm(s_v[...].T, panel_rows[pl.ds(quarter, 3 * quarter)])
    out[pl.ds(0, quarter)] = value.T.astype(BF)
    out[pl.ds(quarter, half)] = root_rows[pl.ds(0, half)]


def leaf_swap(value):
    return lax.ppermute(value, "leaf", [(0, 1), (1, 0)])


def row_swap(value, phase):
    route = []
    for leaf in range(2):
        apart = (1 + leaf, 2 - leaf, 3)[phase]
        route += [(4 * leaf + r, 4 * leaf + (r ^ apart)) for r in range(4)]
    return lax.ppermute(value, ("leaf", "row"), route)


def added(left, right):
    return left.astype(F32) + right.astype(F32)


def two_levels(rhs, pivot_inverse, panel, live, parent_map):
    columns = rhs.shape[1]
    quarter = pivot_inverse.shape[1]
    half = quarter // 2
    front = 4 * quarter
    updates = parent_map.shape[1] * B
    after = lambda value, other: lax.optimization_barrier((value, other))[0]
    smem = [pltpu.SMEM(live.shape, jnp.int32), pltpu.SMEM(parent_map.shape, jnp.int32)]

    parts = 4 if updates % (4 * B) == 0 else 1
    sent, keep, b_v, masked, mask, w_v, d_v = call(
        functools.partial(panel_kernel, (quarter, half, parts, updates)),
        (
            kept(4 * half, columns),
            kept(4 * half, columns),
            kept(quarter + half, columns),
            kept(quarter, columns),
            kept(quarter, columns),
            kept(updates, quarter),
            kept(front + 4 * half, quarter),
        ),
        [ANY] * 5,
        [pltpu.VMEM((front, columns), BF), *smem, pltpu.SemaphoreType.DMA((4 + parts,))],
        57_100_000,
        2 * updates * quarter * columns,
        2 * updates * quarter,
    )(live, parent_map, rhs, panel, pivot_inverse)
    got = leaf_swap(sent)
    update = added(keep, got)
    away_far = update[quarter : quarter + half].astype(BF)
    away_near = update[:quarter].astype(BF)
    from_far = row_swap(away_far, 2)
    from_near = row_swap(away_near, 0)

    pieces = call(
        functools.partial(leaf_pivot_kernel, quarter),
        (kept(quarter, columns),) * 4,
        [VMEM, VMEM, ANY],
        [],
        16 * MIB,
        2 * front * quarter * columns,
        2 * front * quarter,
    )(masked, d_v, away_near)
    from_near = after(from_near, pieces[0])
    leaf_forward = pieces[0].astype(F32)
    for phase in (2, 0, 1):
        leaf_forward = leaf_forward + row_swap(pieces[1 + phase], phase).astype(F32)
    leaf_forward = jnp.where(mask > 0, leaf_forward, 0.0).astype(BF)
    rows_y = row_swap(leaf_forward, 1)
    rows_x = row_swap(leaf_forward, 0)
    rows_d = row_swap(rows_y, 0)

    term = update[quarter + half :] + from_far.astype(F32) - b_v[quarter:].astype(F32)
    from_near = from_near.astype(F32)
    negated_mine = (from_near[:half] + term).astype(BF)
    negated_yours = from_near[half:].astype(BF)
    other_yours = leaf_swap(negated_yours)
    other_mine = leaf_swap(negated_mine)

    partial = call(
        functools.partial(root_pivot_kernel, (half, front)),
        kept(4 * half, columns),
        [VMEM] * 5,
        [pltpu.VMEM((quarter, columns), BF)],
        16 * MIB,
        0,
        0,
    )(negated_mine, negated_yours, other_mine, other_yours, d_v)
    panel_rows = call(
        functools.partial(scatter_kernel, (quarter, updates)),
        kept(front, quarter),
        [ANY, ANY, VMEM, ANY],
        [*smem, pltpu.SemaphoreType.DMA((2,))],
        16 * MIB,
        2000000000,
        4 * front * quarter,
    )(live, parent_map, w_v, after(rows_y, rows_x))
    partial = added(partial, row_swap(partial, 1))
    got = after(row_swap(partial.astype(BF), 0), panel_rows)
    root_forward = (partial + got.astype(F32)).astype(BF)

    part, root_piece = call(
        functools.partial(root_transposed_kernel, (half, front)),
        (kept(quarter, columns), kept(half, columns)),
        [VMEM, VMEM],
        [pltpu.VMEM((quarter, columns), F32)],
        16 * MIB,
        0,
        0,
    )(root_forward, d_v)
    got = after(leaf_swap(part), rows_d)
    root_mine = added(part[:half], got[half:]).astype(BF)
    root_other = added(part[half:], got[:half]).astype(BF)
    root_rows = jnp.concatenate([root_mine, root_other], 0)

    near = row_swap(root_rows, 1)
    far = row_swap(root_mine, 2)
    total, forward = call(
        functools.partial(leaf_transposed_kernel, (quarter, half)),
        (kept(columns, quarter, F32), stored(quarter + half, columns)),
        [VMEM] * 9,
        [pltpu.VMEM((front, columns), BF), pltpu.VMEM((quarter, columns), BF)],
        16 * MIB,
        2 * front * quarter * columns,
        2 * front * quarter,
    )(leaf_forward, rows_x, rows_y, rows_d, d_v, mask, root_rows, panel_rows, root_piece)
    near = after(near, total)
    near_other = leaf_swap(near)
    far_other = leaf_swap(far)
    backward = call(
        functools.partial(last_kernel, (quarter, half)),
        stored(quarter + half, columns),
        [VMEM] * 7,
        [pltpu.VMEM((3 * quarter, columns), BF)],
        16 * MIB,
        front * quarter * columns,
        front * quarter,
    )(near, near_other, far, far_other, total, panel_rows, root_rows)
    return forward, backward


def on_device(rhs, pivot_inverse, panel, live, parent_map):
    if lax.axis_size("leaf") == 2 and lax.axis_size("row") == 4:
        return two_levels(rhs, pivot_inverse, panel, live, parent_map)
    return deep_tree(rhs, pivot_inverse, panel, live, parent_map)


def solution(mesh):
    in_specs = (P(("leaf", "row"), "col"), P("leaf", "row"), P("leaf", "row"), P(), P())
    out_specs = (P(("leaf", "row"), "col"), P(("leaf", "row"), "col"))
    return jax.shard_map(
        on_device, mesh=mesh, in_specs=in_specs, out_specs=out_specs, check_vma=False
    )
```

```python
import functools

import jax
import jax.numpy as jnp
from jax import lax
from jax.experimental import pallas as pl
from jax.experimental.pallas import tpu as pltpu
from jax.sharding import PartitionSpec as P

F = 2560
E = 1536


def from_partner(block, axis, apart):
    count = lax.axis_size(axis)
    route = []
    for low in range(count):
        high = low | 1 << apart
        if high != low and high < count:
            route += [(low, high), (high, low)]
    return lax.ppermute(block, axis, route)


def doubling(stacked, bit_count, leaf_pos, swapper):
    for bit_no in range(bit_count):
        partner = swapper(stacked, bit_no)
        upper_half = jnp.right_shift(leaf_pos, bit_no) % 2 == 1
        stacked = jnp.where(
            upper_half,
            jnp.concatenate([partner, stacked], 0),
            jnp.concatenate([stacked, partner], 0),
        )
    return stacked


def halving(partial_value, bit_count, leaf_pos, swapper):
    for bit_no in reversed(range(bit_count)):
        halves = partial_value.reshape((2, partial_value.shape[0] // 2) + partial_value.shape[1:])
        upper_half = jnp.right_shift(leaf_pos, bit_no) % 2 == 1
        kept_half = jnp.where(upper_half, halves[1], halves[0])
        sent_half = jnp.where(upper_half, halves[0], halves[1])
        partial_value = kept_half + swapper(sent_half, bit_no)
    return partial_value[0]


def to_front(group_block, row_count):
    count_g, total_rows, row_width = group_block.shape
    piece_rows = total_rows // row_count
    return (
        group_block.reshape(count_g, row_count, piece_rows, row_width)
        .transpose(1, 0, 2, 3)
        .reshape(count_g * total_rows, row_width)
    )


def block_onehot(mapping):
    return (jnp.arange(F // 128, dtype=jnp.int32)[:, None] == mapping[None, :]).astype(jnp.bfloat16)


def pivot_sum(diag_block, quarter_rows):
    return lax.psum_scatter(
        jnp.dot(diag_block, quarter_rows, preferred_element_type=jnp.float32).astype(jnp.bfloat16),
        "row",
        scatter_dimension=0,
        tiled=True,
    ).astype(jnp.float32)


def quarter_swap(values, bit_no):
    return from_partner(values, "leaf", bit_no)


def update_swap(values, bit_no):
    return from_partner(values, "leaf", bit_no)


def parent_swap(values, bit_no):
    return from_partner(values, "leaf", bit_no)


def reduce_swap(values, bit_no):
    return from_partner(values.astype(jnp.bfloat16), "leaf", bit_no).astype(values.dtype)


def deep_tree(rhs, pivot_inverse, panel, live, parent_map):
    leaves = lax.axis_size("leaf")
    row_count = lax.axis_size("row")
    tree_depth = leaves.bit_length() - 1
    leaf_pos = lax.axis_index("leaf")
    row_pos = lax.axis_index("row")
    columns = rhs.shape[1]
    quarter = F // row_count
    parent_blocks = F // 128
    child_blocks = E // 128
    layout = []
    vec_off, piv_off, pan_off, front_base = (0, 0, 0, 0)
    for level_no in range(tree_depth + 1):
        groups = 2**level_no
        layout.append((groups, vec_off, piv_off, pan_off, front_base))
        vec_off += F // (row_count * groups)
        piv_off += F // groups
        pan_off += E // groups
        front_base += leaves // groups
    forward_parts = []
    live_masks = []
    incoming = None
    for level_no in range(tree_depth + 1):
        groups, vec_off, piv_off, pan_off, front_base = layout[level_no]
        piece_rows = F // (row_count * groups)
        panel_rows = E // (row_count * groups)
        inner_pos = leaf_pos % groups
        front_no = jnp.right_shift(leaf_pos, level_no)
        live_rows = lax.dynamic_index_in_dim(live, front_base + front_no, 0, keepdims=False) * 128
        first_row = (row_pos * groups + inner_pos) * piece_rows
        live_mask = (first_row + jnp.arange(piece_rows, dtype=jnp.int32) < live_rows)[:, None]
        live_masks.append(live_mask)
        right_side = rhs[vec_off : vec_off + piece_rows]
        if incoming is not None:
            right_side = (right_side.astype(jnp.float32) - incoming).astype(jnp.bfloat16)
        masked = jnp.where(live_mask, right_side, jnp.zeros_like(right_side))
        quarter_rows = doubling(masked[None], level_no, leaf_pos, quarter_swap).reshape(
            quarter, columns
        )
        diag_block = pivot_inverse[piv_off : piv_off + F // groups]
        if level_no < tree_depth:
            off_block = panel[pan_off : pan_off + E // groups]
            forward_value = pivot_sum(diag_block, quarter_rows)
            update_rows = lax.psum(
                jnp.dot(off_block, quarter_rows, preferred_element_type=jnp.float32), "row"
            ).astype(jnp.bfloat16)
        else:
            forward_value = pivot_sum(diag_block, quarter_rows)
        forward_parts.append(jnp.where(live_mask, forward_value, 0.0).astype(jnp.bfloat16))
        if level_no < tree_depth:
            gathered = doubling(update_rows[None], level_no + 1, leaf_pos, update_swap)
            parent_front = jnp.right_shift(leaf_pos, level_no + 1)
            assembled = jnp.zeros((parent_blocks, 128, columns), jnp.float32)
            for side_no in range(2):
                child_update = to_front(
                    gathered[side_no * groups : (side_no + 1) * groups], row_count
                )
                mapping = lax.dynamic_index_in_dim(
                    parent_map, front_base + 2 * parent_front + side_no, 0, keepdims=False
                )
                assembled = assembled + jnp.einsum(
                    "ke,eab->kab",
                    block_onehot(mapping),
                    child_update.reshape(child_blocks, 128, columns),
                    preferred_element_type=jnp.float32,
                )
            parent_groups = 2 * groups
            parent_rows = F // (row_count * parent_groups)
            parent_first = (row_pos * parent_groups + leaf_pos % parent_groups) * parent_rows
            incoming = lax.dynamic_slice_in_dim(
                assembled.reshape(F, columns), parent_first, parent_rows, 0
            )
    backward_parts = [None] * (tree_depth + 1)
    parent_value = None
    for level_no in reversed(range(tree_depth + 1)):
        groups, vec_off, piv_off, pan_off, front_base = layout[level_no]
        piece_rows = F // (row_count * groups)
        panel_rows = E // (row_count * groups)
        inner_pos = leaf_pos % groups
        front_no = jnp.right_shift(leaf_pos, level_no)
        diag_block = pivot_inverse[piv_off : piv_off + F // groups]
        own_piece = forward_parts[level_no]
        if level_no == tree_depth:
            own_rows = lax.all_gather(own_piece, "row", axis=0, tiled=True)
            partial_value = jnp.einsum(
                "ik,ia->ka", diag_block, own_rows, preferred_element_type=jnp.float32
            )
        else:
            own_rows, parent_gathered = (
                lax.all_gather(own_piece, "row", axis=0, tiled=True),
                lax.all_gather(parent_value, "row", axis=0, tiled=True),
            )
            whole_parent = doubling(parent_gathered[None], level_no + 1, leaf_pos, parent_swap)
            parent_full = to_front(whole_parent, row_count)
            mapping = lax.dynamic_index_in_dim(parent_map, front_base + front_no, 0, keepdims=False)
            taken_rows = jnp.einsum(
                "ke,kab->eab",
                block_onehot(mapping),
                parent_full.reshape(parent_blocks, 128, columns),
                preferred_element_type=jnp.float32,
            ).astype(jnp.bfloat16)
            taken_rows = lax.dynamic_index_in_dim(
                taken_rows.reshape(row_count, groups, panel_rows, columns),
                inner_pos,
                1,
                keepdims=False,
            ).reshape(row_count * panel_rows, columns)
            off_block = panel[pan_off : pan_off + E // groups]
            partial_value = jnp.einsum(
                "ik,ia->ka", diag_block, own_rows, preferred_element_type=jnp.float32
            ) - jnp.einsum("ik,ia->ka", off_block, taken_rows, preferred_element_type=jnp.float32)
        if level_no == 0:
            reduced = partial_value
        else:
            reduced = halving(
                partial_value.reshape(groups, piece_rows, columns), level_no, leaf_pos, reduce_swap
            )
        parent_value = jnp.where(live_masks[level_no], reduced, 0.0).astype(jnp.bfloat16)
        backward_parts[level_no] = parent_value
    return (jnp.concatenate(forward_parts, 0), jnp.concatenate(backward_parts, 0))


B = 128
VMEM = pl.BlockSpec(memory_space=pltpu.VMEM)
ANY = pl.BlockSpec(memory_space=pl.ANY)
BF = jnp.bfloat16
F32 = jnp.float32
MIB = 1024 * 1024


def stored(rows, columns, dtype=BF):
    return jax.ShapeDtypeStruct((rows, columns), dtype)


def kept(rows, columns, dtype=BF):
    return pltpu.VMEM((rows, columns), dtype)


def call(body, out_shape, in_specs, scratch, limit, flops, bytes_moved):
    return pl.pallas_call(
        body,
        out_shape=out_shape,
        in_specs=in_specs,
        out_specs=jax.tree.map(lambda _: VMEM, out_shape, is_leaf=lambda s: hasattr(s, "shape")),
        scratch_shapes=scratch,
        compiler_params=pltpu.CompilerParams(vmem_limit_bytes=limit),
        cost_estimate=pl.CostEstimate(flops=flops, bytes_accessed=bytes_moved, transcendentals=0),
    )


def rows_at(start, size):
    return pl.ds(pl.multiple_of(start, 16), size)


def mm(left, right):
    return jnp.dot(left, right, preferred_element_type=F32)


def row_order(row_pos, leaf_pos):
    return (row_pos, row_pos ^ (1 + leaf_pos), row_pos ^ (2 - leaf_pos), row_pos ^ 3)


def panel_kernel(
    sizes,
    live,
    pmap,
    rhs,
    panel,
    send,
    keep,
    b_v,
    masked,
    mask,
    w_v,
    c_v,
    live_s,
    pmap_s,
    sems,
):
    quarter, half, parts, update_rows = sizes
    leaf_pos = lax.axis_index("leaf")
    row_pos = lax.axis_index("row")
    gets = [
        pltpu.make_async_copy(live, live_s, sems.at[0]),
        pltpu.make_async_copy(rhs, b_v, sems.at[1]),
        pltpu.make_async_copy(pmap, pmap_s, sems.at[2]),
    ]
    step = update_rows // parts
    for i in range(parts):
        rows = pl.ds(i * step, step)
        gets.append(pltpu.make_async_copy(panel.at[rows], w_v.at[rows], sems.at[3 + i]))
    for get in gets:
        get.start()
    c_v[...] = jnp.zeros_like(c_v)
    gets[0].wait()
    gets[1].wait()
    value = b_v[pl.ds(0, quarter)]
    row = row_pos * quarter + lax.broadcasted_iota(jnp.int32, value.shape, 0)
    alive = row < live_s[leaf_pos] * B
    mask[...] = jnp.where(alive, 1.0, 0.0).astype(BF)
    masked[...] = jnp.where(alive, value, jnp.zeros_like(value))
    right = masked[...]
    gets[2].wait()
    for i in range(parts):
        gets[3 + i].wait()
        product = mm(w_v[pl.ds(i * step, step)], right).astype(BF)
        for e in range(step // B):
            block = pmap_s[leaf_pos, i * (step // B) + e]
            c_v[pl.ds(pl.multiple_of(block * B, B), B)] = product[e * B : (e + 1) * B]
    for out, side in ((keep, leaf_pos), (send, 1 - leaf_pos)):
        near = (row_pos ^ (1 + side)) * quarter
        mine, other = side * half, (1 - side) * half
        out[pl.ds(0, half)] = c_v[rows_at(near + mine, half)]
        out[pl.ds(half, half)] = c_v[rows_at(near + other, half)]
        out[pl.ds(quarter, half)] = c_v[rows_at((row_pos ^ 3) * quarter + mine, half)]
        out[pl.ds(quarter + half, half)] = c_v[rows_at(row_pos * quarter + mine, half)]


def load_kernel(rows, pivot, after, d_v, sem):
    get = pltpu.make_async_copy(pivot.at[pl.ds(0, rows)], d_v, sem)
    get.start()
    get.wait()


def leaf_pivot_kernel(sizes, masked, d_v, pivot, after, *outs_and_scratch):
    quarter, base, rows = sizes
    *outs, root_d, sem = outs_and_scratch
    get = pltpu.make_async_copy(pivot.at[pl.ds(base, rows)], root_d, sem)
    get.start()
    order = row_order(lax.axis_index("row"), lax.axis_index("leaf"))
    right = masked[...]
    for k in (3, 1, 2, 0):
        product = mm(d_v[rows_at(order[k] * quarter, quarter)], right)
        outs[k][...] = product.astype(BF)
    get.wait()


def scatter_kernel(sizes, live, pmap, w_v, after, out, live_s, pmap_s, sems):
    quarter, update_rows = sizes
    leaf_pos = lax.axis_index("leaf")
    row_pos = lax.axis_index("row")
    gets = [
        pltpu.make_async_copy(live, live_s, sems.at[0]),
        pltpu.make_async_copy(pmap, pmap_s, sems.at[1]),
    ]
    for get in gets:
        get.start()
    per_row = quarter // B
    out[...] = jnp.zeros_like(out)
    for get in gets:
        get.wait()
    column = row_pos * quarter + lax.broadcasted_iota(jnp.int32, (B, quarter), 1)
    alive = column < live_s[leaf_pos] * B
    for e in range(update_rows // B):
        value = w_v[pl.ds(e * B, B)]
        block = pmap_s[leaf_pos, e]
        away = (block // per_row) ^ row_pos
        slot = jnp.where(away == 1 + leaf_pos, 1, jnp.where(away == 2 - leaf_pos, 2, away))
        at = (slot * per_row + block % per_row) * B
        out[pl.ds(pl.multiple_of(at, B), B)] = jnp.where(alive, value, jnp.zeros_like(value))


def root_pivot_kernel(sizes, mine, yours, other_mine, other_yours, d_v, out, q_v):
    half = sizes
    leaf_pos = lax.axis_index("leaf")
    for own, other, at in ((mine, other_yours, leaf_pos), (yours, other_mine, 1 - leaf_pos)):
        value = own[...].astype(F32) + other[...].astype(F32)
        q_v[rows_at(at * half, half)] = (-value).astype(BF)
    out[...] = mm(d_v[pl.ds(0, 4 * half)], q_v[...]).astype(BF)


def root_transposed_kernel(sizes, y, d_v, out, piece, s_v):
    half = sizes
    leaf_pos = lax.axis_index("leaf")
    row_pos = lax.axis_index("row")
    piece[...] = y[rows_at(row_pos * half, half)]
    s_v[...] = mm(y[...].T, d_v[pl.ds(0, 4 * half)]).T
    out[pl.ds(0, half)] = s_v[rows_at(leaf_pos * half, half)].astype(BF)
    out[pl.ds(half, half)] = s_v[rows_at((1 - leaf_pos) * half, half)].astype(BF)


def put(target, slot, half, source, order):
    for k, side in enumerate(order):
        at = 2 * slot * half + side * half
        target[rows_at(at, half)] = source[pl.ds(k * half, half)]


def leaf_transposed_kernel(
    sizes,
    own,
    rows_x,
    rows_y,
    rows_d,
    d_v,
    mask,
    root_rows,
    panel_rows,
    root_piece,
    total,
    forward,
    y_v,
    s_v,
):
    quarter, half = sizes
    row_pos = lax.axis_index("row")
    leaf_pos = lax.axis_index("leaf")
    order = row_order(row_pos, leaf_pos)
    forward[pl.ds(0, quarter)] = own[...]
    forward[pl.ds(quarter, half)] = root_piece[...]
    for k, part in enumerate((own, rows_x, rows_y, rows_d)):
        y_v[rows_at(order[k] * quarter, quarter)] = part[...]
    value = mm(y_v[...].T, d_v[pl.ds(0, 4 * quarter)])
    value = jnp.where(mask[...].astype(F32).T > 0.0, value, 0.0)
    put(s_v, 0, half, root_rows, (leaf_pos, 1 - leaf_pos))
    total[...] = value - mm(s_v[...].T, panel_rows[pl.ds(0, quarter)])


def last_kernel(sizes, mine, theirs, mine_far, theirs_far, total, panel_rows, root_rows, out, s_v):
    quarter, half = sizes
    leaf_pos = lax.axis_index("leaf")
    put(s_v, 1, half, mine, (leaf_pos, 1 - leaf_pos))
    put(s_v, 0, half, theirs, (1 - leaf_pos, leaf_pos))
    put(s_v, 2, half, mine_far, (leaf_pos,))
    put(s_v, 2, half, theirs_far, (1 - leaf_pos,))
    value = total[...] - mm(s_v[...].T, panel_rows[pl.ds(quarter, 3 * quarter)])
    out[pl.ds(0, quarter)] = value.T.astype(BF)
    out[pl.ds(quarter, half)] = root_rows[pl.ds(0, half)]


def leaf_swap(value):
    return lax.ppermute(value, "leaf", [(0, 1), (1, 0)])


def row_swap(value, phase):
    route = []
    for leaf in range(2):
        apart = (1 + leaf, 2 - leaf, 3)[phase]
        route += [(4 * leaf + r, 4 * leaf + (r ^ apart)) for r in range(4)]
    return lax.ppermute(value, ("leaf", "row"), route)


def added(left, right):
    return left.astype(F32) + right.astype(F32)


def two_levels(rhs, pivot_inverse, panel, live, parent_map):
    columns = rhs.shape[1]
    quarter = pivot_inverse.shape[1]
    half = quarter // 2
    front = 4 * quarter
    updates = parent_map.shape[1] * B
    after = lambda value, other: lax.optimization_barrier((value, other))[0]
    smem = [pltpu.SMEM(live.shape, jnp.int32), pltpu.SMEM(parent_map.shape, jnp.int32)]

    parts = 4 if updates % (4 * B) == 0 else 1
    sent, keep, b_v, masked, mask, w_v = call(
        functools.partial(panel_kernel, (quarter, half, parts, updates)),
        (
            kept(4 * half, columns),
            kept(4 * half, columns),
            kept(quarter + half, columns),
            kept(quarter, columns),
            kept(quarter, columns),
            kept(updates, quarter),
        ),
        [ANY] * 4,
        [pltpu.VMEM((front, columns), BF), *smem, pltpu.SemaphoreType.DMA((3 + parts,))],
        62_100_000,
        2 * updates * quarter * columns,
        2 * updates * quarter,
    )(live, parent_map, rhs, panel)
    d_v = call(
        functools.partial(load_kernel, front),
        kept(front, quarter),
        [ANY, ANY],
        [pltpu.SemaphoreType.DMA],
        51_000_000,
        0,
        2 * front * quarter,
    )(pivot_inverse, sent)
    got = after(leaf_swap(sent), d_v)
    update = added(keep, got)
    away_far = update[quarter : quarter + half].astype(BF)
    away_near = update[:quarter].astype(BF)
    from_far = row_swap(away_far, 2)
    from_near = row_swap(away_near, 0)

    *pieces, root_d = call(
        functools.partial(leaf_pivot_kernel, (quarter, front, 4 * half)),
        (*(kept(quarter, columns),) * 4, kept(4 * half, quarter)),
        [VMEM, VMEM, ANY, ANY],
        [pltpu.SemaphoreType.DMA],
        49_500_000,
        2 * front * quarter * columns,
        2 * front * quarter,
    )(masked, d_v, pivot_inverse, away_near)
    from_near = after(from_near, (pieces[0],))
    leaf_forward = pieces[0].astype(F32)
    for phase in (2, 0, 1):
        leaf_forward = leaf_forward + row_swap(pieces[1 + phase], phase).astype(F32)
    leaf_forward = jnp.where(mask > 0, leaf_forward, 0.0).astype(BF)
    rows_y = row_swap(leaf_forward, 1)
    rows_x = row_swap(leaf_forward, 0)
    rows_d = row_swap(rows_y, 0)
    panel_rows = call(
        functools.partial(scatter_kernel, (quarter, updates)),
        kept(front, quarter),
        [ANY, ANY, VMEM, ANY],
        [*smem, pltpu.SemaphoreType.DMA((2,))],
        16 * MIB,
        2000000000,
        4 * front * quarter,
    )(live, parent_map, w_v, after(rows_y, rows_x))

    term = update[quarter + half :] + from_far.astype(F32) - b_v[quarter:].astype(F32)
    from_near = from_near.astype(F32)
    negated_mine = (from_near[:half] + term).astype(BF)
    negated_yours = from_near[half:].astype(BF)
    other_yours = leaf_swap(negated_yours)
    other_mine = leaf_swap(negated_mine)
    other_mine = other_mine

    partial = call(
        functools.partial(root_pivot_kernel, half),
        kept(4 * half, columns),
        [VMEM] * 5,
        [pltpu.VMEM((quarter, columns), BF)],
        16 * MIB,
        0,
        front * quarter,
    )(negated_mine, negated_yours, other_mine, other_yours, root_d)
    got = row_swap(partial, 1)
    partial = added(partial, got)
    got = row_swap(partial.astype(BF), 0)
    root_forward = added(partial, after(got, (panel_rows,))).astype(BF)

    part, root_piece = call(
        functools.partial(root_transposed_kernel, half),
        (kept(quarter, columns), kept(half, columns)),
        [VMEM] * 2,
        [pltpu.VMEM((quarter, columns), F32)],
        16 * MIB,
        0,
        front * quarter,
    )(root_forward, root_d)
    got = after(leaf_swap(part), (rows_d,))
    root_mine = added(part[:half], got[half:]).astype(BF)
    root_other = added(part[half:], got[:half]).astype(BF)
    root_rows = jnp.concatenate([root_mine, root_other], 0)

    near = row_swap(root_rows, 1)
    far = row_swap(root_mine, 2)
    total, forward = call(
        functools.partial(leaf_transposed_kernel, (quarter, half)),
        (kept(columns, quarter, F32), stored(quarter + half, columns)),
        [VMEM] * 9,
        [pltpu.VMEM((front, columns), BF), pltpu.VMEM((quarter, columns), BF)],
        16 * MIB,
        2 * front * quarter * columns,
        2 * front * quarter,
    )(leaf_forward, rows_x, rows_y, rows_d, d_v, mask, root_rows, panel_rows, root_piece)
    near = after(near, (total, far))
    near_other = leaf_swap(near)
    far_other = leaf_swap(far)
    backward = call(
        functools.partial(last_kernel, (quarter, half)),
        stored(quarter + half, columns),
        [VMEM] * 7,
        [pltpu.VMEM((3 * quarter, columns), BF)],
        16 * MIB,
        front * quarter * columns,
        front * quarter,
    )(near, near_other, far, far_other, total, panel_rows, root_rows)
    return forward, backward


def on_device(rhs, pivot_inverse, panel, live, parent_map):
    if lax.axis_size("leaf") == 2 and lax.axis_size("row") == 4:
        return two_levels(rhs, pivot_inverse, panel, live, parent_map)
    return deep_tree(rhs, pivot_inverse, panel, live, parent_map)


def solution(mesh):
    in_specs = (P(("leaf", "row"), "col"), P("leaf", "row"), P("leaf", "row"), P(), P())
    out_specs = (P(("leaf", "row"), "col"), P(("leaf", "row"), "col"))
    return jax.shard_map(
        on_device, mesh=mesh, in_specs=in_specs, out_specs=out_specs, check_vma=False
    )
```

```python
import functools

import jax
import jax.numpy as jnp
from jax import lax
from jax.experimental import pallas as pl
from jax.experimental.pallas import tpu as pltpu
from jax.sharding import PartitionSpec as P

F = 2560
E = 1536


def from_partner(block, axis, apart):
    count = lax.axis_size(axis)
    route = []
    for low in range(count):
        high = low | 1 << apart
        if high != low and high < count:
            route += [(low, high), (high, low)]
    return lax.ppermute(block, axis, route)


def doubling(stacked, bit_count, leaf_pos, swapper):
    for bit_no in range(bit_count):
        partner = swapper(stacked, bit_no)
        upper_half = jnp.right_shift(leaf_pos, bit_no) % 2 == 1
        stacked = jnp.where(
            upper_half,
            jnp.concatenate([partner, stacked], 0),
            jnp.concatenate([stacked, partner], 0),
        )
    return stacked


def halving(partial_value, bit_count, leaf_pos, swapper):
    for bit_no in reversed(range(bit_count)):
        halves = partial_value.reshape((2, partial_value.shape[0] // 2) + partial_value.shape[1:])
        upper_half = jnp.right_shift(leaf_pos, bit_no) % 2 == 1
        kept_half = jnp.where(upper_half, halves[1], halves[0])
        sent_half = jnp.where(upper_half, halves[0], halves[1])
        partial_value = kept_half + swapper(sent_half, bit_no)
    return partial_value[0]


def to_front(group_block, row_count):
    count_g, total_rows, row_width = group_block.shape
    piece_rows = total_rows // row_count
    return (
        group_block.reshape(count_g, row_count, piece_rows, row_width)
        .transpose(1, 0, 2, 3)
        .reshape(count_g * total_rows, row_width)
    )


def block_onehot(mapping):
    return (jnp.arange(F // 128, dtype=jnp.int32)[:, None] == mapping[None, :]).astype(jnp.bfloat16)


def pivot_sum(diag_block, quarter_rows):
    return lax.psum_scatter(
        jnp.dot(diag_block, quarter_rows, preferred_element_type=jnp.float32).astype(jnp.bfloat16),
        "row",
        scatter_dimension=0,
        tiled=True,
    ).astype(jnp.float32)


def quarter_swap(values, bit_no):
    return from_partner(values, "leaf", bit_no)


def update_swap(values, bit_no):
    return from_partner(values, "leaf", bit_no)


def parent_swap(values, bit_no):
    return from_partner(values, "leaf", bit_no)


def reduce_swap(values, bit_no):
    return from_partner(values.astype(jnp.bfloat16), "leaf", bit_no).astype(values.dtype)


def deep_tree(rhs, pivot_inverse, panel, live, parent_map):
    leaves = lax.axis_size("leaf")
    row_count = lax.axis_size("row")
    tree_depth = leaves.bit_length() - 1
    leaf_pos = lax.axis_index("leaf")
    row_pos = lax.axis_index("row")
    columns = rhs.shape[1]
    quarter = F // row_count
    parent_blocks = F // 128
    child_blocks = E // 128
    layout = []
    vec_off, piv_off, pan_off, front_base = (0, 0, 0, 0)
    for level_no in range(tree_depth + 1):
        groups = 2**level_no
        layout.append((groups, vec_off, piv_off, pan_off, front_base))
        vec_off += F // (row_count * groups)
        piv_off += F // groups
        pan_off += E // groups
        front_base += leaves // groups
    forward_parts = []
    live_masks = []
    incoming = None
    for level_no in range(tree_depth + 1):
        groups, vec_off, piv_off, pan_off, front_base = layout[level_no]
        piece_rows = F // (row_count * groups)
        panel_rows = E // (row_count * groups)
        inner_pos = leaf_pos % groups
        front_no = jnp.right_shift(leaf_pos, level_no)
        live_rows = lax.dynamic_index_in_dim(live, front_base + front_no, 0, keepdims=False) * 128
        first_row = (row_pos * groups + inner_pos) * piece_rows
        live_mask = (first_row + jnp.arange(piece_rows, dtype=jnp.int32) < live_rows)[:, None]
        live_masks.append(live_mask)
        right_side = rhs[vec_off : vec_off + piece_rows]
        if incoming is not None:
            right_side = (right_side.astype(jnp.float32) - incoming).astype(jnp.bfloat16)
        masked = jnp.where(live_mask, right_side, jnp.zeros_like(right_side))
        quarter_rows = doubling(masked[None], level_no, leaf_pos, quarter_swap).reshape(
            quarter, columns
        )
        diag_block = pivot_inverse[piv_off : piv_off + F // groups]
        if level_no < tree_depth:
            off_block = panel[pan_off : pan_off + E // groups]
            forward_value = pivot_sum(diag_block, quarter_rows)
            update_rows = lax.psum(
                jnp.dot(off_block, quarter_rows, preferred_element_type=jnp.float32), "row"
            ).astype(jnp.bfloat16)
        else:
            forward_value = pivot_sum(diag_block, quarter_rows)
        forward_parts.append(jnp.where(live_mask, forward_value, 0.0).astype(jnp.bfloat16))
        if level_no < tree_depth:
            gathered = doubling(update_rows[None], level_no + 1, leaf_pos, update_swap)
            parent_front = jnp.right_shift(leaf_pos, level_no + 1)
            assembled = jnp.zeros((parent_blocks, 128, columns), jnp.float32)
            for side_no in range(2):
                child_update = to_front(
                    gathered[side_no * groups : (side_no + 1) * groups], row_count
                )
                mapping = lax.dynamic_index_in_dim(
                    parent_map, front_base + 2 * parent_front + side_no, 0, keepdims=False
                )
                assembled = assembled + jnp.einsum(
                    "ke,eab->kab",
                    block_onehot(mapping),
                    child_update.reshape(child_blocks, 128, columns),
                    preferred_element_type=jnp.float32,
                )
            parent_groups = 2 * groups
            parent_rows = F // (row_count * parent_groups)
            parent_first = (row_pos * parent_groups + leaf_pos % parent_groups) * parent_rows
            incoming = lax.dynamic_slice_in_dim(
                assembled.reshape(F, columns), parent_first, parent_rows, 0
            )
    backward_parts = [None] * (tree_depth + 1)
    parent_value = None
    for level_no in reversed(range(tree_depth + 1)):
        groups, vec_off, piv_off, pan_off, front_base = layout[level_no]
        piece_rows = F // (row_count * groups)
        panel_rows = E // (row_count * groups)
        inner_pos = leaf_pos % groups
        front_no = jnp.right_shift(leaf_pos, level_no)
        diag_block = pivot_inverse[piv_off : piv_off + F // groups]
        own_piece = forward_parts[level_no]
        if level_no == tree_depth:
            own_rows = lax.all_gather(own_piece, "row", axis=0, tiled=True)
            partial_value = jnp.einsum(
                "ik,ia->ka", diag_block, own_rows, preferred_element_type=jnp.float32
            )
        else:
            own_rows, parent_gathered = (
                lax.all_gather(own_piece, "row", axis=0, tiled=True),
                lax.all_gather(parent_value, "row", axis=0, tiled=True),
            )
            whole_parent = doubling(parent_gathered[None], level_no + 1, leaf_pos, parent_swap)
            parent_full = to_front(whole_parent, row_count)
            mapping = lax.dynamic_index_in_dim(parent_map, front_base + front_no, 0, keepdims=False)
            taken_rows = jnp.einsum(
                "ke,kab->eab",
                block_onehot(mapping),
                parent_full.reshape(parent_blocks, 128, columns),
                preferred_element_type=jnp.float32,
            ).astype(jnp.bfloat16)
            taken_rows = lax.dynamic_index_in_dim(
                taken_rows.reshape(row_count, groups, panel_rows, columns),
                inner_pos,
                1,
                keepdims=False,
            ).reshape(row_count * panel_rows, columns)
            off_block = panel[pan_off : pan_off + E // groups]
            partial_value = jnp.einsum(
                "ik,ia->ka", diag_block, own_rows, preferred_element_type=jnp.float32
            ) - jnp.einsum("ik,ia->ka", off_block, taken_rows, preferred_element_type=jnp.float32)
        if level_no == 0:
            reduced = partial_value
        else:
            reduced = halving(
                partial_value.reshape(groups, piece_rows, columns), level_no, leaf_pos, reduce_swap
            )
        parent_value = jnp.where(live_masks[level_no], reduced, 0.0).astype(jnp.bfloat16)
        backward_parts[level_no] = parent_value
    return (jnp.concatenate(forward_parts, 0), jnp.concatenate(backward_parts, 0))


B = 128
VMEM = pl.BlockSpec(memory_space=pltpu.VMEM)
ANY = pl.BlockSpec(memory_space=pl.ANY)
BF = jnp.bfloat16
F32 = jnp.float32
MIB = 1024 * 1024


def stored(rows, columns, dtype=BF):
    return jax.ShapeDtypeStruct((rows, columns), dtype)


def kept(rows, columns, dtype=BF):
    return pltpu.VMEM((rows, columns), dtype)


def call(body, out_shape, in_specs, scratch, limit, flops, bytes_moved):
    return pl.pallas_call(
        body,
        out_shape=out_shape,
        in_specs=in_specs,
        out_specs=jax.tree.map(lambda _: VMEM, out_shape, is_leaf=lambda s: hasattr(s, "shape")),
        scratch_shapes=scratch,
        compiler_params=pltpu.CompilerParams(vmem_limit_bytes=limit),
        cost_estimate=pl.CostEstimate(flops=flops, bytes_accessed=bytes_moved, transcendentals=0),
    )


def rows_at(start, size):
    return pl.ds(pl.multiple_of(start, 16), size)


def mm(left, right):
    return jnp.dot(left, right, preferred_element_type=F32)


def row_order(row_pos, leaf_pos):
    return (row_pos, row_pos ^ (1 + leaf_pos), row_pos ^ (2 - leaf_pos), row_pos ^ 3)


def panel_kernel(
    sizes,
    live,
    pmap,
    rhs,
    panel,
    pivot,
    send_near,
    send_rest,
    keep_near,
    keep_rest,
    b_v,
    masked,
    mask,
    w_v,
    d_v,
    c_v,
    live_s,
    pmap_s,
    sems,
):
    quarter, half, parts, update_rows = sizes
    leaf_pos = lax.axis_index("leaf")
    row_pos = lax.axis_index("row")
    gets = [
        pltpu.make_async_copy(live, live_s, sems.at[0]),
        pltpu.make_async_copy(rhs, b_v, sems.at[1]),
        pltpu.make_async_copy(pmap, pmap_s, sems.at[2]),
    ]
    step = update_rows // parts
    for i in range(parts):
        rows = pl.ds(i * step, step)
        gets.append(pltpu.make_async_copy(panel.at[rows], w_v.at[rows], sems.at[3 + i]))
    get = pltpu.make_async_copy(pivot.at[pl.ds(0, 4 * quarter)], d_v, sems.at[3 + parts])
    gets.append(get)
    for get in gets:
        get.start()
    c_v[...] = jnp.zeros_like(c_v)
    gets[0].wait()
    gets[1].wait()
    value = b_v[pl.ds(0, quarter)]
    row = row_pos * quarter + lax.broadcasted_iota(jnp.int32, value.shape, 0)
    alive = row < live_s[leaf_pos] * B
    mask[...] = jnp.where(alive, 1.0, 0.0).astype(BF)
    masked[...] = jnp.where(alive, value, jnp.zeros_like(value))
    right = masked[...]
    gets[2].wait()
    for i in range(parts):
        gets[3 + i].wait()
        product = mm(w_v[pl.ds(i * step, step)], right).astype(BF)
        for e in range(step // B):
            block = pmap_s[leaf_pos, i * (step // B) + e]
            c_v[pl.ds(pl.multiple_of(block * B, B), B)] = product[e * B : (e + 1) * B]
    for near_out, rest, side in (
        (send_near, send_rest, 1 - leaf_pos),
        (keep_near, keep_rest, leaf_pos),
    ):
        near = (row_pos ^ (1 + side)) * quarter
        mine, other = side * half, (1 - side) * half
        near_out[pl.ds(0, half)] = c_v[rows_at(near + mine, half)]
        near_out[pl.ds(half, half)] = c_v[rows_at(near + other, half)]
        rest[pl.ds(0, half)] = c_v[rows_at((row_pos ^ 3) * quarter + mine, half)]
        rest[pl.ds(half, half)] = c_v[rows_at(row_pos * quarter + mine, half)]
    gets[3 + parts].wait()


def leaf_pivot_kernel(sizes, masked, d_v, pivot, after, *outs_and_scratch):
    quarter, rows = sizes
    *outs, root_d, sem = outs_and_scratch
    get = pltpu.make_async_copy(pivot.at[pl.ds(4 * quarter, rows)], root_d, sem)
    get.start()
    order = row_order(lax.axis_index("row"), lax.axis_index("leaf"))
    right = masked[...]
    for k in (3, 1, 2, 0):
        product = mm(d_v[rows_at(order[k] * quarter, quarter)], right)
        outs[k][...] = product.astype(BF)
    get.wait()


def scatter_kernel(sizes, live, pmap, w_v, after, out, live_s, pmap_s, sems):
    quarter, update_rows = sizes
    leaf_pos = lax.axis_index("leaf")
    row_pos = lax.axis_index("row")
    gets = [
        pltpu.make_async_copy(live, live_s, sems.at[0]),
        pltpu.make_async_copy(pmap, pmap_s, sems.at[1]),
    ]
    for get in gets:
        get.start()
    per_row = quarter // B
    out[...] = jnp.zeros_like(out)
    for get in gets:
        get.wait()
    column = row_pos * quarter + lax.broadcasted_iota(jnp.int32, (B, quarter), 1)
    alive = column < live_s[leaf_pos] * B
    for e in range(update_rows // B):
        value = w_v[pl.ds(e * B, B)]
        block = pmap_s[leaf_pos, e]
        away = (block // per_row) ^ row_pos
        slot = jnp.where(away == 1 + leaf_pos, 1, jnp.where(away == 2 - leaf_pos, 2, away))
        at = (slot * per_row + block % per_row) * B
        out[pl.ds(pl.multiple_of(at, B), B)] = jnp.where(alive, value, jnp.zeros_like(value))


def root_pivot_kernel(sizes, mine, yours, other_mine, other_yours, d_v, out, q_v):
    half = sizes
    leaf_pos = lax.axis_index("leaf")
    for own, other, at in ((mine, other_yours, leaf_pos), (yours, other_mine, 1 - leaf_pos)):
        value = own[...].astype(F32) + other[...].astype(F32)
        q_v[rows_at(at * half, half)] = (-value).astype(BF)
    out[...] = mm(d_v[pl.ds(0, 4 * half)], q_v[...]).astype(BF)


def root_transposed_kernel(sizes, y, d_v, out, piece, s_v):
    half = sizes
    leaf_pos = lax.axis_index("leaf")
    row_pos = lax.axis_index("row")
    piece[...] = y[rows_at(row_pos * half, half)]
    s_v[...] = mm(y[...].T, d_v[pl.ds(0, 4 * half)]).T
    out[pl.ds(0, half)] = s_v[rows_at(leaf_pos * half, half)].astype(BF)
    out[pl.ds(half, half)] = s_v[rows_at((1 - leaf_pos) * half, half)].astype(BF)


def put(target, slot, half, source, order):
    for k, side in enumerate(order):
        at = 2 * slot * half + side * half
        target[rows_at(at, half)] = source[pl.ds(k * half, half)]


def leaf_transposed_kernel(
    sizes,
    own,
    rows_x,
    rows_y,
    rows_d,
    d_v,
    mask,
    root_rows,
    panel_rows,
    root_piece,
    total,
    forward,
    y_v,
    s_v,
):
    quarter, half = sizes
    row_pos = lax.axis_index("row")
    leaf_pos = lax.axis_index("leaf")
    order = row_order(row_pos, leaf_pos)
    forward[pl.ds(0, quarter)] = own[...]
    forward[pl.ds(quarter, half)] = root_piece[...]
    for k, part in enumerate((own, rows_x, rows_y, rows_d)):
        y_v[rows_at(order[k] * quarter, quarter)] = part[...]
    value = mm(y_v[...].T, d_v[pl.ds(0, 4 * quarter)])
    value = jnp.where(mask[...].astype(F32).T > 0.0, value, 0.0)
    put(s_v, 0, half, root_rows, (leaf_pos, 1 - leaf_pos))
    total[...] = value - mm(s_v[...].T, panel_rows[pl.ds(0, quarter)])


def own_kernel(sizes, near, far, total, panel_rows, out, s_v):
    quarter, half = sizes
    leaf_pos = lax.axis_index("leaf")
    put(s_v, 0, half, near, (leaf_pos, 1 - leaf_pos))
    value = total[...] - mm(s_v[...].T, panel_rows[pl.ds(2 * quarter, quarter)])
    rows = rows_at(3 * quarter + leaf_pos * half, half)
    out[...] = value - mm(far[...].T, panel_rows[rows])


def last_kernel(sizes, near, far, total, panel_rows, root_rows, out, s_v):
    quarter, half = sizes
    leaf_pos = lax.axis_index("leaf")
    put(s_v, 0, half, near, (1 - leaf_pos, leaf_pos))
    value = total[...] - mm(s_v[...].T, panel_rows[pl.ds(quarter, quarter)])
    rows = rows_at(3 * quarter + (1 - leaf_pos) * half, half)
    value = value - mm(far[...].T, panel_rows[rows])
    out[pl.ds(0, quarter)] = value.T.astype(BF)
    out[pl.ds(quarter, half)] = root_rows[pl.ds(0, half)]


def leaf_swap(value):
    return lax.ppermute(value, "leaf", [(0, 1), (1, 0)])


def row_swap(value, phase):
    route = []
    for leaf in range(2):
        apart = (1 + leaf, 2 - leaf, 3)[phase]
        route += [(4 * leaf + r, 4 * leaf + (r ^ apart)) for r in range(4)]
    return lax.ppermute(value, ("leaf", "row"), route)


def added(left, right):
    return left.astype(F32) + right.astype(F32)


def two_levels(rhs, pivot_inverse, panel, live, parent_map):
    columns = rhs.shape[1]
    quarter = pivot_inverse.shape[1]
    half = quarter // 2
    front = 4 * quarter
    updates = parent_map.shape[1] * B
    after = lambda value, other: lax.optimization_barrier((value, other))[0]
    smem = [pltpu.SMEM(live.shape, jnp.int32), pltpu.SMEM(parent_map.shape, jnp.int32)]

    parts = 4 if updates % (4 * B) == 0 else 1
    send_near, send_rest, keep_near, keep_rest, b_v, masked, mask, w_v, d_v = call(
        functools.partial(panel_kernel, (quarter, half, parts, updates)),
        (
            kept(quarter, columns),
            kept(quarter, columns),
            kept(quarter, columns),
            kept(quarter, columns),
            kept(quarter + half, columns),
            kept(quarter, columns),
            kept(quarter, columns),
            kept(updates, quarter),
            kept(front, quarter),
        ),
        [ANY] * 5,
        [pltpu.VMEM((front, columns), BF), *smem, pltpu.SemaphoreType.DMA((4 + parts,))],
        58_700_000,
        2 * updates * quarter * columns,
        2 * updates * quarter,
    )(live, parent_map, rhs, panel, pivot_inverse)
    away_near = added(keep_near, leaf_swap(send_near)).astype(BF)
    rest = added(keep_rest, leaf_swap(send_rest))
    away_far = rest[:half].astype(BF)
    from_far = row_swap(away_far, 2)
    from_near = row_swap(away_near, 0)

    *pieces, root_d = call(
        functools.partial(leaf_pivot_kernel, (quarter, 4 * half)),
        (*(kept(quarter, columns),) * 4, kept(4 * half, quarter)),
        [VMEM, VMEM, ANY, ANY],
        [pltpu.SemaphoreType.DMA],
        49_500_000,
        2 * front * quarter * columns,
        2 * front * quarter,
    )(masked, d_v, pivot_inverse, away_near)
    from_near = after(from_near, pieces[0])
    leaf_forward = pieces[0].astype(F32)
    for phase in (2, 0, 1):
        leaf_forward = leaf_forward + row_swap(pieces[1 + phase], phase).astype(F32)
    leaf_forward = jnp.where(mask > 0, leaf_forward, 0.0).astype(BF)
    rows_y = row_swap(leaf_forward, 1)
    rows_x = row_swap(leaf_forward, 0)
    rows_d = row_swap(rows_y, 0)

    term = rest[half:] + from_far.astype(F32) - b_v[quarter:].astype(F32)
    from_near = from_near.astype(F32)
    negated_mine = (from_near[:half] + term).astype(BF)
    negated_yours = from_near[half:].astype(BF)
    other_yours = leaf_swap(negated_yours)
    other_mine = leaf_swap(negated_mine)

    partial = call(
        functools.partial(root_pivot_kernel, half),
        kept(4 * half, columns),
        [VMEM] * 5,
        [pltpu.VMEM((quarter, columns), BF)],
        16 * MIB,
        0,
        0,
    )(negated_mine, negated_yours, other_mine, other_yours, root_d)
    panel_rows = call(
        functools.partial(scatter_kernel, (quarter, updates)),
        kept(front, quarter),
        [ANY, ANY, VMEM, ANY],
        [*smem, pltpu.SemaphoreType.DMA((2,))],
        16 * MIB,
        2000000000,
        4 * front * quarter,
    )(live, parent_map, w_v, after(rows_y, rows_x))
    partial = added(partial, row_swap(partial, 1))
    got = after(row_swap(partial.astype(BF), 0), panel_rows)
    root_forward = (partial + got.astype(F32)).astype(BF)

    part, root_piece = call(
        functools.partial(root_transposed_kernel, half),
        (kept(quarter, columns), kept(half, columns)),
        [VMEM, VMEM],
        [pltpu.VMEM((quarter, columns), F32)],
        16 * MIB,
        0,
        0,
    )(root_forward, root_d)
    got = after(leaf_swap(part), rows_d)
    root_mine = added(part[:half], got[half:]).astype(BF)
    root_other = added(part[half:], got[:half]).astype(BF)
    root_rows = jnp.concatenate([root_mine, root_other], 0)

    near = row_swap(root_rows, 1)
    far = row_swap(root_mine, 2)
    total, forward = call(
        functools.partial(leaf_transposed_kernel, (quarter, half)),
        (kept(columns, quarter, F32), stored(quarter + half, columns)),
        [VMEM] * 9,
        [pltpu.VMEM((front, columns), BF), pltpu.VMEM((quarter, columns), BF)],
        16 * MIB,
        2 * front * quarter * columns,
        2 * front * quarter,
    )(leaf_forward, rows_x, rows_y, rows_d, d_v, mask, root_rows, panel_rows, root_piece)
    near = after(near, total)
    near_other = leaf_swap(near)
    far_other = leaf_swap(far)
    total = call(
        functools.partial(own_kernel, (quarter, half)),
        kept(columns, quarter, F32),
        [VMEM] * 4,
        [pltpu.VMEM((quarter, columns), BF)],
        16 * MIB,
        0,
        0,
    )(near, far, total, panel_rows)
    backward = call(
        functools.partial(last_kernel, (quarter, half)),
        stored(quarter + half, columns),
        [VMEM] * 5,
        [pltpu.VMEM((quarter, columns), BF)],
        16 * MIB,
        front * quarter * columns,
        front * quarter,
    )(near_other, far_other, total, panel_rows, root_rows)
    return forward, backward


def on_device(rhs, pivot_inverse, panel, live, parent_map):
    if lax.axis_size("leaf") == 2 and lax.axis_size("row") == 4:
        return two_levels(rhs, pivot_inverse, panel, live, parent_map)
    return deep_tree(rhs, pivot_inverse, panel, live, parent_map)


def solution(mesh):
    in_specs = (P(("leaf", "row"), "col"), P("leaf", "row"), P("leaf", "row"), P(), P())
    out_specs = (P(("leaf", "row"), "col"), P(("leaf", "row"), "col"))
    return jax.shard_map(
        on_device, mesh=mesh, in_specs=in_specs, out_specs=out_specs, check_vma=False
    )
```

```python
import functools

import jax
import jax.numpy as jnp
from jax import lax
from jax.experimental import pallas as pl
from jax.experimental.pallas import tpu as pltpu
from jax.sharding import PartitionSpec as P

F = 2560
E = 1536


def from_partner(block, axis, apart):
    count = lax.axis_size(axis)
    route = []
    for low in range(count):
        high = low | 1 << apart
        if high != low and high < count:
            route += [(low, high), (high, low)]
    return lax.ppermute(block, axis, route)


def doubling(stacked, bit_count, leaf_pos, swapper):
    for bit_no in range(bit_count):
        partner = swapper(stacked, bit_no)
        upper_half = jnp.right_shift(leaf_pos, bit_no) % 2 == 1
        stacked = jnp.where(
            upper_half,
            jnp.concatenate([partner, stacked], 0),
            jnp.concatenate([stacked, partner], 0),
        )
    return stacked


def halving(partial_value, bit_count, leaf_pos, swapper):
    for bit_no in reversed(range(bit_count)):
        halves = partial_value.reshape((2, partial_value.shape[0] // 2) + partial_value.shape[1:])
        upper_half = jnp.right_shift(leaf_pos, bit_no) % 2 == 1
        kept_half = jnp.where(upper_half, halves[1], halves[0])
        sent_half = jnp.where(upper_half, halves[0], halves[1])
        partial_value = kept_half + swapper(sent_half, bit_no)
    return partial_value[0]


def to_front(group_block, row_count):
    count_g, total_rows, row_width = group_block.shape
    piece_rows = total_rows // row_count
    return (
        group_block.reshape(count_g, row_count, piece_rows, row_width)
        .transpose(1, 0, 2, 3)
        .reshape(count_g * total_rows, row_width)
    )


def block_onehot(mapping):
    return (jnp.arange(F // 128, dtype=jnp.int32)[:, None] == mapping[None, :]).astype(jnp.bfloat16)


def pivot_sum(diag_block, quarter_rows):
    return lax.psum_scatter(
        jnp.dot(diag_block, quarter_rows, preferred_element_type=jnp.float32).astype(jnp.bfloat16),
        "row",
        scatter_dimension=0,
        tiled=True,
    ).astype(jnp.float32)


def quarter_swap(values, bit_no):
    return from_partner(values, "leaf", bit_no)


def update_swap(values, bit_no):
    return from_partner(values, "leaf", bit_no)


def parent_swap(values, bit_no):
    return from_partner(values, "leaf", bit_no)


def reduce_swap(values, bit_no):
    return from_partner(values.astype(jnp.bfloat16), "leaf", bit_no).astype(values.dtype)


def deep_tree(rhs, pivot_inverse, panel, live, parent_map):
    leaves = lax.axis_size("leaf")
    row_count = lax.axis_size("row")
    tree_depth = leaves.bit_length() - 1
    leaf_pos = lax.axis_index("leaf")
    row_pos = lax.axis_index("row")
    columns = rhs.shape[1]
    quarter = F // row_count
    parent_blocks = F // 128
    child_blocks = E // 128
    layout = []
    vec_off, piv_off, pan_off, front_base = (0, 0, 0, 0)
    for level_no in range(tree_depth + 1):
        groups = 2**level_no
        layout.append((groups, vec_off, piv_off, pan_off, front_base))
        vec_off += F // (row_count * groups)
        piv_off += F // groups
        pan_off += E // groups
        front_base += leaves // groups
    forward_parts = []
    live_masks = []
    incoming = None
    for level_no in range(tree_depth + 1):
        groups, vec_off, piv_off, pan_off, front_base = layout[level_no]
        piece_rows = F // (row_count * groups)
        panel_rows = E // (row_count * groups)
        inner_pos = leaf_pos % groups
        front_no = jnp.right_shift(leaf_pos, level_no)
        live_rows = lax.dynamic_index_in_dim(live, front_base + front_no, 0, keepdims=False) * 128
        first_row = (row_pos * groups + inner_pos) * piece_rows
        live_mask = (first_row + jnp.arange(piece_rows, dtype=jnp.int32) < live_rows)[:, None]
        live_masks.append(live_mask)
        right_side = rhs[vec_off : vec_off + piece_rows]
        if incoming is not None:
            right_side = (right_side.astype(jnp.float32) - incoming).astype(jnp.bfloat16)
        masked = jnp.where(live_mask, right_side, jnp.zeros_like(right_side))
        quarter_rows = doubling(masked[None], level_no, leaf_pos, quarter_swap).reshape(
            quarter, columns
        )
        diag_block = pivot_inverse[piv_off : piv_off + F // groups]
        if level_no < tree_depth:
            off_block = panel[pan_off : pan_off + E // groups]
            forward_value = pivot_sum(diag_block, quarter_rows)
            update_rows = lax.psum(
                jnp.dot(off_block, quarter_rows, preferred_element_type=jnp.float32), "row"
            ).astype(jnp.bfloat16)
        else:
            forward_value = pivot_sum(diag_block, quarter_rows)
        forward_parts.append(jnp.where(live_mask, forward_value, 0.0).astype(jnp.bfloat16))
        if level_no < tree_depth:
            gathered = doubling(update_rows[None], level_no + 1, leaf_pos, update_swap)
            parent_front = jnp.right_shift(leaf_pos, level_no + 1)
            assembled = jnp.zeros((parent_blocks, 128, columns), jnp.float32)
            for side_no in range(2):
                child_update = to_front(
                    gathered[side_no * groups : (side_no + 1) * groups], row_count
                )
                mapping = lax.dynamic_index_in_dim(
                    parent_map, front_base + 2 * parent_front + side_no, 0, keepdims=False
                )
                assembled = assembled + jnp.einsum(
                    "ke,eab->kab",
                    block_onehot(mapping),
                    child_update.reshape(child_blocks, 128, columns),
                    preferred_element_type=jnp.float32,
                )
            parent_groups = 2 * groups
            parent_rows = F // (row_count * parent_groups)
            parent_first = (row_pos * parent_groups + leaf_pos % parent_groups) * parent_rows
            incoming = lax.dynamic_slice_in_dim(
                assembled.reshape(F, columns), parent_first, parent_rows, 0
            )
    backward_parts = [None] * (tree_depth + 1)
    parent_value = None
    for level_no in reversed(range(tree_depth + 1)):
        groups, vec_off, piv_off, pan_off, front_base = layout[level_no]
        piece_rows = F // (row_count * groups)
        panel_rows = E // (row_count * groups)
        inner_pos = leaf_pos % groups
        front_no = jnp.right_shift(leaf_pos, level_no)
        diag_block = pivot_inverse[piv_off : piv_off + F // groups]
        own_piece = forward_parts[level_no]
        if level_no == tree_depth:
            own_rows = lax.all_gather(own_piece, "row", axis=0, tiled=True)
            partial_value = jnp.einsum(
                "ik,ia->ka", diag_block, own_rows, preferred_element_type=jnp.float32
            )
        else:
            own_rows, parent_gathered = (
                lax.all_gather(own_piece, "row", axis=0, tiled=True),
                lax.all_gather(parent_value, "row", axis=0, tiled=True),
            )
            whole_parent = doubling(parent_gathered[None], level_no + 1, leaf_pos, parent_swap)
            parent_full = to_front(whole_parent, row_count)
            mapping = lax.dynamic_index_in_dim(parent_map, front_base + front_no, 0, keepdims=False)
            taken_rows = jnp.einsum(
                "ke,kab->eab",
                block_onehot(mapping),
                parent_full.reshape(parent_blocks, 128, columns),
                preferred_element_type=jnp.float32,
            ).astype(jnp.bfloat16)
            taken_rows = lax.dynamic_index_in_dim(
                taken_rows.reshape(row_count, groups, panel_rows, columns),
                inner_pos,
                1,
                keepdims=False,
            ).reshape(row_count * panel_rows, columns)
            off_block = panel[pan_off : pan_off + E // groups]
            partial_value = jnp.einsum(
                "ik,ia->ka", diag_block, own_rows, preferred_element_type=jnp.float32
            ) - jnp.einsum("ik,ia->ka", off_block, taken_rows, preferred_element_type=jnp.float32)
        if level_no == 0:
            reduced = partial_value
        else:
            reduced = halving(
                partial_value.reshape(groups, piece_rows, columns), level_no, leaf_pos, reduce_swap
            )
        parent_value = jnp.where(live_masks[level_no], reduced, 0.0).astype(jnp.bfloat16)
        backward_parts[level_no] = parent_value
    return (jnp.concatenate(forward_parts, 0), jnp.concatenate(backward_parts, 0))


B = 128
VMEM = pl.BlockSpec(memory_space=pltpu.VMEM)
ANY = pl.BlockSpec(memory_space=pl.ANY)
BF = jnp.bfloat16
F32 = jnp.float32
MIB = 1024 * 1024


def stored(rows, columns, dtype=BF):
    return jax.ShapeDtypeStruct((rows, columns), dtype)


def kept(rows, columns, dtype=BF):
    return pltpu.VMEM((rows, columns), dtype)


def call(body, out_shape, in_specs, scratch, limit, flops, bytes_moved):
    return pl.pallas_call(
        body,
        out_shape=out_shape,
        in_specs=in_specs,
        out_specs=jax.tree.map(lambda _: VMEM, out_shape, is_leaf=lambda s: hasattr(s, "shape")),
        scratch_shapes=scratch,
        compiler_params=pltpu.CompilerParams(vmem_limit_bytes=limit),
        cost_estimate=pl.CostEstimate(flops=flops, bytes_accessed=bytes_moved, transcendentals=0),
    )


def rows_at(start, size):
    return pl.ds(pl.multiple_of(start, 16), size)


def mm(left, right):
    return jnp.dot(left, right, preferred_element_type=F32)


def copies(source, first_row, target, rows, parts, sems, first_sem):
    step = rows // parts
    return [
        pltpu.make_async_copy(
            source.at[pl.ds(first_row + i * step, step)],
            target.at[pl.ds(i * step, step)],
            sems.at[first_sem + i],
        )
        for i in range(parts)
    ]


def row_order(row_pos, leaf_pos):
    return (row_pos, row_pos ^ (1 + leaf_pos), row_pos ^ (2 - leaf_pos), row_pos ^ 3)


def panel_kernel(
    sizes,
    live,
    pmap,
    rhs,
    panel,
    pivot,
    send_near,
    send_rest,
    keep_near,
    keep_rest,
    b_v,
    masked,
    mask,
    w_v,
    d_v,
    c_v,
    live_s,
    pmap_s,
    sems,
):
    quarter, half, parts, update_rows = sizes
    leaf_pos = lax.axis_index("leaf")
    row_pos = lax.axis_index("row")
    gets = [
        pltpu.make_async_copy(live, live_s, sems.at[0]),
        pltpu.make_async_copy(rhs, b_v, sems.at[1]),
        pltpu.make_async_copy(pmap, pmap_s, sems.at[2]),
    ]
    step = update_rows // parts
    for i in range(parts):
        rows = pl.ds(i * step, step)
        gets.append(pltpu.make_async_copy(panel.at[rows], w_v.at[rows], sems.at[3 + i]))
    gets += copies(pivot, 0, d_v, 4 * quarter, 8, sems, 3 + parts)
    for get in gets:
        get.start()
    c_v[...] = jnp.zeros_like(c_v)
    gets[0].wait()
    gets[1].wait()
    value = b_v[pl.ds(0, quarter)]
    row = row_pos * quarter + lax.broadcasted_iota(jnp.int32, value.shape, 0)
    alive = row < live_s[leaf_pos] * B
    mask[...] = jnp.where(alive, 1.0, 0.0).astype(BF)
    masked[...] = jnp.where(alive, value, jnp.zeros_like(value))
    right = masked[...]
    gets[2].wait()
    for i in range(parts):
        gets[3 + i].wait()
        product = mm(w_v[pl.ds(i * step, step)], right).astype(BF)
        for e in range(step // B):
            block = pmap_s[leaf_pos, i * (step // B) + e]
            c_v[pl.ds(pl.multiple_of(block * B, B), B)] = product[e * B : (e + 1) * B]
    for near_out, rest, side in (
        (send_near, send_rest, 1 - leaf_pos),
        (keep_near, keep_rest, leaf_pos),
    ):
        near = (row_pos ^ (1 + side)) * quarter
        mine, other = side * half, (1 - side) * half
        near_out[pl.ds(0, half)] = c_v[rows_at(near + mine, half)]
        near_out[pl.ds(half, half)] = c_v[rows_at(near + other, half)]
        rest[pl.ds(0, half)] = c_v[rows_at((row_pos ^ 3) * quarter + mine, half)]
        rest[pl.ds(half, half)] = c_v[rows_at(row_pos * quarter + mine, half)]
    for get in gets[3 + parts :]:
        get.wait()


def leaf_pivot_kernel(sizes, masked, d_v, pivot, after, *outs_and_scratch):
    quarter, rows = sizes
    *outs, root_d, sems = outs_and_scratch
    gets = copies(pivot, 4 * quarter, root_d, rows, 4, sems, 0)
    for get in gets:
        get.start()
    order = row_order(lax.axis_index("row"), lax.axis_index("leaf"))
    right = masked[...]
    for k in (3, 1, 2, 0):
        product = mm(d_v[rows_at(order[k] * quarter, quarter)], right)
        outs[k][...] = product.astype(BF)
    for get in gets:
        get.wait()


def scatter_kernel(sizes, live, pmap, w_v, after, out, live_s, pmap_s, sems):
    quarter, update_rows = sizes
    leaf_pos = lax.axis_index("leaf")
    row_pos = lax.axis_index("row")
    gets = [
        pltpu.make_async_copy(live, live_s, sems.at[0]),
        pltpu.make_async_copy(pmap, pmap_s, sems.at[1]),
    ]
    for get in gets:
        get.start()
    per_row = quarter // B
    out[...] = jnp.zeros_like(out)
    for get in gets:
        get.wait()
    column = row_pos * quarter + lax.broadcasted_iota(jnp.int32, (B, quarter), 1)
    alive = column < live_s[leaf_pos] * B
    for e in range(update_rows // B):
        value = w_v[pl.ds(e * B, B)]
        block = pmap_s[leaf_pos, e]
        away = (block // per_row) ^ row_pos
        slot = jnp.where(away == 1 + leaf_pos, 1, jnp.where(away == 2 - leaf_pos, 2, away))
        at = (slot * per_row + block % per_row) * B
        out[pl.ds(pl.multiple_of(at, B), B)] = jnp.where(alive, value, jnp.zeros_like(value))


def root_pivot_kernel(sizes, mine, yours, other_mine, other_yours, d_v, out, q_v):
    half = sizes
    leaf_pos = lax.axis_index("leaf")
    for own, other, at in ((mine, other_yours, leaf_pos), (yours, other_mine, 1 - leaf_pos)):
        value = own[...].astype(F32) + other[...].astype(F32)
        q_v[rows_at(at * half, half)] = (-value).astype(BF)
    out[...] = mm(d_v[pl.ds(0, 4 * half)], q_v[...]).astype(BF)


def root_transposed_kernel(sizes, y, d_v, out, piece, s_v):
    half = sizes
    leaf_pos = lax.axis_index("leaf")
    row_pos = lax.axis_index("row")
    piece[...] = y[rows_at(row_pos * half, half)]
    s_v[...] = mm(y[...].T, d_v[pl.ds(0, 4 * half)]).T
    out[pl.ds(0, half)] = s_v[rows_at(leaf_pos * half, half)].astype(BF)
    out[pl.ds(half, half)] = s_v[rows_at((1 - leaf_pos) * half, half)].astype(BF)


def put(target, slot, half, source, order):
    for k, side in enumerate(order):
        at = 2 * slot * half + side * half
        target[rows_at(at, half)] = source[pl.ds(k * half, half)]


def leaf_transposed_kernel(
    sizes,
    own,
    rows_x,
    rows_y,
    rows_d,
    d_v,
    mask,
    root_rows,
    panel_rows,
    root_piece,
    total,
    forward,
    y_v,
    s_v,
):
    quarter, half = sizes
    row_pos = lax.axis_index("row")
    leaf_pos = lax.axis_index("leaf")
    order = row_order(row_pos, leaf_pos)
    forward[pl.ds(0, quarter)] = own[...]
    forward[pl.ds(quarter, half)] = root_piece[...]
    for k, part in enumerate((own, rows_x, rows_y, rows_d)):
        y_v[rows_at(order[k] * quarter, quarter)] = part[...]
    value = mm(y_v[...].T, d_v[pl.ds(0, 4 * quarter)])
    value = jnp.where(mask[...].astype(F32).T > 0.0, value, 0.0)
    put(s_v, 0, half, root_rows, (leaf_pos, 1 - leaf_pos))
    total[...] = value - mm(s_v[...].T, panel_rows[pl.ds(0, quarter)])


def own_kernel(sizes, near, far, total, panel_rows, out, s_v):
    quarter, half = sizes
    leaf_pos = lax.axis_index("leaf")
    put(s_v, 0, half, near, (leaf_pos, 1 - leaf_pos))
    value = total[...] - mm(s_v[...].T, panel_rows[pl.ds(2 * quarter, quarter)])
    rows = rows_at(3 * quarter + leaf_pos * half, half)
    out[...] = value - mm(far[...].T, panel_rows[rows])


def last_kernel(sizes, near, far, total, panel_rows, root_rows, out, s_v):
    quarter, half = sizes
    leaf_pos = lax.axis_index("leaf")
    put(s_v, 0, half, near, (1 - leaf_pos, leaf_pos))
    value = total[...] - mm(s_v[...].T, panel_rows[pl.ds(quarter, quarter)])
    rows = rows_at(3 * quarter + (1 - leaf_pos) * half, half)
    value = value - mm(far[...].T, panel_rows[rows])
    out[pl.ds(0, quarter)] = value.T.astype(BF)
    out[pl.ds(quarter, half)] = root_rows[pl.ds(0, half)]


def leaf_swap(value):
    return lax.ppermute(value, "leaf", [(0, 1), (1, 0)])


def row_swap(value, phase):
    route = []
    for leaf in range(2):
        apart = (1 + leaf, 2 - leaf, 3)[phase]
        route += [(4 * leaf + r, 4 * leaf + (r ^ apart)) for r in range(4)]
    return lax.ppermute(value, ("leaf", "row"), route)


def added(left, right):
    return left.astype(F32) + right.astype(F32)


def two_levels(rhs, pivot_inverse, panel, live, parent_map):
    columns = rhs.shape[1]
    quarter = pivot_inverse.shape[1]
    half = quarter // 2
    front = 4 * quarter
    updates = parent_map.shape[1] * B
    after = lambda value, other: lax.optimization_barrier((value, other))[0]
    smem = [pltpu.SMEM(live.shape, jnp.int32), pltpu.SMEM(parent_map.shape, jnp.int32)]

    parts = 4 if updates % (4 * B) == 0 else 1
    send_near, send_rest, keep_near, keep_rest, b_v, masked, mask, w_v, d_v = call(
        functools.partial(panel_kernel, (quarter, half, parts, updates)),
        (
            kept(quarter, columns),
            kept(quarter, columns),
            kept(quarter, columns),
            kept(quarter, columns),
            kept(quarter + half, columns),
            kept(quarter, columns),
            kept(quarter, columns),
            kept(updates, quarter),
            kept(front, quarter),
        ),
        [ANY] * 5,
        [pltpu.VMEM((front, columns), BF), *smem, pltpu.SemaphoreType.DMA((11 + parts,))],
        58_700_000,
        2 * updates * quarter * columns,
        2 * updates * quarter,
    )(live, parent_map, rhs, panel, pivot_inverse)
    away_near = added(keep_near, leaf_swap(send_near)).astype(BF)
    rest = added(keep_rest, leaf_swap(send_rest))
    away_far = rest[:half].astype(BF)
    from_far = row_swap(away_far, 2)
    from_near = row_swap(away_near, 0)

    *pieces, root_d = call(
        functools.partial(leaf_pivot_kernel, (quarter, 4 * half)),
        (*(kept(quarter, columns),) * 4, kept(4 * half, quarter)),
        [VMEM, VMEM, ANY, ANY],
        [pltpu.SemaphoreType.DMA((4,))],
        49_500_000,
        2 * front * quarter * columns,
        2 * front * quarter,
    )(masked, d_v, pivot_inverse, away_near)
    from_near = after(from_near, pieces[0])
    leaf_forward = pieces[0].astype(F32)
    for phase in (2, 0, 1):
        leaf_forward = leaf_forward + row_swap(pieces[1 + phase], phase).astype(F32)
    leaf_forward = jnp.where(mask > 0, leaf_forward, 0.0).astype(BF)
    rows_y = row_swap(leaf_forward, 1)
    rows_x = row_swap(leaf_forward, 0)
    rows_d = row_swap(rows_y, 0)

    term = rest[half:] + from_far.astype(F32) - b_v[quarter:].astype(F32)
    from_near = from_near.astype(F32)
    negated_mine = (from_near[:half] + term).astype(BF)
    negated_yours = from_near[half:].astype(BF)
    other_yours = leaf_swap(negated_yours)
    other_mine = leaf_swap(negated_mine)

    partial = call(
        functools.partial(root_pivot_kernel, half),
        kept(4 * half, columns),
        [VMEM] * 5,
        [pltpu.VMEM((quarter, columns), BF)],
        16 * MIB,
        0,
        0,
    )(negated_mine, negated_yours, other_mine, other_yours, root_d)
    panel_rows = call(
        functools.partial(scatter_kernel, (quarter, updates)),
        kept(front, quarter),
        [ANY, ANY, VMEM, ANY],
        [*smem, pltpu.SemaphoreType.DMA((2,))],
        16 * MIB,
        2000000000,
        4 * front * quarter,
    )(live, parent_map, w_v, after(rows_y, rows_x))
    partial = added(partial, row_swap(partial, 1))
    got = after(row_swap(partial.astype(BF), 0), panel_rows)
    root_forward = (partial + got.astype(F32)).astype(BF)

    part, root_piece = call(
        functools.partial(root_transposed_kernel, half),
        (kept(quarter, columns), kept(half, columns)),
        [VMEM, VMEM],
        [pltpu.VMEM((quarter, columns), F32)],
        16 * MIB,
        0,
        0,
    )(root_forward, root_d)
    got = after(leaf_swap(part), rows_d)
    root_mine = added(part[:half], got[half:]).astype(BF)
    root_other = added(part[half:], got[:half]).astype(BF)
    root_rows = jnp.concatenate([root_mine, root_other], 0)

    near = row_swap(root_rows, 1)
    far = row_swap(root_mine, 2)
    total, forward = call(
        functools.partial(leaf_transposed_kernel, (quarter, half)),
        (kept(columns, quarter, F32), stored(quarter + half, columns)),
        [VMEM] * 9,
        [pltpu.VMEM((front, columns), BF), pltpu.VMEM((quarter, columns), BF)],
        16 * MIB,
        2 * front * quarter * columns,
        2 * front * quarter,
    )(leaf_forward, rows_x, rows_y, rows_d, d_v, mask, root_rows, panel_rows, root_piece)
    near = after(near, total)
    near_other = leaf_swap(near)
    far_other = leaf_swap(far)
    total = call(
        functools.partial(own_kernel, (quarter, half)),
        kept(columns, quarter, F32),
        [VMEM] * 4,
        [pltpu.VMEM((quarter, columns), BF)],
        16 * MIB,
        0,
        0,
    )(near, far, total, panel_rows)
    backward = call(
        functools.partial(last_kernel, (quarter, half)),
        stored(quarter + half, columns),
        [VMEM] * 5,
        [pltpu.VMEM((quarter, columns), BF)],
        16 * MIB,
        front * quarter * columns,
        front * quarter,
    )(near_other, far_other, total, panel_rows, root_rows)
    return forward, backward


def on_device(rhs, pivot_inverse, panel, live, parent_map):
    if lax.axis_size("leaf") == 2 and lax.axis_size("row") == 4:
        return two_levels(rhs, pivot_inverse, panel, live, parent_map)
    return deep_tree(rhs, pivot_inverse, panel, live, parent_map)


def solution(mesh):
    in_specs = (P(("leaf", "row"), "col"), P("leaf", "row"), P("leaf", "row"), P(), P())
    out_specs = (P(("leaf", "row"), "col"), P(("leaf", "row"), "col"))
    return jax.shard_map(
        on_device, mesh=mesh, in_specs=in_specs, out_specs=out_specs, check_vma=False
    )
```

```python
import functools

import jax
import jax.numpy as jnp
from jax import lax
from jax.experimental import pallas as pl
from jax.experimental.pallas import tpu as pltpu
from jax.sharding import PartitionSpec as P

F = 2560
E = 1536


def from_partner(block, axis, apart):
    count = lax.axis_size(axis)
    route = []
    for low in range(count):
        high = low | 1 << apart
        if high != low and high < count:
            route += [(low, high), (high, low)]
    return lax.ppermute(block, axis, route)


def doubling(stacked, bit_count, leaf_pos, swapper):
    for bit_no in range(bit_count):
        partner = swapper(stacked, bit_no)
        upper_half = jnp.right_shift(leaf_pos, bit_no) % 2 == 1
        stacked = jnp.where(
            upper_half,
            jnp.concatenate([partner, stacked], 0),
            jnp.concatenate([stacked, partner], 0),
        )
    return stacked


def halving(partial_value, bit_count, leaf_pos, swapper):
    for bit_no in reversed(range(bit_count)):
        halves = partial_value.reshape((2, partial_value.shape[0] // 2) + partial_value.shape[1:])
        upper_half = jnp.right_shift(leaf_pos, bit_no) % 2 == 1
        kept_half = jnp.where(upper_half, halves[1], halves[0])
        sent_half = jnp.where(upper_half, halves[0], halves[1])
        partial_value = kept_half + swapper(sent_half, bit_no)
    return partial_value[0]


def to_front(group_block, row_count):
    count_g, total_rows, row_width = group_block.shape
    piece_rows = total_rows // row_count
    return (
        group_block.reshape(count_g, row_count, piece_rows, row_width)
        .transpose(1, 0, 2, 3)
        .reshape(count_g * total_rows, row_width)
    )


def block_onehot(mapping):
    return (jnp.arange(F // 128, dtype=jnp.int32)[:, None] == mapping[None, :]).astype(jnp.bfloat16)


def pivot_sum(diag_block, quarter_rows):
    return lax.psum_scatter(
        jnp.dot(diag_block, quarter_rows, preferred_element_type=jnp.float32).astype(jnp.bfloat16),
        "row",
        scatter_dimension=0,
        tiled=True,
    ).astype(jnp.float32)


def quarter_swap(values, bit_no):
    return from_partner(values, "leaf", bit_no)


def update_swap(values, bit_no):
    return from_partner(values, "leaf", bit_no)


def parent_swap(values, bit_no):
    return from_partner(values, "leaf", bit_no)


def reduce_swap(values, bit_no):
    return from_partner(values.astype(jnp.bfloat16), "leaf", bit_no).astype(values.dtype)


def deep_tree(rhs, pivot_inverse, panel, live, parent_map):
    leaves = lax.axis_size("leaf")
    row_count = lax.axis_size("row")
    tree_depth = leaves.bit_length() - 1
    leaf_pos = lax.axis_index("leaf")
    row_pos = lax.axis_index("row")
    columns = rhs.shape[1]
    quarter = F // row_count
    parent_blocks = F // 128
    child_blocks = E // 128
    layout = []
    vec_off, piv_off, pan_off, front_base = (0, 0, 0, 0)
    for level_no in range(tree_depth + 1):
        groups = 2**level_no
        layout.append((groups, vec_off, piv_off, pan_off, front_base))
        vec_off += F // (row_count * groups)
        piv_off += F // groups
        pan_off += E // groups
        front_base += leaves // groups
    forward_parts = []
    live_masks = []
    incoming = None
    for level_no in range(tree_depth + 1):
        groups, vec_off, piv_off, pan_off, front_base = layout[level_no]
        piece_rows = F // (row_count * groups)
        panel_rows = E // (row_count * groups)
        inner_pos = leaf_pos % groups
        front_no = jnp.right_shift(leaf_pos, level_no)
        live_rows = lax.dynamic_index_in_dim(live, front_base + front_no, 0, keepdims=False) * 128
        first_row = (row_pos * groups + inner_pos) * piece_rows
        live_mask = (first_row + jnp.arange(piece_rows, dtype=jnp.int32) < live_rows)[:, None]
        live_masks.append(live_mask)
        right_side = rhs[vec_off : vec_off + piece_rows]
        if incoming is not None:
            right_side = (right_side.astype(jnp.float32) - incoming).astype(jnp.bfloat16)
        masked = jnp.where(live_mask, right_side, jnp.zeros_like(right_side))
        quarter_rows = doubling(masked[None], level_no, leaf_pos, quarter_swap).reshape(
            quarter, columns
        )
        diag_block = pivot_inverse[piv_off : piv_off + F // groups]
        if level_no < tree_depth:
            off_block = panel[pan_off : pan_off + E // groups]
            forward_value = pivot_sum(diag_block, quarter_rows)
            update_rows = lax.psum(
                jnp.dot(off_block, quarter_rows, preferred_element_type=jnp.float32), "row"
            ).astype(jnp.bfloat16)
        else:
            forward_value = pivot_sum(diag_block, quarter_rows)
        forward_parts.append(jnp.where(live_mask, forward_value, 0.0).astype(jnp.bfloat16))
        if level_no < tree_depth:
            gathered = doubling(update_rows[None], level_no + 1, leaf_pos, update_swap)
            parent_front = jnp.right_shift(leaf_pos, level_no + 1)
            assembled = jnp.zeros((parent_blocks, 128, columns), jnp.float32)
            for side_no in range(2):
                child_update = to_front(
                    gathered[side_no * groups : (side_no + 1) * groups], row_count
                )
                mapping = lax.dynamic_index_in_dim(
                    parent_map, front_base + 2 * parent_front + side_no, 0, keepdims=False
                )
                assembled = assembled + jnp.einsum(
                    "ke,eab->kab",
                    block_onehot(mapping),
                    child_update.reshape(child_blocks, 128, columns),
                    preferred_element_type=jnp.float32,
                )
            parent_groups = 2 * groups
            parent_rows = F // (row_count * parent_groups)
            parent_first = (row_pos * parent_groups + leaf_pos % parent_groups) * parent_rows
            incoming = lax.dynamic_slice_in_dim(
                assembled.reshape(F, columns), parent_first, parent_rows, 0
            )
    backward_parts = [None] * (tree_depth + 1)
    parent_value = None
    for level_no in reversed(range(tree_depth + 1)):
        groups, vec_off, piv_off, pan_off, front_base = layout[level_no]
        piece_rows = F // (row_count * groups)
        panel_rows = E // (row_count * groups)
        inner_pos = leaf_pos % groups
        front_no = jnp.right_shift(leaf_pos, level_no)
        diag_block = pivot_inverse[piv_off : piv_off + F // groups]
        own_piece = forward_parts[level_no]
        if level_no == tree_depth:
            own_rows = lax.all_gather(own_piece, "row", axis=0, tiled=True)
            partial_value = jnp.einsum(
                "ik,ia->ka", diag_block, own_rows, preferred_element_type=jnp.float32
            )
        else:
            own_rows, parent_gathered = (
                lax.all_gather(own_piece, "row", axis=0, tiled=True),
                lax.all_gather(parent_value, "row", axis=0, tiled=True),
            )
            whole_parent = doubling(parent_gathered[None], level_no + 1, leaf_pos, parent_swap)
            parent_full = to_front(whole_parent, row_count)
            mapping = lax.dynamic_index_in_dim(parent_map, front_base + front_no, 0, keepdims=False)
            taken_rows = jnp.einsum(
                "ke,kab->eab",
                block_onehot(mapping),
                parent_full.reshape(parent_blocks, 128, columns),
                preferred_element_type=jnp.float32,
            ).astype(jnp.bfloat16)
            taken_rows = lax.dynamic_index_in_dim(
                taken_rows.reshape(row_count, groups, panel_rows, columns),
                inner_pos,
                1,
                keepdims=False,
            ).reshape(row_count * panel_rows, columns)
            off_block = panel[pan_off : pan_off + E // groups]
            partial_value = jnp.einsum(
                "ik,ia->ka", diag_block, own_rows, preferred_element_type=jnp.float32
            ) - jnp.einsum("ik,ia->ka", off_block, taken_rows, preferred_element_type=jnp.float32)
        if level_no == 0:
            reduced = partial_value
        else:
            reduced = halving(
                partial_value.reshape(groups, piece_rows, columns), level_no, leaf_pos, reduce_swap
            )
        parent_value = jnp.where(live_masks[level_no], reduced, 0.0).astype(jnp.bfloat16)
        backward_parts[level_no] = parent_value
    return (jnp.concatenate(forward_parts, 0), jnp.concatenate(backward_parts, 0))


B = 128
VMEM = pl.BlockSpec(memory_space=pltpu.VMEM)
ANY = pl.BlockSpec(memory_space=pl.ANY)
BF = jnp.bfloat16
F32 = jnp.float32
MIB = 1024 * 1024


def stored(rows, columns, dtype=BF):
    return jax.ShapeDtypeStruct((rows, columns), dtype)


def kept(rows, columns, dtype=BF):
    return pltpu.VMEM((rows, columns), dtype)


def call(body, out_shape, in_specs, scratch, limit, flops, bytes_moved):
    return pl.pallas_call(
        body,
        out_shape=out_shape,
        in_specs=in_specs,
        out_specs=jax.tree.map(lambda _: VMEM, out_shape, is_leaf=lambda s: hasattr(s, "shape")),
        scratch_shapes=scratch,
        compiler_params=pltpu.CompilerParams(vmem_limit_bytes=limit),
        cost_estimate=pl.CostEstimate(flops=flops, bytes_accessed=bytes_moved, transcendentals=0),
    )


def rows_at(start, size):
    return pl.ds(pl.multiple_of(start, 16), size)


def mm(left, right):
    return jnp.dot(left, right, preferred_element_type=F32)


def row_order(row_pos, leaf_pos):
    return (row_pos, row_pos ^ (1 + leaf_pos), row_pos ^ (2 - leaf_pos), row_pos ^ 3)


def panel_kernel(
    sizes,
    live,
    pmap,
    rhs,
    panel,
    pivot,
    send_near,
    send_rest,
    keep_near,
    keep_rest,
    first,
    b_v,
    masked,
    mask,
    w_v,
    d_v,
    c_v,
    live_s,
    pmap_s,
    sems,
):
    quarter, half, parts, update_rows = sizes
    leaf_pos = lax.axis_index("leaf")
    row_pos = lax.axis_index("row")
    gets = [
        pltpu.make_async_copy(live, live_s, sems.at[0]),
        pltpu.make_async_copy(rhs, b_v, sems.at[1]),
        pltpu.make_async_copy(pmap, pmap_s, sems.at[2]),
    ]
    step = update_rows // parts
    for i in range(parts):
        rows = pl.ds(i * step, step)
        gets.append(pltpu.make_async_copy(panel.at[rows], w_v.at[rows], sems.at[3 + i]))
    order = row_order(row_pos, leaf_pos)
    for k in (1, 0, 2, 3):
        rows = rows_at(order[k] * quarter, quarter)
        get = pltpu.make_async_copy(pivot.at[rows], d_v.at[rows], sems.at[3 + parts + k])
        gets.append(get)
    for get in gets:
        get.start()
    c_v[...] = jnp.zeros_like(c_v)
    gets[0].wait()
    gets[1].wait()
    value = b_v[pl.ds(0, quarter)]
    row = row_pos * quarter + lax.broadcasted_iota(jnp.int32, value.shape, 0)
    alive = row < live_s[leaf_pos] * B
    mask[...] = jnp.where(alive, 1.0, 0.0).astype(BF)
    masked[...] = jnp.where(alive, value, jnp.zeros_like(value))
    right = masked[...]
    gets[2].wait()
    for i in range(parts):
        gets[3 + i].wait()
        product = mm(w_v[pl.ds(i * step, step)], right).astype(BF)
        for e in range(step // B):
            block = pmap_s[leaf_pos, i * (step // B) + e]
            c_v[pl.ds(pl.multiple_of(block * B, B), B)] = product[e * B : (e + 1) * B]
    for near_out, rest, side in (
        (send_near, send_rest, 1 - leaf_pos),
        (keep_near, keep_rest, leaf_pos),
    ):
        near = (row_pos ^ (1 + side)) * quarter
        mine, other = side * half, (1 - side) * half
        near_out[pl.ds(0, half)] = c_v[rows_at(near + mine, half)]
        near_out[pl.ds(half, half)] = c_v[rows_at(near + other, half)]
        rest[pl.ds(0, half)] = c_v[rows_at((row_pos ^ 3) * quarter + mine, half)]
        rest[pl.ds(half, half)] = c_v[rows_at(row_pos * quarter + mine, half)]
    gets[3 + parts].wait()
    first[...] = mm(d_v[rows_at(order[1] * quarter, quarter)], right).astype(BF)
    for get in gets[4 + parts :]:
        get.wait()


def leaf_pivot_kernel(sizes, masked, d_v, pivot, after, *outs_and_scratch):
    quarter, rows = sizes
    *outs, root_d, sem = outs_and_scratch
    get = pltpu.make_async_copy(pivot.at[pl.ds(4 * quarter, rows)], root_d, sem)
    get.start()
    order = row_order(lax.axis_index("row"), lax.axis_index("leaf"))
    right = masked[...]
    for k, out in zip((3, 2, 0), outs):
        product = mm(d_v[rows_at(order[k] * quarter, quarter)], right)
        out[...] = product.astype(BF)
    get.wait()


def scatter_kernel(sizes, live, pmap, w_v, after, out, live_s, pmap_s, sems):
    quarter, update_rows = sizes
    leaf_pos = lax.axis_index("leaf")
    row_pos = lax.axis_index("row")
    gets = [
        pltpu.make_async_copy(live, live_s, sems.at[0]),
        pltpu.make_async_copy(pmap, pmap_s, sems.at[1]),
    ]
    for get in gets:
        get.start()
    per_row = quarter // B
    out[...] = jnp.zeros_like(out)
    for get in gets:
        get.wait()
    column = row_pos * quarter + lax.broadcasted_iota(jnp.int32, (B, quarter), 1)
    alive = column < live_s[leaf_pos] * B
    for e in range(update_rows // B):
        value = w_v[pl.ds(e * B, B)]
        block = pmap_s[leaf_pos, e]
        away = (block // per_row) ^ row_pos
        slot = jnp.where(away == 1 + leaf_pos, 1, jnp.where(away == 2 - leaf_pos, 2, away))
        at = (slot * per_row + block % per_row) * B
        out[pl.ds(pl.multiple_of(at, B), B)] = jnp.where(alive, value, jnp.zeros_like(value))


def root_pivot_kernel(sizes, mine, yours, other_mine, other_yours, d_v, out, q_v):
    half = sizes
    leaf_pos = lax.axis_index("leaf")
    for own, other, at in ((mine, other_yours, leaf_pos), (yours, other_mine, 1 - leaf_pos)):
        value = own[...].astype(F32) + other[...].astype(F32)
        q_v[rows_at(at * half, half)] = (-value).astype(BF)
    out[...] = mm(d_v[pl.ds(0, 4 * half)], q_v[...]).astype(BF)


def root_transposed_kernel(sizes, y, d_v, out, piece, s_v):
    half = sizes
    leaf_pos = lax.axis_index("leaf")
    row_pos = lax.axis_index("row")
    piece[...] = y[rows_at(row_pos * half, half)]
    s_v[...] = mm(y[...].T, d_v[pl.ds(0, 4 * half)]).T
    out[pl.ds(0, half)] = s_v[rows_at(leaf_pos * half, half)].astype(BF)
    out[pl.ds(half, half)] = s_v[rows_at((1 - leaf_pos) * half, half)].astype(BF)


def put(target, slot, half, source, order):
    for k, side in enumerate(order):
        at = 2 * slot * half + side * half
        target[rows_at(at, half)] = source[pl.ds(k * half, half)]


def leaf_transposed_kernel(
    sizes,
    own,
    rows_x,
    rows_y,
    rows_d,
    d_v,
    mask,
    root_rows,
    panel_rows,
    root_piece,
    total,
    forward,
    y_v,
    s_v,
):
    quarter, half = sizes
    row_pos = lax.axis_index("row")
    leaf_pos = lax.axis_index("leaf")
    order = row_order(row_pos, leaf_pos)
    forward[pl.ds(0, quarter)] = own[...]
    forward[pl.ds(quarter, half)] = root_piece[...]
    for k, part in enumerate((own, rows_x, rows_y, rows_d)):
        y_v[rows_at(order[k] * quarter, quarter)] = part[...]
    value = mm(y_v[...].T, d_v[pl.ds(0, 4 * quarter)])
    value = jnp.where(mask[...].astype(F32).T > 0.0, value, 0.0)
    put(s_v, 0, half, root_rows, (leaf_pos, 1 - leaf_pos))
    total[...] = value - mm(s_v[...].T, panel_rows[pl.ds(0, quarter)])


def own_kernel(sizes, near, far, total, panel_rows, out, s_v):
    quarter, half = sizes
    leaf_pos = lax.axis_index("leaf")
    put(s_v, 0, half, near, (leaf_pos, 1 - leaf_pos))
    value = total[...] - mm(s_v[...].T, panel_rows[pl.ds(2 * quarter, quarter)])
    rows = rows_at(3 * quarter + leaf_pos * half, half)
    out[...] = value - mm(far[...].T, panel_rows[rows])


def last_kernel(sizes, near, far, total, panel_rows, root_rows, out, s_v):
    quarter, half = sizes
    leaf_pos = lax.axis_index("leaf")
    put(s_v, 0, half, near, (1 - leaf_pos, leaf_pos))
    value = total[...] - mm(s_v[...].T, panel_rows[pl.ds(quarter, quarter)])
    rows = rows_at(3 * quarter + (1 - leaf_pos) * half, half)
    value = value - mm(far[...].T, panel_rows[rows])
    out[pl.ds(0, quarter)] = value.T.astype(BF)
    out[pl.ds(quarter, half)] = root_rows[pl.ds(0, half)]


def leaf_swap(value):
    return lax.ppermute(value, "leaf", [(0, 1), (1, 0)])


def row_swap(value, phase):
    route = []
    for leaf in range(2):
        apart = (1 + leaf, 2 - leaf, 3)[phase]
        route += [(4 * leaf + r, 4 * leaf + (r ^ apart)) for r in range(4)]
    return lax.ppermute(value, ("leaf", "row"), route)


def added(left, right):
    return left.astype(F32) + right.astype(F32)


def two_levels(rhs, pivot_inverse, panel, live, parent_map):
    columns = rhs.shape[1]
    quarter = pivot_inverse.shape[1]
    half = quarter // 2
    front = 4 * quarter
    updates = parent_map.shape[1] * B
    after = lambda value, other: lax.optimization_barrier((value, other))[0]
    smem = [pltpu.SMEM(live.shape, jnp.int32), pltpu.SMEM(parent_map.shape, jnp.int32)]

    parts = 4 if updates % (4 * B) == 0 else 1
    (
        send_near,
        send_rest,
        keep_near,
        keep_rest,
        first,
        b_v,
        masked,
        mask,
        w_v,
        d_v,
    ) = call(
        functools.partial(panel_kernel, (quarter, half, parts, updates)),
        (
            kept(quarter, columns),
            kept(quarter, columns),
            kept(quarter, columns),
            kept(quarter, columns),
            kept(quarter, columns),
            kept(quarter + half, columns),
            kept(quarter, columns),
            kept(quarter, columns),
            kept(updates, quarter),
            kept(front, quarter),
        ),
        [ANY] * 5,
        [pltpu.VMEM((front, columns), BF), *smem, pltpu.SemaphoreType.DMA((7 + parts,))],
        58_700_000,
        2 * updates * quarter * columns,
        2 * updates * quarter,
    )(live, parent_map, rhs, panel, pivot_inverse)
    away_near = added(keep_near, leaf_swap(send_near)).astype(BF)
    rest = added(keep_rest, leaf_swap(send_rest))
    away_far = rest[:half].astype(BF)
    from_far = row_swap(away_far, 2)
    from_near = row_swap(away_near, 0)

    got_first = row_swap(first, 0)
    *pieces, root_d = call(
        functools.partial(leaf_pivot_kernel, (quarter, 4 * half)),
        (*(kept(quarter, columns),) * 3, kept(4 * half, quarter)),
        [VMEM, VMEM, ANY, ANY],
        [pltpu.SemaphoreType.DMA],
        49_500_000,
        2 * front * quarter * columns,
        2 * front * quarter,
    )(masked, d_v, pivot_inverse, after(got_first,(away_near,away_far)))
    from_near = after(from_near, pieces[0])
    leaf_forward = added(pieces[2], got_first)
    leaf_forward = leaf_forward + row_swap(pieces[0], 2).astype(F32)
    leaf_forward = leaf_forward + row_swap(pieces[1], 1).astype(F32)
    leaf_forward = jnp.where(mask > 0, leaf_forward, 0.0).astype(BF)
    rows_y = row_swap(leaf_forward, 1)
    rows_x = row_swap(leaf_forward, 0)
    rows_d = row_swap(rows_y, 0)

    term = rest[half:] + from_far.astype(F32) - b_v[quarter:].astype(F32)
    from_near = from_near.astype(F32)
    negated_mine = (from_near[:half] + term).astype(BF)
    negated_yours = from_near[half:].astype(BF)
    other_yours = leaf_swap(negated_yours)
    other_mine = leaf_swap(negated_mine)

    partial = call(
        functools.partial(root_pivot_kernel, half),
        kept(4 * half, columns),
        [VMEM] * 5,
        [pltpu.VMEM((quarter, columns), BF)],
        16 * MIB,
        0,
        0,
    )(negated_mine, negated_yours, other_mine, other_yours, root_d)
    panel_rows = call(
        functools.partial(scatter_kernel, (quarter, updates)),
        kept(front, quarter),
        [ANY, ANY, VMEM, ANY],
        [*smem, pltpu.SemaphoreType.DMA((2,))],
        16 * MIB,
        2000000000,
        4 * front * quarter,
    )(live, parent_map, w_v, after(rows_y, rows_x))
    partial = added(partial, row_swap(partial, 1))
    got = after(row_swap(partial.astype(BF), 0), panel_rows)
    root_forward = (partial + got.astype(F32)).astype(BF)

    part, root_piece = call(
        functools.partial(root_transposed_kernel, half),
        (kept(quarter, columns), kept(half, columns)),
        [VMEM, VMEM],
        [pltpu.VMEM((quarter, columns), F32)],
        16 * MIB,
        0,
        0,
    )(root_forward, root_d)
    got = after(leaf_swap(part), rows_d)
    root_mine = added(part[:half], got[half:]).astype(BF)
    root_other = added(part[half:], got[:half]).astype(BF)
    root_rows = jnp.concatenate([root_mine, root_other], 0)

    near = row_swap(root_rows, 1)
    far = row_swap(root_mine, 2)
    total, forward = call(
        functools.partial(leaf_transposed_kernel, (quarter, half)),
        (kept(columns, quarter, F32), stored(quarter + half, columns)),
        [VMEM] * 9,
        [pltpu.VMEM((front, columns), BF), pltpu.VMEM((quarter, columns), BF)],
        16 * MIB,
        2 * front * quarter * columns,
        2 * front * quarter,
    )(leaf_forward, rows_x, rows_y, rows_d, d_v, mask, root_rows, panel_rows, root_piece)
    near = after(near, total)
    near_other = leaf_swap(near)
    far_other = leaf_swap(far)
    total = call(
        functools.partial(own_kernel, (quarter, half)),
        kept(columns, quarter, F32),
        [VMEM] * 4,
        [pltpu.VMEM((quarter, columns), BF)],
        16 * MIB,
        0,
        0,
    )(near, far, total, panel_rows)
    backward = call(
        functools.partial(last_kernel, (quarter, half)),
        stored(quarter + half, columns),
        [VMEM] * 5,
        [pltpu.VMEM((quarter, columns), BF)],
        16 * MIB,
        front * quarter * columns,
        front * quarter,
    )(near_other, far_other, total, panel_rows, root_rows)
    return forward, backward


def on_device(rhs, pivot_inverse, panel, live, parent_map):
    if lax.axis_size("leaf") == 2 and lax.axis_size("row") == 4:
        return two_levels(rhs, pivot_inverse, panel, live, parent_map)
    return deep_tree(rhs, pivot_inverse, panel, live, parent_map)


def solution(mesh):
    in_specs = (P(("leaf", "row"), "col"), P("leaf", "row"), P("leaf", "row"), P(), P())
    out_specs = (P(("leaf", "row"), "col"), P(("leaf", "row"), "col"))
    return jax.shard_map(
        on_device, mesh=mesh, in_specs=in_specs, out_specs=out_specs, check_vma=False
    )
```

```python
import functools

import jax
import jax.numpy as jnp
from jax import lax
from jax.experimental import pallas as pl
from jax.experimental.pallas import tpu as pltpu
from jax.sharding import PartitionSpec as P

F = 2560
E = 1536


def from_partner(block, axis, apart):
    count = lax.axis_size(axis)
    route = []
    for low in range(count):
        high = low | 1 << apart
        if high != low and high < count:
            route += [(low, high), (high, low)]
    return lax.ppermute(block, axis, route)


def doubling(stacked, bit_count, leaf_pos, swapper):
    for bit_no in range(bit_count):
        partner = swapper(stacked, bit_no)
        upper_half = jnp.right_shift(leaf_pos, bit_no) % 2 == 1
        stacked = jnp.where(
            upper_half,
            jnp.concatenate([partner, stacked], 0),
            jnp.concatenate([stacked, partner], 0),
        )
    return stacked


def halving(partial_value, bit_count, leaf_pos, swapper):
    for bit_no in reversed(range(bit_count)):
        halves = partial_value.reshape((2, partial_value.shape[0] // 2) + partial_value.shape[1:])
        upper_half = jnp.right_shift(leaf_pos, bit_no) % 2 == 1
        kept_half = jnp.where(upper_half, halves[1], halves[0])
        sent_half = jnp.where(upper_half, halves[0], halves[1])
        partial_value = kept_half + swapper(sent_half, bit_no)
    return partial_value[0]


def to_front(group_block, row_count):
    count_g, total_rows, row_width = group_block.shape
    piece_rows = total_rows // row_count
    return (
        group_block.reshape(count_g, row_count, piece_rows, row_width)
        .transpose(1, 0, 2, 3)
        .reshape(count_g * total_rows, row_width)
    )


def block_onehot(mapping):
    return (jnp.arange(F // 128, dtype=jnp.int32)[:, None] == mapping[None, :]).astype(jnp.bfloat16)


def pivot_sum(diag_block, quarter_rows):
    return lax.psum_scatter(
        jnp.dot(diag_block, quarter_rows, preferred_element_type=jnp.float32).astype(jnp.bfloat16),
        "row",
        scatter_dimension=0,
        tiled=True,
    ).astype(jnp.float32)


def quarter_swap(values, bit_no):
    return from_partner(values, "leaf", bit_no)


def update_swap(values, bit_no):
    return from_partner(values, "leaf", bit_no)


def parent_swap(values, bit_no):
    return from_partner(values, "leaf", bit_no)


def reduce_swap(values, bit_no):
    return from_partner(values.astype(jnp.bfloat16), "leaf", bit_no).astype(values.dtype)


def deep_tree(rhs, pivot_inverse, panel, live, parent_map):
    leaves = lax.axis_size("leaf")
    row_count = lax.axis_size("row")
    tree_depth = leaves.bit_length() - 1
    leaf_pos = lax.axis_index("leaf")
    row_pos = lax.axis_index("row")
    columns = rhs.shape[1]
    quarter = F // row_count
    parent_blocks = F // 128
    child_blocks = E // 128
    layout = []
    vec_off, piv_off, pan_off, front_base = (0, 0, 0, 0)
    for level_no in range(tree_depth + 1):
        groups = 2**level_no
        layout.append((groups, vec_off, piv_off, pan_off, front_base))
        vec_off += F // (row_count * groups)
        piv_off += F // groups
        pan_off += E // groups
        front_base += leaves // groups
    forward_parts = []
    live_masks = []
    incoming = None
    for level_no in range(tree_depth + 1):
        groups, vec_off, piv_off, pan_off, front_base = layout[level_no]
        piece_rows = F // (row_count * groups)
        panel_rows = E // (row_count * groups)
        inner_pos = leaf_pos % groups
        front_no = jnp.right_shift(leaf_pos, level_no)
        live_rows = lax.dynamic_index_in_dim(live, front_base + front_no, 0, keepdims=False) * 128
        first_row = (row_pos * groups + inner_pos) * piece_rows
        live_mask = (first_row + jnp.arange(piece_rows, dtype=jnp.int32) < live_rows)[:, None]
        live_masks.append(live_mask)
        right_side = rhs[vec_off : vec_off + piece_rows]
        if incoming is not None:
            right_side = (right_side.astype(jnp.float32) - incoming).astype(jnp.bfloat16)
        masked = jnp.where(live_mask, right_side, jnp.zeros_like(right_side))
        quarter_rows = doubling(masked[None], level_no, leaf_pos, quarter_swap).reshape(
            quarter, columns
        )
        diag_block = pivot_inverse[piv_off : piv_off + F // groups]
        if level_no < tree_depth:
            off_block = panel[pan_off : pan_off + E // groups]
            forward_value = pivot_sum(diag_block, quarter_rows)
            update_rows = lax.psum(
                jnp.dot(off_block, quarter_rows, preferred_element_type=jnp.float32), "row"
            ).astype(jnp.bfloat16)
        else:
            forward_value = pivot_sum(diag_block, quarter_rows)
        forward_parts.append(jnp.where(live_mask, forward_value, 0.0).astype(jnp.bfloat16))
        if level_no < tree_depth:
            gathered = doubling(update_rows[None], level_no + 1, leaf_pos, update_swap)
            parent_front = jnp.right_shift(leaf_pos, level_no + 1)
            assembled = jnp.zeros((parent_blocks, 128, columns), jnp.float32)
            for side_no in range(2):
                child_update = to_front(
                    gathered[side_no * groups : (side_no + 1) * groups], row_count
                )
                mapping = lax.dynamic_index_in_dim(
                    parent_map, front_base + 2 * parent_front + side_no, 0, keepdims=False
                )
                assembled = assembled + jnp.einsum(
                    "ke,eab->kab",
                    block_onehot(mapping),
                    child_update.reshape(child_blocks, 128, columns),
                    preferred_element_type=jnp.float32,
                )
            parent_groups = 2 * groups
            parent_rows = F // (row_count * parent_groups)
            parent_first = (row_pos * parent_groups + leaf_pos % parent_groups) * parent_rows
            incoming = lax.dynamic_slice_in_dim(
                assembled.reshape(F, columns), parent_first, parent_rows, 0
            )
    backward_parts = [None] * (tree_depth + 1)
    parent_value = None
    for level_no in reversed(range(tree_depth + 1)):
        groups, vec_off, piv_off, pan_off, front_base = layout[level_no]
        piece_rows = F // (row_count * groups)
        panel_rows = E // (row_count * groups)
        inner_pos = leaf_pos % groups
        front_no = jnp.right_shift(leaf_pos, level_no)
        diag_block = pivot_inverse[piv_off : piv_off + F // groups]
        own_piece = forward_parts[level_no]
        if level_no == tree_depth:
            own_rows = lax.all_gather(own_piece, "row", axis=0, tiled=True)
            partial_value = jnp.einsum(
                "ik,ia->ka", diag_block, own_rows, preferred_element_type=jnp.float32
            )
        else:
            own_rows, parent_gathered = (
                lax.all_gather(own_piece, "row", axis=0, tiled=True),
                lax.all_gather(parent_value, "row", axis=0, tiled=True),
            )
            whole_parent = doubling(parent_gathered[None], level_no + 1, leaf_pos, parent_swap)
            parent_full = to_front(whole_parent, row_count)
            mapping = lax.dynamic_index_in_dim(parent_map, front_base + front_no, 0, keepdims=False)
            taken_rows = jnp.einsum(
                "ke,kab->eab",
                block_onehot(mapping),
                parent_full.reshape(parent_blocks, 128, columns),
                preferred_element_type=jnp.float32,
            ).astype(jnp.bfloat16)
            taken_rows = lax.dynamic_index_in_dim(
                taken_rows.reshape(row_count, groups, panel_rows, columns),
                inner_pos,
                1,
                keepdims=False,
            ).reshape(row_count * panel_rows, columns)
            off_block = panel[pan_off : pan_off + E // groups]
            partial_value = jnp.einsum(
                "ik,ia->ka", diag_block, own_rows, preferred_element_type=jnp.float32
            ) - jnp.einsum("ik,ia->ka", off_block, taken_rows, preferred_element_type=jnp.float32)
        if level_no == 0:
            reduced = partial_value
        else:
            reduced = halving(
                partial_value.reshape(groups, piece_rows, columns), level_no, leaf_pos, reduce_swap
            )
        parent_value = jnp.where(live_masks[level_no], reduced, 0.0).astype(jnp.bfloat16)
        backward_parts[level_no] = parent_value
    return (jnp.concatenate(forward_parts, 0), jnp.concatenate(backward_parts, 0))


B = 128
VMEM = pl.BlockSpec(memory_space=pltpu.VMEM)
ANY = pl.BlockSpec(memory_space=pl.ANY)
BF = jnp.bfloat16
F32 = jnp.float32
MIB = 1024 * 1024


def stored(rows, columns, dtype=BF):
    return jax.ShapeDtypeStruct((rows, columns), dtype)


def kept(rows, columns, dtype=BF):
    return pltpu.VMEM((rows, columns), dtype)


def call(body, out_shape, in_specs, scratch, limit, flops, bytes_moved):
    return pl.pallas_call(
        body,
        out_shape=out_shape,
        in_specs=in_specs,
        out_specs=jax.tree.map(lambda _: VMEM, out_shape, is_leaf=lambda s: hasattr(s, "shape")),
        scratch_shapes=scratch,
        compiler_params=pltpu.CompilerParams(vmem_limit_bytes=limit),
        cost_estimate=pl.CostEstimate(flops=flops, bytes_accessed=bytes_moved, transcendentals=0),
    )


def rows_at(start, size):
    return pl.ds(pl.multiple_of(start, 16), size)


def mm(left, right):
    return jnp.dot(left, right, preferred_element_type=F32)


def row_order(row_pos, leaf_pos):
    return (row_pos, row_pos ^ (1 + leaf_pos), row_pos ^ (2 - leaf_pos), row_pos ^ 3)


def panel_kernel(
    sizes,
    live,
    pmap,
    rhs,
    panel,
    pivot,
    send_near,
    send_rest,
    keep_near,
    keep_rest,
    first,
    b_v,
    masked,
    mask,
    w_v,
    d_v,
    c_v,
    live_s,
    pmap_s,
    sems,
):
    quarter, half, parts, update_rows = sizes
    leaf_pos = lax.axis_index("leaf")
    row_pos = lax.axis_index("row")
    gets = [
        pltpu.make_async_copy(live, live_s, sems.at[0]),
        pltpu.make_async_copy(rhs, b_v, sems.at[1]),
        pltpu.make_async_copy(pmap, pmap_s, sems.at[2]),
    ]
    step = update_rows // parts
    for i in range(parts):
        rows = pl.ds(i * step, step)
        gets.append(pltpu.make_async_copy(panel.at[rows], w_v.at[rows], sems.at[3 + i]))
    order = row_order(row_pos, leaf_pos)
    for k in (1, 0, 2, 3):
        rows = rows_at(order[k] * quarter, quarter)
        get = pltpu.make_async_copy(pivot.at[rows], d_v.at[rows], sems.at[3 + parts + k])
        gets.append(get)
    for get in gets:
        get.start()
    c_v[...] = jnp.zeros_like(c_v)
    gets[0].wait()
    gets[1].wait()
    value = b_v[pl.ds(0, quarter)]
    row = row_pos * quarter + lax.broadcasted_iota(jnp.int32, value.shape, 0)
    alive = row < live_s[leaf_pos] * B
    mask[...] = jnp.where(alive, 1.0, 0.0).astype(BF)
    masked[...] = jnp.where(alive, value, jnp.zeros_like(value))
    right = masked[...]
    gets[2].wait()
    for i in range(parts):
        gets[3 + i].wait()
        product = mm(w_v[pl.ds(i * step, step)], right).astype(BF)
        for e in range(step // B):
            block = pmap_s[leaf_pos, i * (step // B) + e]
            c_v[pl.ds(pl.multiple_of(block * B, B), B)] = product[e * B : (e + 1) * B]
    for near_out, rest, side in (
        (send_near, send_rest, 1 - leaf_pos),
        (keep_near, keep_rest, leaf_pos),
    ):
        near = (row_pos ^ (1 + side)) * quarter
        mine, other = side * half, (1 - side) * half
        near_out[pl.ds(0, half)] = c_v[rows_at(near + mine, half)]
        near_out[pl.ds(half, half)] = c_v[rows_at(near + other, half)]
        rest[pl.ds(0, half)] = c_v[rows_at((row_pos ^ 3) * quarter + mine, half)]
        rest[pl.ds(half, half)] = c_v[rows_at(row_pos * quarter + mine, half)]
    gets[3 + parts].wait()
    first[...] = mm(d_v[rows_at(order[1] * quarter, quarter)], right).astype(BF)
    for get in gets[4 + parts :]:
        get.wait()


def leaf_pivot_kernel(sizes, masked, d_v, pivot, after, *outs_and_scratch):
    quarter, rows = sizes
    *outs, root_d, sem = outs_and_scratch
    get = pltpu.make_async_copy(pivot.at[pl.ds(4 * quarter, rows)], root_d, sem)
    get.start()
    order = row_order(lax.axis_index("row"), lax.axis_index("leaf"))
    right = masked[...]
    for k, out in zip((3, 2, 0), outs):
        product = mm(d_v[rows_at(order[k] * quarter, quarter)], right)
        out[...] = product.astype(BF)
    get.wait()


def scatter_kernel(sizes, live, pmap, w_v, after, out, live_s, pmap_s, sems):
    quarter, update_rows = sizes
    leaf_pos = lax.axis_index("leaf")
    row_pos = lax.axis_index("row")
    gets = [
        pltpu.make_async_copy(live, live_s, sems.at[0]),
        pltpu.make_async_copy(pmap, pmap_s, sems.at[1]),
    ]
    for get in gets:
        get.start()
    per_row = quarter // B
    out[...] = jnp.zeros_like(out)
    for get in gets:
        get.wait()
    column = row_pos * quarter + lax.broadcasted_iota(jnp.int32, (B, quarter), 1)
    alive = column < live_s[leaf_pos] * B
    for e in range(update_rows // B):
        value = w_v[pl.ds(e * B, B)]
        block = pmap_s[leaf_pos, e]
        away = (block // per_row) ^ row_pos
        slot = jnp.where(away == 1 + leaf_pos, 1, jnp.where(away == 2 - leaf_pos, 2, away))
        at = (slot * per_row + block % per_row) * B
        out[pl.ds(pl.multiple_of(at, B), B)] = jnp.where(alive, value, jnp.zeros_like(value))


def root_pivot_kernel(sizes, mine, yours, other_mine, other_yours, d_v, out, q_v):
    half = sizes
    leaf_pos = lax.axis_index("leaf")
    for own, other, at in ((mine, other_yours, leaf_pos), (yours, other_mine, 1 - leaf_pos)):
        value = own[...].astype(F32) + other[...].astype(F32)
        q_v[rows_at(at * half, half)] = (-value).astype(BF)
    out[...] = mm(d_v[pl.ds(0, 4 * half)], q_v[...]).astype(BF)


def root_transposed_kernel(sizes, y, d_v, out, piece, s_v):
    half = sizes
    leaf_pos = lax.axis_index("leaf")
    row_pos = lax.axis_index("row")
    piece[...] = y[rows_at(row_pos * half, half)]
    s_v[...] = mm(y[...].T, d_v[pl.ds(0, 4 * half)]).T
    out[pl.ds(0, half)] = s_v[rows_at(leaf_pos * half, half)].astype(BF)
    out[pl.ds(half, half)] = s_v[rows_at((1 - leaf_pos) * half, half)].astype(BF)


def put(target, slot, half, source, order):
    for k, side in enumerate(order):
        at = 2 * slot * half + side * half
        target[rows_at(at, half)] = source[pl.ds(k * half, half)]


def leaf_transposed_kernel(
    sizes,
    own,
    rows_x,
    rows_y,
    rows_d,
    d_v,
    mask,
    root_rows,
    panel_rows,
    root_piece,
    total,
    forward,
    y_v,
    s_v,
):
    quarter, half = sizes
    row_pos = lax.axis_index("row")
    leaf_pos = lax.axis_index("leaf")
    order = row_order(row_pos, leaf_pos)
    forward[pl.ds(0, quarter)] = own[...]
    forward[pl.ds(quarter, half)] = root_piece[...]
    for k, part in enumerate((own, rows_x, rows_y, rows_d)):
        y_v[rows_at(order[k] * quarter, quarter)] = part[...]
    value = mm(y_v[...].T, d_v[pl.ds(0, 4 * quarter)])
    value = jnp.where(mask[...].astype(F32).T > 0.0, value, 0.0)
    put(s_v, 0, half, root_rows, (leaf_pos, 1 - leaf_pos))
    total[...] = value - mm(s_v[...].T, panel_rows[pl.ds(0, quarter)])


def own_kernel(sizes, near, far, total, panel_rows, out, s_v):
    quarter, half = sizes
    leaf_pos = lax.axis_index("leaf")
    put(s_v, 0, half, near, (leaf_pos, 1 - leaf_pos))
    value = total[...] - mm(s_v[...].T, panel_rows[pl.ds(2 * quarter, quarter)])
    rows = rows_at(3 * quarter + leaf_pos * half, half)
    out[...] = value - mm(far[...].T, panel_rows[rows])


def last_kernel(sizes, near, far, total, panel_rows, root_rows, out, s_v):
    quarter, half = sizes
    leaf_pos = lax.axis_index("leaf")
    put(s_v, 0, half, near, (1 - leaf_pos, leaf_pos))
    value = total[...] - mm(s_v[...].T, panel_rows[pl.ds(quarter, quarter)])
    rows = rows_at(3 * quarter + (1 - leaf_pos) * half, half)
    value = value - mm(far[...].T, panel_rows[rows])
    out[pl.ds(0, quarter)] = value.T.astype(BF)
    out[pl.ds(quarter, half)] = root_rows[pl.ds(0, half)]


def leaf_swap(value):
    return lax.ppermute(value, "leaf", [(0, 1), (1, 0)])


def row_swap(value, phase):
    route = []
    for leaf in range(2):
        apart = (1 + leaf, 2 - leaf, 3)[phase]
        route += [(4 * leaf + r, 4 * leaf + (r ^ apart)) for r in range(4)]
    return lax.ppermute(value, ("leaf", "row"), route)


def added(left, right):
    return left.astype(F32) + right.astype(F32)


def two_levels(rhs, pivot_inverse, panel, live, parent_map):
    columns = rhs.shape[1]
    quarter = pivot_inverse.shape[1]
    half = quarter // 2
    front = 4 * quarter
    updates = parent_map.shape[1] * B
    after = lambda value, other: lax.optimization_barrier((value, other))[0]
    smem = [pltpu.SMEM(live.shape, jnp.int32), pltpu.SMEM(parent_map.shape, jnp.int32)]

    parts = 4 if updates % (4 * B) == 0 else 1
    (
        send_near,
        send_rest,
        keep_near,
        keep_rest,
        first,
        b_v,
        masked,
        mask,
        w_v,
        d_v,
    ) = call(
        functools.partial(panel_kernel, (quarter, half, parts, updates)),
        (
            kept(quarter, columns),
            kept(quarter, columns),
            kept(quarter, columns),
            kept(quarter, columns),
            kept(quarter, columns),
            kept(quarter + half, columns),
            kept(quarter, columns),
            kept(quarter, columns),
            kept(updates, quarter),
            kept(front, quarter),
        ),
        [ANY] * 5,
        [pltpu.VMEM((front, columns), BF), *smem, pltpu.SemaphoreType.DMA((7 + parts,))],
        58_700_000,
        2 * updates * quarter * columns,
        2 * updates * quarter,
    )(live, parent_map, rhs, panel, pivot_inverse)
    away_near = added(keep_near, leaf_swap(send_near)).astype(BF)
    rest = added(keep_rest, leaf_swap(send_rest))
    away_far = rest[:half].astype(BF)
    from_far = row_swap(away_far, 2)
    from_near = row_swap(away_near, 0)

    got_first = row_swap(first, 0)
    *pieces, root_d = call(
        functools.partial(leaf_pivot_kernel, (quarter, 4 * half)),
        (*(kept(quarter, columns),) * 3, kept(4 * half, quarter)),
        [VMEM, VMEM, ANY, ANY],
        [pltpu.SemaphoreType.DMA],
        49_500_000,
        2 * front * quarter * columns,
        2 * front * quarter,
    )(masked, d_v, pivot_inverse, after(away_near,away_far))
    from_near = after(from_near, pieces[0])
    leaf_forward = added(pieces[2], got_first)
    leaf_forward = leaf_forward + row_swap(pieces[0], 2).astype(F32)
    second = row_swap(after(pieces[1], got_first), 1)
    leaf_forward = leaf_forward + second.astype(F32)
    leaf_forward = jnp.where(mask > 0, leaf_forward, 0.0).astype(BF)
    rows_y = row_swap(leaf_forward, 1)
    rows_x = row_swap(leaf_forward, 0)
    rows_d = row_swap(rows_y, 0)

    term = rest[half:] + from_far.astype(F32) - b_v[quarter:].astype(F32)
    from_near = from_near.astype(F32)
    negated_mine = (from_near[:half] + term).astype(BF)
    negated_yours = from_near[half:].astype(BF)
    other_yours = leaf_swap(negated_yours)
    other_mine = leaf_swap(negated_mine)

    partial = call(
        functools.partial(root_pivot_kernel, half),
        kept(4 * half, columns),
        [VMEM] * 5,
        [pltpu.VMEM((quarter, columns), BF)],
        16 * MIB,
        0,
        0,
    )(negated_mine, negated_yours, other_mine, other_yours, root_d)
    panel_rows = call(
        functools.partial(scatter_kernel, (quarter, updates)),
        kept(front, quarter),
        [ANY, ANY, VMEM, ANY],
        [*smem, pltpu.SemaphoreType.DMA((2,))],
        16 * MIB,
        2000000000,
        4 * front * quarter,
    )(live, parent_map, w_v, after(rows_y, rows_x))
    partial = added(partial, row_swap(partial, 1))
    got = after(row_swap(partial.astype(BF), 0), panel_rows)
    root_forward = (partial + got.astype(F32)).astype(BF)

    part, root_piece = call(
        functools.partial(root_transposed_kernel, half),
        (kept(quarter, columns), kept(half, columns)),
        [VMEM, VMEM],
        [pltpu.VMEM((quarter, columns), F32)],
        16 * MIB,
        0,
        0,
    )(root_forward, root_d)
    got = after(leaf_swap(part), rows_d)
    root_mine = added(part[:half], got[half:]).astype(BF)
    root_other = added(part[half:], got[:half]).astype(BF)
    root_rows = jnp.concatenate([root_mine, root_other], 0)

    near = row_swap(root_rows, 1)
    far = row_swap(root_mine, 2)
    total, forward = call(
        functools.partial(leaf_transposed_kernel, (quarter, half)),
        (kept(columns, quarter, F32), stored(quarter + half, columns)),
        [VMEM] * 9,
        [pltpu.VMEM((front, columns), BF), pltpu.VMEM((quarter, columns), BF)],
        16 * MIB,
        2 * front * quarter * columns,
        2 * front * quarter,
    )(leaf_forward, rows_x, rows_y, rows_d, d_v, mask, root_rows, panel_rows, root_piece)
    near = after(near, total)
    near_other = leaf_swap(near)
    far_other = leaf_swap(far)
    total = call(
        functools.partial(own_kernel, (quarter, half)),
        kept(columns, quarter, F32),
        [VMEM] * 4,
        [pltpu.VMEM((quarter, columns), BF)],
        16 * MIB,
        0,
        0,
    )(near, far, total, panel_rows)
    backward = call(
        functools.partial(last_kernel, (quarter, half)),
        stored(quarter + half, columns),
        [VMEM] * 5,
        [pltpu.VMEM((quarter, columns), BF)],
        16 * MIB,
        front * quarter * columns,
        front * quarter,
    )(near_other, far_other, total, panel_rows, root_rows)
    return forward, backward


def on_device(rhs, pivot_inverse, panel, live, parent_map):
    if lax.axis_size("leaf") == 2 and lax.axis_size("row") == 4:
        return two_levels(rhs, pivot_inverse, panel, live, parent_map)
    return deep_tree(rhs, pivot_inverse, panel, live, parent_map)


def solution(mesh):
    in_specs = (P(("leaf", "row"), "col"), P("leaf", "row"), P("leaf", "row"), P(), P())
    out_specs = (P(("leaf", "row"), "col"), P(("leaf", "row"), "col"))
    return jax.shard_map(
        on_device, mesh=mesh, in_specs=in_specs, out_specs=out_specs, check_vma=False
    )
```

```python
import functools

import jax
import jax.numpy as jnp
from jax import lax
from jax.experimental import pallas as pl
from jax.experimental.pallas import tpu as pltpu
from jax.sharding import PartitionSpec as P

F = 2560
E = 1536


def from_partner(block, axis, apart):
    count = lax.axis_size(axis)
    route = []
    for low in range(count):
        high = low | 1 << apart
        if high != low and high < count:
            route += [(low, high), (high, low)]
    return lax.ppermute(block, axis, route)


def doubling(stacked, bit_count, leaf_pos, swapper):
    for bit_no in range(bit_count):
        partner = swapper(stacked, bit_no)
        upper_half = jnp.right_shift(leaf_pos, bit_no) % 2 == 1
        stacked = jnp.where(
            upper_half,
            jnp.concatenate([partner, stacked], 0),
            jnp.concatenate([stacked, partner], 0),
        )
    return stacked


def halving(partial_value, bit_count, leaf_pos, swapper):
    for bit_no in reversed(range(bit_count)):
        halves = partial_value.reshape((2, partial_value.shape[0] // 2) + partial_value.shape[1:])
        upper_half = jnp.right_shift(leaf_pos, bit_no) % 2 == 1
        kept_half = jnp.where(upper_half, halves[1], halves[0])
        sent_half = jnp.where(upper_half, halves[0], halves[1])
        partial_value = kept_half + swapper(sent_half, bit_no)
    return partial_value[0]


def to_front(group_block, row_count):
    count_g, total_rows, row_width = group_block.shape
    piece_rows = total_rows // row_count
    return (
        group_block.reshape(count_g, row_count, piece_rows, row_width)
        .transpose(1, 0, 2, 3)
        .reshape(count_g * total_rows, row_width)
    )


def block_onehot(mapping):
    return (jnp.arange(F // 128, dtype=jnp.int32)[:, None] == mapping[None, :]).astype(jnp.bfloat16)


def pivot_sum(diag_block, quarter_rows):
    return lax.psum_scatter(
        jnp.dot(diag_block, quarter_rows, preferred_element_type=jnp.float32).astype(jnp.bfloat16),
        "row",
        scatter_dimension=0,
        tiled=True,
    ).astype(jnp.float32)


def quarter_swap(values, bit_no):
    return from_partner(values, "leaf", bit_no)


def update_swap(values, bit_no):
    return from_partner(values, "leaf", bit_no)


def parent_swap(values, bit_no):
    return from_partner(values, "leaf", bit_no)


def reduce_swap(values, bit_no):
    return from_partner(values.astype(jnp.bfloat16), "leaf", bit_no).astype(values.dtype)


def deep_tree(rhs, pivot_inverse, panel, live, parent_map):
    leaves = lax.axis_size("leaf")
    row_count = lax.axis_size("row")
    tree_depth = leaves.bit_length() - 1
    leaf_pos = lax.axis_index("leaf")
    row_pos = lax.axis_index("row")
    columns = rhs.shape[1]
    quarter = F // row_count
    parent_blocks = F // 128
    child_blocks = E // 128
    layout = []
    vec_off, piv_off, pan_off, front_base = (0, 0, 0, 0)
    for level_no in range(tree_depth + 1):
        groups = 2**level_no
        layout.append((groups, vec_off, piv_off, pan_off, front_base))
        vec_off += F // (row_count * groups)
        piv_off += F // groups
        pan_off += E // groups
        front_base += leaves // groups
    forward_parts = []
    live_masks = []
    incoming = None
    for level_no in range(tree_depth + 1):
        groups, vec_off, piv_off, pan_off, front_base = layout[level_no]
        piece_rows = F // (row_count * groups)
        panel_rows = E // (row_count * groups)
        inner_pos = leaf_pos % groups
        front_no = jnp.right_shift(leaf_pos, level_no)
        live_rows = lax.dynamic_index_in_dim(live, front_base + front_no, 0, keepdims=False) * 128
        first_row = (row_pos * groups + inner_pos) * piece_rows
        live_mask = (first_row + jnp.arange(piece_rows, dtype=jnp.int32) < live_rows)[:, None]
        live_masks.append(live_mask)
        right_side = rhs[vec_off : vec_off + piece_rows]
        if incoming is not None:
            right_side = (right_side.astype(jnp.float32) - incoming).astype(jnp.bfloat16)
        masked = jnp.where(live_mask, right_side, jnp.zeros_like(right_side))
        quarter_rows = doubling(masked[None], level_no, leaf_pos, quarter_swap).reshape(
            quarter, columns
        )
        diag_block = pivot_inverse[piv_off : piv_off + F // groups]
        if level_no < tree_depth:
            off_block = panel[pan_off : pan_off + E // groups]
            forward_value = pivot_sum(diag_block, quarter_rows)
            update_rows = lax.psum(
                jnp.dot(off_block, quarter_rows, preferred_element_type=jnp.float32), "row"
            ).astype(jnp.bfloat16)
        else:
            forward_value = pivot_sum(diag_block, quarter_rows)
        forward_parts.append(jnp.where(live_mask, forward_value, 0.0).astype(jnp.bfloat16))
        if level_no < tree_depth:
            gathered = doubling(update_rows[None], level_no + 1, leaf_pos, update_swap)
            parent_front = jnp.right_shift(leaf_pos, level_no + 1)
            assembled = jnp.zeros((parent_blocks, 128, columns), jnp.float32)
            for side_no in range(2):
                child_update = to_front(
                    gathered[side_no * groups : (side_no + 1) * groups], row_count
                )
                mapping = lax.dynamic_index_in_dim(
                    parent_map, front_base + 2 * parent_front + side_no, 0, keepdims=False
                )
                assembled = assembled + jnp.einsum(
                    "ke,eab->kab",
                    block_onehot(mapping),
                    child_update.reshape(child_blocks, 128, columns),
                    preferred_element_type=jnp.float32,
                )
            parent_groups = 2 * groups
            parent_rows = F // (row_count * parent_groups)
            parent_first = (row_pos * parent_groups + leaf_pos % parent_groups) * parent_rows
            incoming = lax.dynamic_slice_in_dim(
                assembled.reshape(F, columns), parent_first, parent_rows, 0
            )
    backward_parts = [None] * (tree_depth + 1)
    parent_value = None
    for level_no in reversed(range(tree_depth + 1)):
        groups, vec_off, piv_off, pan_off, front_base = layout[level_no]
        piece_rows = F // (row_count * groups)
        panel_rows = E // (row_count * groups)
        inner_pos = leaf_pos % groups
        front_no = jnp.right_shift(leaf_pos, level_no)
        diag_block = pivot_inverse[piv_off : piv_off + F // groups]
        own_piece = forward_parts[level_no]
        if level_no == tree_depth:
            own_rows = lax.all_gather(own_piece, "row", axis=0, tiled=True)
            partial_value = jnp.einsum(
                "ik,ia->ka", diag_block, own_rows, preferred_element_type=jnp.float32
            )
        else:
            own_rows, parent_gathered = (
                lax.all_gather(own_piece, "row", axis=0, tiled=True),
                lax.all_gather(parent_value, "row", axis=0, tiled=True),
            )
            whole_parent = doubling(parent_gathered[None], level_no + 1, leaf_pos, parent_swap)
            parent_full = to_front(whole_parent, row_count)
            mapping = lax.dynamic_index_in_dim(parent_map, front_base + front_no, 0, keepdims=False)
            taken_rows = jnp.einsum(
                "ke,kab->eab",
                block_onehot(mapping),
                parent_full.reshape(parent_blocks, 128, columns),
                preferred_element_type=jnp.float32,
            ).astype(jnp.bfloat16)
            taken_rows = lax.dynamic_index_in_dim(
                taken_rows.reshape(row_count, groups, panel_rows, columns),
                inner_pos,
                1,
                keepdims=False,
            ).reshape(row_count * panel_rows, columns)
            off_block = panel[pan_off : pan_off + E // groups]
            partial_value = jnp.einsum(
                "ik,ia->ka", diag_block, own_rows, preferred_element_type=jnp.float32
            ) - jnp.einsum("ik,ia->ka", off_block, taken_rows, preferred_element_type=jnp.float32)
        if level_no == 0:
            reduced = partial_value
        else:
            reduced = halving(
                partial_value.reshape(groups, piece_rows, columns), level_no, leaf_pos, reduce_swap
            )
        parent_value = jnp.where(live_masks[level_no], reduced, 0.0).astype(jnp.bfloat16)
        backward_parts[level_no] = parent_value
    return (jnp.concatenate(forward_parts, 0), jnp.concatenate(backward_parts, 0))


B = 128
VMEM = pl.BlockSpec(memory_space=pltpu.VMEM)
ANY = pl.BlockSpec(memory_space=pl.ANY)
BF = jnp.bfloat16
F32 = jnp.float32
MIB = 1024 * 1024


def stored(rows, columns, dtype=BF):
    return jax.ShapeDtypeStruct((rows, columns), dtype)


def kept(rows, columns, dtype=BF):
    return pltpu.VMEM((rows, columns), dtype)


def call(body, out_shape, in_specs, scratch, limit, flops, bytes_moved):
    return pl.pallas_call(
        body,
        out_shape=out_shape,
        in_specs=in_specs,
        out_specs=jax.tree.map(lambda _: VMEM, out_shape, is_leaf=lambda s: hasattr(s, "shape")),
        scratch_shapes=scratch,
        compiler_params=pltpu.CompilerParams(vmem_limit_bytes=limit),
        cost_estimate=pl.CostEstimate(flops=flops, bytes_accessed=bytes_moved, transcendentals=0),
    )


def rows_at(start, size):
    return pl.ds(pl.multiple_of(start, 16), size)


def mm(left, right):
    return jnp.dot(left, right, preferred_element_type=F32)


def row_order(row_pos, leaf_pos):
    return (row_pos, row_pos ^ (1 + leaf_pos), row_pos ^ (2 - leaf_pos), row_pos ^ 3)


def panel_kernel(
    sizes,
    live,
    pmap,
    rhs,
    panel,
    pivot,
    send_near,
    send_rest,
    keep_near,
    keep_rest,
    b_v,
    masked,
    mask,
    w_v,
    d_v,
    c_v,
    live_s,
    pmap_s,
    sems,
):
    quarter, half, parts, update_rows = sizes
    leaf_pos = lax.axis_index("leaf")
    row_pos = lax.axis_index("row")
    gets = [
        pltpu.make_async_copy(live, live_s, sems.at[0]),
        pltpu.make_async_copy(rhs, b_v, sems.at[1]),
        pltpu.make_async_copy(pmap, pmap_s, sems.at[2]),
    ]
    step = update_rows // parts
    for i in range(parts):
        rows = pl.ds(i * step, step)
        gets.append(pltpu.make_async_copy(panel.at[rows], w_v.at[rows], sems.at[3 + i]))
    get = pltpu.make_async_copy(pivot.at[pl.ds(0, 4 * quarter)], d_v, sems.at[3 + parts])
    gets.append(get)
    for get in gets:
        get.start()
    c_v[...] = jnp.zeros_like(c_v)
    gets[0].wait()
    gets[1].wait()
    value = b_v[pl.ds(0, quarter)]
    row = row_pos * quarter + lax.broadcasted_iota(jnp.int32, value.shape, 0)
    alive = row < live_s[leaf_pos] * B
    mask[...] = jnp.where(alive, 1.0, 0.0).astype(BF)
    masked[...] = jnp.where(alive, value, jnp.zeros_like(value))
    right = masked[...]
    gets[2].wait()
    for i in range(parts):
        gets[3 + i].wait()
        product = mm(w_v[pl.ds(i * step, step)], right).astype(BF)
        for e in range(step // B):
            block = pmap_s[leaf_pos, i * (step // B) + e]
            c_v[pl.ds(pl.multiple_of(block * B, B), B)] = product[e * B : (e + 1) * B]
    for near_out, rest, side in (
        (send_near, send_rest, 1 - leaf_pos),
        (keep_near, keep_rest, leaf_pos),
    ):
        near = (row_pos ^ (1 + side)) * quarter
        mine, other = side * half, (1 - side) * half
        near_out[pl.ds(0, half)] = c_v[rows_at(near + mine, half)]
        near_out[pl.ds(half, half)] = c_v[rows_at(near + other, half)]
        rest[pl.ds(0, half)] = c_v[rows_at((row_pos ^ 3) * quarter + mine, half)]
        rest[pl.ds(half, half)] = c_v[rows_at(row_pos * quarter + mine, half)]
    gets[3 + parts].wait()


def leaf_pivot_kernel(sizes, masked, d_v, pivot, after, *outs_and_scratch):
    quarter, rows = sizes
    *outs, root_d, sem = outs_and_scratch
    get = pltpu.make_async_copy(pivot.at[pl.ds(4 * quarter, rows)], root_d, sem)
    get.start()
    order = row_order(lax.axis_index("row"), lax.axis_index("leaf"))
    right = masked[...]
    for k in (3, 1, 2, 0):
        product = mm(d_v[rows_at(order[k] * quarter, quarter)], right)
        outs[k][...] = product.astype(BF)
    get.wait()


def scatter_kernel(sizes, live, pmap, w_v, after, out, live_s, pmap_s, sems):
    quarter, update_rows = sizes
    leaf_pos = lax.axis_index("leaf")
    row_pos = lax.axis_index("row")
    gets = [
        pltpu.make_async_copy(live, live_s, sems.at[0]),
        pltpu.make_async_copy(pmap, pmap_s, sems.at[1]),
    ]
    for get in gets:
        get.start()
    per_row = quarter // B
    out[...] = jnp.zeros_like(out)
    for get in gets:
        get.wait()
    column = row_pos * quarter + lax.broadcasted_iota(jnp.int32, (B, quarter), 1)
    alive = column < live_s[leaf_pos] * B
    for e in range(update_rows // B):
        value = w_v[pl.ds(e * B, B)]
        block = pmap_s[leaf_pos, e]
        away = (block // per_row) ^ row_pos
        slot = jnp.where(away == 1 + leaf_pos, 1, jnp.where(away == 2 - leaf_pos, 2, away))
        at = (slot * per_row + block % per_row) * B
        out[pl.ds(pl.multiple_of(at, B), B)] = jnp.where(alive, value, jnp.zeros_like(value))


def root_pivot_kernel(sizes, mine, yours, other_mine, other_yours, d_v, out, q_v):
    half = sizes
    leaf_pos = lax.axis_index("leaf")
    for own, other, at in ((mine, other_yours, leaf_pos), (yours, other_mine, 1 - leaf_pos)):
        value = own[...].astype(F32) + other[...].astype(F32)
        q_v[rows_at(at * half, half)] = (-value).astype(BF)
    out[...] = mm(d_v[pl.ds(0, 4 * half)], q_v[...]).astype(BF)


def root_transposed_kernel(sizes, y, d_v, out, piece, s_v):
    half = sizes
    leaf_pos = lax.axis_index("leaf")
    row_pos = lax.axis_index("row")
    piece[...] = y[rows_at(row_pos * half, half)]
    s_v[...] = mm(y[...].T, d_v[pl.ds(0, 4 * half)]).T
    out[pl.ds(0, half)] = s_v[rows_at(leaf_pos * half, half)].astype(BF)
    out[pl.ds(half, half)] = s_v[rows_at((1 - leaf_pos) * half, half)].astype(BF)


def put(target, slot, half, source, order):
    for k, side in enumerate(order):
        at = 2 * slot * half + side * half
        target[rows_at(at, half)] = source[pl.ds(k * half, half)]


def leaf_transposed_kernel(
    sizes,
    own,
    rows_y,
    rows_x,
    rows_d,
    d_v,
    mask,
    root_rows,
    panel_rows,
    root_piece,
    total,
    forward,
    y_v,
    s_v,
):
    quarter, half = sizes
    row_pos = lax.axis_index("row")
    leaf_pos = lax.axis_index("leaf")
    order = row_order(row_pos, leaf_pos)
    forward[pl.ds(0, quarter)] = own[...]
    forward[pl.ds(quarter, half)] = root_piece[...]
    for k, part in enumerate((own, rows_x, rows_y, rows_d)):
        y_v[rows_at(order[k] * quarter, quarter)] = part[...]
    value = mm(y_v[...].T, d_v[pl.ds(0, 4 * quarter)])
    value = jnp.where(mask[...].astype(F32).T > 0.0, value, 0.0)
    put(s_v, 0, half, root_rows, (leaf_pos, 1 - leaf_pos))
    total[...] = value - mm(s_v[...].T, panel_rows[pl.ds(0, quarter)])


def own_kernel(sizes, near, far, total, panel_rows, out, s_v):
    quarter, half = sizes
    leaf_pos = lax.axis_index("leaf")
    put(s_v, 0, half, near, (leaf_pos, 1 - leaf_pos))
    value = total[...] - mm(s_v[...].T, panel_rows[pl.ds(2 * quarter, quarter)])
    rows = rows_at(3 * quarter + leaf_pos * half, half)
    out[...] = value - mm(far[...].T, panel_rows[rows])


def last_kernel(sizes, near, far, total, panel_rows, root_rows, out, s_v):
    quarter, half = sizes
    leaf_pos = lax.axis_index("leaf")
    put(s_v, 0, half, near, (1 - leaf_pos, leaf_pos))
    value = total[...] - mm(s_v[...].T, panel_rows[pl.ds(quarter, quarter)])
    rows = rows_at(3 * quarter + (1 - leaf_pos) * half, half)
    value = value - mm(far[...].T, panel_rows[rows])
    out[pl.ds(0, quarter)] = value.T.astype(BF)
    out[pl.ds(quarter, half)] = root_rows[pl.ds(0, half)]


def leaf_swap(value):
    return lax.ppermute(value, "leaf", [(0, 1), (1, 0)])


def row_swap(value, phase):
    route = []
    for leaf in range(2):
        apart = (1 + leaf, 2 - leaf, 3)[phase]
        route += [(4 * leaf + r, 4 * leaf + (r ^ apart)) for r in range(4)]
    return lax.ppermute(value, ("leaf", "row"), route)


def added(left, right):
    return left.astype(F32) + right.astype(F32)


def two_levels(rhs, pivot_inverse, panel, live, parent_map):
    columns = rhs.shape[1]
    quarter = pivot_inverse.shape[1]
    half = quarter // 2
    front = 4 * quarter
    updates = parent_map.shape[1] * B
    after = lambda value, other: lax.optimization_barrier((value, other))[0]
    smem = [pltpu.SMEM(live.shape, jnp.int32), pltpu.SMEM(parent_map.shape, jnp.int32)]

    parts = 4 if updates % (4 * B) == 0 else 1
    send_near, send_rest, keep_near, keep_rest, b_v, masked, mask, w_v, d_v = call(
        functools.partial(panel_kernel, (quarter, half, parts, updates)),
        (
            kept(quarter, columns),
            kept(quarter, columns),
            kept(quarter, columns),
            kept(quarter, columns),
            kept(quarter + half, columns),
            kept(quarter, columns),
            kept(quarter, columns),
            kept(updates, quarter),
            kept(front, quarter),
        ),
        [ANY] * 5,
        [pltpu.VMEM((front, columns), BF), *smem, pltpu.SemaphoreType.DMA((4 + parts,))],
        58_700_000,
        2 * updates * quarter * columns,
        2 * updates * quarter,
    )(live, parent_map, rhs, panel, pivot_inverse)
    away_near = added(keep_near, leaf_swap(send_near)).astype(BF)
    rest = added(keep_rest, leaf_swap(send_rest))
    away_far = rest[:half].astype(BF)
    from_far = row_swap(away_far, 2)
    from_near = row_swap(away_near, 0)

    *pieces, root_d = call(
        functools.partial(leaf_pivot_kernel, (quarter, 4 * half)),
        (*(kept(quarter, columns),) * 4, kept(4 * half, quarter)),
        [VMEM, VMEM, ANY, ANY],
        [pltpu.SemaphoreType.DMA],
        49_500_000,
        2 * front * quarter * columns,
        2 * front * quarter,
    )(masked, d_v, pivot_inverse, away_near)
    from_near = after(from_near, pieces[0])
    leaf_forward = pieces[0].astype(F32)
    for phase in (2, 0, 1):
        leaf_forward = leaf_forward + row_swap(pieces[1 + phase], phase).astype(F32)
    leaf_forward = jnp.where(mask > 0, leaf_forward, 0.0).astype(BF)
    rows_y = row_swap(leaf_forward, 1)
    rows_x = row_swap(leaf_forward, 0)
    rows_d = row_swap(rows_y, 0)

    term = rest[half:] + from_far.astype(F32) - b_v[quarter:].astype(F32)
    from_near = from_near.astype(F32)
    negated_mine = (from_near[:half] + term).astype(BF)
    negated_yours = from_near[half:].astype(BF)
    other_yours = leaf_swap(negated_yours)
    other_mine = leaf_swap(negated_mine)

    partial = call(
        functools.partial(root_pivot_kernel, half),
        kept(4 * half, columns),
        [VMEM] * 5,
        [pltpu.VMEM((quarter, columns), BF)],
        16 * MIB,
        0,
        0,
    )(negated_mine, negated_yours, other_mine, other_yours, root_d)
    panel_rows = call(
        functools.partial(scatter_kernel, (quarter, updates)),
        kept(front, quarter),
        [ANY, ANY, VMEM, ANY],
        [*smem, pltpu.SemaphoreType.DMA((2,))],
        16 * MIB,
        2000000000,
        4 * front * quarter,
    )(live, parent_map, w_v, after(rows_y, rows_x))
    partial = added(partial, row_swap(partial, 1))
    got = after(row_swap(partial.astype(BF), 0), panel_rows)
    root_forward = (partial + got.astype(F32)).astype(BF)

    part, root_piece = call(
        functools.partial(root_transposed_kernel, half),
        (kept(quarter, columns), kept(half, columns)),
        [VMEM, VMEM],
        [pltpu.VMEM((quarter, columns), F32)],
        16 * MIB,
        0,
        0,
    )(root_forward, root_d)
    got = after(leaf_swap(part), rows_d)
    root_mine = added(part[:half], got[half:]).astype(BF)
    root_other = added(part[half:], got[:half]).astype(BF)
    root_rows = jnp.concatenate([root_mine, root_other], 0)

    near = row_swap(root_rows, 1)
    far = row_swap(root_mine, 2)
    total, forward = call(
        functools.partial(leaf_transposed_kernel, (quarter, half)),
        (kept(columns, quarter, F32), stored(quarter + half, columns)),
        [VMEM] * 9,
        [pltpu.VMEM((front, columns), BF), pltpu.VMEM((quarter, columns), BF)],
        16 * MIB,
        2 * front * quarter * columns,
        2 * front * quarter,
    )(leaf_forward, rows_y, rows_x, rows_d, d_v, mask, root_rows, panel_rows, root_piece)
    near = after(near, total)
    near_other = leaf_swap(near)
    far_other = leaf_swap(far)
    total = call(
        functools.partial(own_kernel, (quarter, half)),
        kept(columns, quarter, F32),
        [VMEM] * 4,
        [pltpu.VMEM((quarter, columns), BF)],
        16 * MIB,
        0,
        0,
    )(near, far, total, panel_rows)
    backward = call(
        functools.partial(last_kernel, (quarter, half)),
        stored(quarter + half, columns),
        [VMEM] * 5,
        [pltpu.VMEM((quarter, columns), BF)],
        16 * MIB,
        front * quarter * columns,
        front * quarter,
    )(near_other, far_other, total, panel_rows, root_rows)
    return forward, backward


def on_device(rhs, pivot_inverse, panel, live, parent_map):
    if lax.axis_size("leaf") == 2 and lax.axis_size("row") == 4:
        return two_levels(rhs, pivot_inverse, panel, live, parent_map)
    return deep_tree(rhs, pivot_inverse, panel, live, parent_map)


def solution(mesh):
    in_specs = (P(("leaf", "row"), "col"), P("leaf", "row"), P("leaf", "row"), P(), P())
    out_specs = (P(("leaf", "row"), "col"), P(("leaf", "row"), "col"))
    return jax.shard_map(
        on_device, mesh=mesh, in_specs=in_specs, out_specs=out_specs, check_vma=False
    )
```

```python
import functools

import jax
import jax.numpy as jnp
from jax import lax
from jax.experimental import pallas as pl
from jax.experimental.pallas import tpu as pltpu
from jax.sharding import PartitionSpec as P

F = 2560
E = 1536


def from_partner(block, axis, apart):
    count = lax.axis_size(axis)
    route = []
    for low in range(count):
        high = low | 1 << apart
        if high != low and high < count:
            route += [(low, high), (high, low)]
    return lax.ppermute(block, axis, route)


def doubling(stacked, bit_count, leaf_pos, swapper):
    for bit_no in range(bit_count):
        partner = swapper(stacked, bit_no)
        upper_half = jnp.right_shift(leaf_pos, bit_no) % 2 == 1
        stacked = jnp.where(
            upper_half,
            jnp.concatenate([partner, stacked], 0),
            jnp.concatenate([stacked, partner], 0),
        )
    return stacked


def halving(partial_value, bit_count, leaf_pos, swapper):
    for bit_no in reversed(range(bit_count)):
        halves = partial_value.reshape((2, partial_value.shape[0] // 2) + partial_value.shape[1:])
        upper_half = jnp.right_shift(leaf_pos, bit_no) % 2 == 1
        kept_half = jnp.where(upper_half, halves[1], halves[0])
        sent_half = jnp.where(upper_half, halves[0], halves[1])
        partial_value = kept_half + swapper(sent_half, bit_no)
    return partial_value[0]


def to_front(group_block, row_count):
    count_g, total_rows, row_width = group_block.shape
    piece_rows = total_rows // row_count
    return (
        group_block.reshape(count_g, row_count, piece_rows, row_width)
        .transpose(1, 0, 2, 3)
        .reshape(count_g * total_rows, row_width)
    )


def block_onehot(mapping):
    return (jnp.arange(F // 128, dtype=jnp.int32)[:, None] == mapping[None, :]).astype(jnp.bfloat16)


def pivot_sum(diag_block, quarter_rows):
    return lax.psum_scatter(
        jnp.dot(diag_block, quarter_rows, preferred_element_type=jnp.float32).astype(jnp.bfloat16),
        "row",
        scatter_dimension=0,
        tiled=True,
    ).astype(jnp.float32)


def quarter_swap(values, bit_no):
    return from_partner(values, "leaf", bit_no)


def update_swap(values, bit_no):
    return from_partner(values, "leaf", bit_no)


def parent_swap(values, bit_no):
    return from_partner(values, "leaf", bit_no)


def reduce_swap(values, bit_no):
    return from_partner(values.astype(jnp.bfloat16), "leaf", bit_no).astype(values.dtype)


def deep_tree(rhs, pivot_inverse, panel, live, parent_map):
    leaves = lax.axis_size("leaf")
    row_count = lax.axis_size("row")
    tree_depth = leaves.bit_length() - 1
    leaf_pos = lax.axis_index("leaf")
    row_pos = lax.axis_index("row")
    columns = rhs.shape[1]
    quarter = F // row_count
    parent_blocks = F // 128
    child_blocks = E // 128
    layout = []
    vec_off, piv_off, pan_off, front_base = (0, 0, 0, 0)
    for level_no in range(tree_depth + 1):
        groups = 2**level_no
        layout.append((groups, vec_off, piv_off, pan_off, front_base))
        vec_off += F // (row_count * groups)
        piv_off += F // groups
        pan_off += E // groups
        front_base += leaves // groups
    forward_parts = []
    live_masks = []
    incoming = None
    for level_no in range(tree_depth + 1):
        groups, vec_off, piv_off, pan_off, front_base = layout[level_no]
        piece_rows = F // (row_count * groups)
        panel_rows = E // (row_count * groups)
        inner_pos = leaf_pos % groups
        front_no = jnp.right_shift(leaf_pos, level_no)
        live_rows = lax.dynamic_index_in_dim(live, front_base + front_no, 0, keepdims=False) * 128
        first_row = (row_pos * groups + inner_pos) * piece_rows
        live_mask = (first_row + jnp.arange(piece_rows, dtype=jnp.int32) < live_rows)[:, None]
        live_masks.append(live_mask)
        right_side = rhs[vec_off : vec_off + piece_rows]
        if incoming is not None:
            right_side = (right_side.astype(jnp.float32) - incoming).astype(jnp.bfloat16)
        masked = jnp.where(live_mask, right_side, jnp.zeros_like(right_side))
        quarter_rows = doubling(masked[None], level_no, leaf_pos, quarter_swap).reshape(
            quarter, columns
        )
        diag_block = pivot_inverse[piv_off : piv_off + F // groups]
        if level_no < tree_depth:
            off_block = panel[pan_off : pan_off + E // groups]
            forward_value = pivot_sum(diag_block, quarter_rows)
            update_rows = lax.psum(
                jnp.dot(off_block, quarter_rows, preferred_element_type=jnp.float32), "row"
            ).astype(jnp.bfloat16)
        else:
            forward_value = pivot_sum(diag_block, quarter_rows)
        forward_parts.append(jnp.where(live_mask, forward_value, 0.0).astype(jnp.bfloat16))
        if level_no < tree_depth:
            gathered = doubling(update_rows[None], level_no + 1, leaf_pos, update_swap)
            parent_front = jnp.right_shift(leaf_pos, level_no + 1)
            assembled = jnp.zeros((parent_blocks, 128, columns), jnp.float32)
            for side_no in range(2):
                child_update = to_front(
                    gathered[side_no * groups : (side_no + 1) * groups], row_count
                )
                mapping = lax.dynamic_index_in_dim(
                    parent_map, front_base + 2 * parent_front + side_no, 0, keepdims=False
                )
                assembled = assembled + jnp.einsum(
                    "ke,eab->kab",
                    block_onehot(mapping),
                    child_update.reshape(child_blocks, 128, columns),
                    preferred_element_type=jnp.float32,
                )
            parent_groups = 2 * groups
            parent_rows = F // (row_count * parent_groups)
            parent_first = (row_pos * parent_groups + leaf_pos % parent_groups) * parent_rows
            incoming = lax.dynamic_slice_in_dim(
                assembled.reshape(F, columns), parent_first, parent_rows, 0
            )
    backward_parts = [None] * (tree_depth + 1)
    parent_value = None
    for level_no in reversed(range(tree_depth + 1)):
        groups, vec_off, piv_off, pan_off, front_base = layout[level_no]
        piece_rows = F // (row_count * groups)
        panel_rows = E // (row_count * groups)
        inner_pos = leaf_pos % groups
        front_no = jnp.right_shift(leaf_pos, level_no)
        diag_block = pivot_inverse[piv_off : piv_off + F // groups]
        own_piece = forward_parts[level_no]
        if level_no == tree_depth:
            own_rows = lax.all_gather(own_piece, "row", axis=0, tiled=True)
            partial_value = jnp.einsum(
                "ik,ia->ka", diag_block, own_rows, preferred_element_type=jnp.float32
            )
        else:
            own_rows, parent_gathered = (
                lax.all_gather(own_piece, "row", axis=0, tiled=True),
                lax.all_gather(parent_value, "row", axis=0, tiled=True),
            )
            whole_parent = doubling(parent_gathered[None], level_no + 1, leaf_pos, parent_swap)
            parent_full = to_front(whole_parent, row_count)
            mapping = lax.dynamic_index_in_dim(parent_map, front_base + front_no, 0, keepdims=False)
            taken_rows = jnp.einsum(
                "ke,kab->eab",
                block_onehot(mapping),
                parent_full.reshape(parent_blocks, 128, columns),
                preferred_element_type=jnp.float32,
            ).astype(jnp.bfloat16)
            taken_rows = lax.dynamic_index_in_dim(
                taken_rows.reshape(row_count, groups, panel_rows, columns),
                inner_pos,
                1,
                keepdims=False,
            ).reshape(row_count * panel_rows, columns)
            off_block = panel[pan_off : pan_off + E // groups]
            partial_value = jnp.einsum(
                "ik,ia->ka", diag_block, own_rows, preferred_element_type=jnp.float32
            ) - jnp.einsum("ik,ia->ka", off_block, taken_rows, preferred_element_type=jnp.float32)
        if level_no == 0:
            reduced = partial_value
        else:
            reduced = halving(
                partial_value.reshape(groups, piece_rows, columns), level_no, leaf_pos, reduce_swap
            )
        parent_value = jnp.where(live_masks[level_no], reduced, 0.0).astype(jnp.bfloat16)
        backward_parts[level_no] = parent_value
    return (jnp.concatenate(forward_parts, 0), jnp.concatenate(backward_parts, 0))


B = 128
VMEM = pl.BlockSpec(memory_space=pltpu.VMEM)
ANY = pl.BlockSpec(memory_space=pl.ANY)
BF = jnp.bfloat16
F32 = jnp.float32
MIB = 1024 * 1024


def stored(rows, columns, dtype=BF):
    return jax.ShapeDtypeStruct((rows, columns), dtype)


def kept(rows, columns, dtype=BF):
    return pltpu.VMEM((rows, columns), dtype)


def call(body, out_shape, in_specs, scratch, limit, flops, bytes_moved):
    return pl.pallas_call(
        body,
        out_shape=out_shape,
        in_specs=in_specs,
        out_specs=jax.tree.map(lambda _: VMEM, out_shape, is_leaf=lambda s: hasattr(s, "shape")),
        scratch_shapes=scratch,
        compiler_params=pltpu.CompilerParams(vmem_limit_bytes=limit),
        cost_estimate=pl.CostEstimate(flops=flops, bytes_accessed=bytes_moved, transcendentals=0),
    )


def rows_at(start, size):
    return pl.ds(pl.multiple_of(start, 16), size)


def mm(left, right):
    return jnp.dot(left, right, preferred_element_type=F32)


def row_order(row_pos, leaf_pos):
    return (row_pos, row_pos ^ (1 + leaf_pos), row_pos ^ (2 - leaf_pos), row_pos ^ 3)


def panel_kernel(
    sizes,
    live,
    pmap,
    rhs,
    panel,
    pivot,
    send_near,
    send_rest,
    keep_near,
    keep_rest,
    b_v,
    masked,
    mask,
    w_v,
    d_v,
    c_v,
    live_s,
    pmap_s,
    sems,
):
    quarter, half, parts, update_rows = sizes
    leaf_pos = lax.axis_index("leaf")
    row_pos = lax.axis_index("row")
    gets = [
        pltpu.make_async_copy(live, live_s, sems.at[0]),
        pltpu.make_async_copy(rhs, b_v, sems.at[1]),
        pltpu.make_async_copy(pmap, pmap_s, sems.at[2]),
    ]
    step = update_rows // parts
    for i in range(parts):
        rows = pl.ds(i * step, step)
        gets.append(pltpu.make_async_copy(panel.at[rows], w_v.at[rows], sems.at[3 + i]))
    get = pltpu.make_async_copy(pivot.at[pl.ds(0, 4 * quarter)], d_v, sems.at[3 + parts])
    gets.append(get)
    for get in gets:
        get.start()
    c_v[...] = jnp.zeros_like(c_v)
    gets[0].wait()
    gets[1].wait()
    value = b_v[pl.ds(0, quarter)]
    row = row_pos * quarter + lax.broadcasted_iota(jnp.int32, value.shape, 0)
    alive = row < live_s[leaf_pos] * B
    mask[...] = jnp.where(alive, 1.0, 0.0).astype(BF)
    masked[...] = jnp.where(alive, value, jnp.zeros_like(value))
    right = masked[...]
    gets[2].wait()
    for i in range(parts):
        gets[3 + i].wait()
        product = mm(w_v[pl.ds(i * step, step)], right).astype(BF)
        for e in range(step // B):
            block = pmap_s[leaf_pos, i * (step // B) + e]
            c_v[pl.ds(pl.multiple_of(block * B, B), B)] = product[e * B : (e + 1) * B]
    for near_out, rest, side in (
        (send_near, send_rest, 1 - leaf_pos),
        (keep_near, keep_rest, leaf_pos),
    ):
        near = (row_pos ^ (1 + side)) * quarter
        mine, other = side * half, (1 - side) * half
        near_out[pl.ds(0, half)] = c_v[rows_at(near + mine, half)]
        near_out[pl.ds(half, half)] = c_v[rows_at(near + other, half)]
        rest[pl.ds(0, half)] = c_v[rows_at((row_pos ^ 3) * quarter + mine, half)]
        rest[pl.ds(half, half)] = c_v[rows_at(row_pos * quarter + mine, half)]
    gets[3 + parts].wait()


def load_kernel(sizes, pivot, after, root_d, sems):
    first, rows = sizes
    step = rows // 4
    gets = [
        pltpu.make_async_copy(
            pivot.at[pl.ds(first + i * step, step)], root_d.at[pl.ds(i * step, step)], sems.at[i]
        )
        for i in range(4)
    ]
    for get in gets:
        get.start()
    for get in gets:
        get.wait()


def leaf_pivot_kernel(sizes, masked, d_v, after, *outs):
    quarter = sizes
    order = row_order(lax.axis_index("row"), lax.axis_index("leaf"))
    right = masked[...]
    for k in (3, 1, 2, 0):
        product = mm(d_v[rows_at(order[k] * quarter, quarter)], right)
        outs[k][...] = product.astype(BF)


def scatter_kernel(sizes, live, pmap, w_v, after, out, live_s, pmap_s, sems):
    quarter, update_rows = sizes
    leaf_pos = lax.axis_index("leaf")
    row_pos = lax.axis_index("row")
    gets = [
        pltpu.make_async_copy(live, live_s, sems.at[0]),
        pltpu.make_async_copy(pmap, pmap_s, sems.at[1]),
    ]
    for get in gets:
        get.start()
    per_row = quarter // B
    out[...] = jnp.zeros_like(out)
    for get in gets:
        get.wait()
    column = row_pos * quarter + lax.broadcasted_iota(jnp.int32, (B, quarter), 1)
    alive = column < live_s[leaf_pos] * B
    for e in range(update_rows // B):
        value = w_v[pl.ds(e * B, B)]
        block = pmap_s[leaf_pos, e]
        away = (block // per_row) ^ row_pos
        slot = jnp.where(away == 1 + leaf_pos, 1, jnp.where(away == 2 - leaf_pos, 2, away))
        at = (slot * per_row + block % per_row) * B
        out[pl.ds(pl.multiple_of(at, B), B)] = jnp.where(alive, value, jnp.zeros_like(value))


def root_pivot_kernel(sizes, mine, yours, other_mine, other_yours, d_v, out, q_v):
    half = sizes
    leaf_pos = lax.axis_index("leaf")
    for own, other, at in ((mine, other_yours, leaf_pos), (yours, other_mine, 1 - leaf_pos)):
        value = own[...].astype(F32) + other[...].astype(F32)
        q_v[rows_at(at * half, half)] = (-value).astype(BF)
    out[...] = mm(d_v[pl.ds(0, 4 * half)], q_v[...]).astype(BF)


def root_transposed_kernel(sizes, y, d_v, out, piece, s_v):
    half = sizes
    leaf_pos = lax.axis_index("leaf")
    row_pos = lax.axis_index("row")
    piece[...] = y[rows_at(row_pos * half, half)]
    s_v[...] = mm(y[...].T, d_v[pl.ds(0, 4 * half)]).T
    out[pl.ds(0, half)] = s_v[rows_at(leaf_pos * half, half)].astype(BF)
    out[pl.ds(half, half)] = s_v[rows_at((1 - leaf_pos) * half, half)].astype(BF)


def put(target, slot, half, source, order):
    for k, side in enumerate(order):
        at = 2 * slot * half + side * half
        target[rows_at(at, half)] = source[pl.ds(k * half, half)]


def leaf_transposed_kernel(
    sizes,
    own,
    rows_y,
    rows_x,
    rows_d,
    d_v,
    mask,
    root_rows,
    panel_rows,
    root_piece,
    total,
    forward,
    y_v,
    s_v,
):
    quarter, half = sizes
    row_pos = lax.axis_index("row")
    leaf_pos = lax.axis_index("leaf")
    order = row_order(row_pos, leaf_pos)
    forward[pl.ds(0, quarter)] = own[...]
    forward[pl.ds(quarter, half)] = root_piece[...]
    for k, part in enumerate((own, rows_x, rows_y, rows_d)):
        y_v[rows_at(order[k] * quarter, quarter)] = part[...]
    value = mm(y_v[...].T, d_v[pl.ds(0, 4 * quarter)])
    value = jnp.where(mask[...].astype(F32).T > 0.0, value, 0.0)
    put(s_v, 0, half, root_rows, (leaf_pos, 1 - leaf_pos))
    total[...] = value - mm(s_v[...].T, panel_rows[pl.ds(0, quarter)])


def own_kernel(sizes, near, far, total, panel_rows, out, s_v):
    quarter, half = sizes
    leaf_pos = lax.axis_index("leaf")
    put(s_v, 0, half, near, (leaf_pos, 1 - leaf_pos))
    value = total[...] - mm(s_v[...].T, panel_rows[pl.ds(2 * quarter, quarter)])
    rows = rows_at(3 * quarter + leaf_pos * half, half)
    out[...] = value - mm(far[...].T, panel_rows[rows])


def last_kernel(sizes, near, far, total, panel_rows, root_rows, out, s_v):
    quarter, half = sizes
    leaf_pos = lax.axis_index("leaf")
    put(s_v, 0, half, near, (1 - leaf_pos, leaf_pos))
    value = total[...] - mm(s_v[...].T, panel_rows[pl.ds(quarter, quarter)])
    rows = rows_at(3 * quarter + (1 - leaf_pos) * half, half)
    value = value - mm(far[...].T, panel_rows[rows])
    out[pl.ds(0, quarter)] = value.T.astype(BF)
    out[pl.ds(quarter, half)] = root_rows[pl.ds(0, half)]


def leaf_swap(value):
    return lax.ppermute(value, "leaf", [(0, 1), (1, 0)])


def row_swap(value, phase):
    route = []
    for leaf in range(2):
        apart = (1 + leaf, 2 - leaf, 3)[phase]
        route += [(4 * leaf + r, 4 * leaf + (r ^ apart)) for r in range(4)]
    return lax.ppermute(value, ("leaf", "row"), route)


def added(left, right):
    return left.astype(F32) + right.astype(F32)


def two_levels(rhs, pivot_inverse, panel, live, parent_map):
    columns = rhs.shape[1]
    quarter = pivot_inverse.shape[1]
    half = quarter // 2
    front = 4 * quarter
    updates = parent_map.shape[1] * B
    after = lambda value, other: lax.optimization_barrier((value, other))[0]
    smem = [pltpu.SMEM(live.shape, jnp.int32), pltpu.SMEM(parent_map.shape, jnp.int32)]

    parts = 4 if updates % (4 * B) == 0 else 1
    send_near, send_rest, keep_near, keep_rest, b_v, masked, mask, w_v, d_v = call(
        functools.partial(panel_kernel, (quarter, half, parts, updates)),
        (
            kept(quarter, columns),
            kept(quarter, columns),
            kept(quarter, columns),
            kept(quarter, columns),
            kept(quarter + half, columns),
            kept(quarter, columns),
            kept(quarter, columns),
            kept(updates, quarter),
            kept(front, quarter),
        ),
        [ANY] * 5,
        [pltpu.VMEM((front, columns), BF), *smem, pltpu.SemaphoreType.DMA((4 + parts,))],
        58_700_000,
        2 * updates * quarter * columns,
        2 * updates * quarter,
    )(live, parent_map, rhs, panel, pivot_inverse)
    away_near = added(keep_near, leaf_swap(send_near)).astype(BF)
    rest = added(keep_rest, leaf_swap(send_rest))
    away_far = rest[:half].astype(BF)
    from_far = row_swap(away_far, 2)
    from_near = row_swap(away_near, 0)

    pieces = call(
        functools.partial(leaf_pivot_kernel, quarter),
        (kept(quarter, columns),) * 4,
        [VMEM, VMEM, ANY],
        [],
        16 * MIB,
        2 * front * quarter * columns,
        2 * front * quarter,
    )(masked, d_v, away_near)
    from_near = after(from_near, pieces[0])
    leaf_forward = pieces[0].astype(F32)
    for phase in (2, 0, 1):
        leaf_forward = leaf_forward + row_swap(pieces[1 + phase], phase).astype(F32)
    leaf_forward = jnp.where(mask > 0, leaf_forward, 0.0).astype(BF)
    rows_y = row_swap(leaf_forward, 1)
    rows_x = row_swap(leaf_forward, 0)
    rows_d = row_swap(rows_y, 0)

    term = rest[half:] + from_far.astype(F32) - b_v[quarter:].astype(F32)
    from_near = from_near.astype(F32)
    negated_mine = (from_near[:half] + term).astype(BF)
    negated_yours = from_near[half:].astype(BF)
    other_yours = leaf_swap(negated_yours)
    other_mine = leaf_swap(negated_mine)

    root_d = call(
        functools.partial(load_kernel, (front, 4 * half)),
        kept(4 * half, quarter),
        [ANY, ANY],
        [pltpu.SemaphoreType.DMA((4,))],
        51_500_000,
        0,
        0,
    )(pivot_inverse, negated_mine)
    partial = call(
        functools.partial(root_pivot_kernel, half),
        kept(4 * half, columns),
        [VMEM] * 5,
        [pltpu.VMEM((quarter, columns), BF)],
        16 * MIB,
        0,
        0,
    )(negated_mine, negated_yours, other_mine, other_yours, root_d)
    panel_rows = call(
        functools.partial(scatter_kernel, (quarter, updates)),
        kept(front, quarter),
        [ANY, ANY, VMEM, ANY],
        [*smem, pltpu.SemaphoreType.DMA((2,))],
        16 * MIB,
        2000000000,
        4 * front * quarter,
    )(live, parent_map, w_v, after(rows_y, rows_x))
    partial = added(partial, row_swap(partial, 1))
    got = after(row_swap(partial.astype(BF), 0), panel_rows)
    root_forward = (partial + got.astype(F32)).astype(BF)

    part, root_piece = call(
        functools.partial(root_transposed_kernel, half),
        (kept(quarter, columns), kept(half, columns)),
        [VMEM, VMEM],
        [pltpu.VMEM((quarter, columns), F32)],
        16 * MIB,
        0,
        0,
    )(root_forward, root_d)
    got = after(leaf_swap(part), rows_d)
    root_mine = added(part[:half], got[half:]).astype(BF)
    root_other = added(part[half:], got[:half]).astype(BF)
    root_rows = jnp.concatenate([root_mine, root_other], 0)

    near = row_swap(root_rows, 1)
    far = row_swap(root_mine, 2)
    total, forward = call(
        functools.partial(leaf_transposed_kernel, (quarter, half)),
        (kept(columns, quarter, F32), stored(quarter + half, columns)),
        [VMEM] * 9,
        [pltpu.VMEM((front, columns), BF), pltpu.VMEM((quarter, columns), BF)],
        16 * MIB,
        2 * front * quarter * columns,
        2 * front * quarter,
    )(leaf_forward, rows_y, rows_x, rows_d, d_v, mask, root_rows, panel_rows, root_piece)
    near = after(near, total)
    near_other = leaf_swap(near)
    far_other = leaf_swap(far)
    total = call(
        functools.partial(own_kernel, (quarter, half)),
        kept(columns, quarter, F32),
        [VMEM] * 4,
        [pltpu.VMEM((quarter, columns), BF)],
        16 * MIB,
        0,
        0,
    )(near, far, total, panel_rows)
    backward = call(
        functools.partial(last_kernel, (quarter, half)),
        stored(quarter + half, columns),
        [VMEM] * 5,
        [pltpu.VMEM((quarter, columns), BF)],
        16 * MIB,
        front * quarter * columns,
        front * quarter,
    )(near_other, far_other, total, panel_rows, root_rows)
    return forward, backward


def on_device(rhs, pivot_inverse, panel, live, parent_map):
    if lax.axis_size("leaf") == 2 and lax.axis_size("row") == 4:
        return two_levels(rhs, pivot_inverse, panel, live, parent_map)
    return deep_tree(rhs, pivot_inverse, panel, live, parent_map)


def solution(mesh):
    in_specs = (P(("leaf", "row"), "col"), P("leaf", "row"), P("leaf", "row"), P(), P())
    out_specs = (P(("leaf", "row"), "col"), P(("leaf", "row"), "col"))
    return jax.shard_map(
        on_device, mesh=mesh, in_specs=in_specs, out_specs=out_specs, check_vma=False
    )
```

```python
import functools

import jax
import jax.numpy as jnp
from jax import lax
from jax.experimental import pallas as pl
from jax.experimental.pallas import tpu as pltpu
from jax.sharding import PartitionSpec as P

F = 2560
E = 1536


def from_partner(block, axis, apart):
    count = lax.axis_size(axis)
    route = []
    for low in range(count):
        high = low | 1 << apart
        if high != low and high < count:
            route += [(low, high), (high, low)]
    return lax.ppermute(block, axis, route)


def doubling(stacked, bit_count, leaf_pos, swapper):
    for bit_no in range(bit_count):
        partner = swapper(stacked, bit_no)
        upper_half = jnp.right_shift(leaf_pos, bit_no) % 2 == 1
        stacked = jnp.where(
            upper_half,
            jnp.concatenate([partner, stacked], 0),
            jnp.concatenate([stacked, partner], 0),
        )
    return stacked


def halving(partial_value, bit_count, leaf_pos, swapper):
    for bit_no in reversed(range(bit_count)):
        halves = partial_value.reshape((2, partial_value.shape[0] // 2) + partial_value.shape[1:])
        upper_half = jnp.right_shift(leaf_pos, bit_no) % 2 == 1
        kept_half = jnp.where(upper_half, halves[1], halves[0])
        sent_half = jnp.where(upper_half, halves[0], halves[1])
        partial_value = kept_half + swapper(sent_half, bit_no)
    return partial_value[0]


def to_front(group_block, row_count):
    count_g, total_rows, row_width = group_block.shape
    piece_rows = total_rows // row_count
    return (
        group_block.reshape(count_g, row_count, piece_rows, row_width)
        .transpose(1, 0, 2, 3)
        .reshape(count_g * total_rows, row_width)
    )


def block_onehot(mapping):
    return (jnp.arange(F // 128, dtype=jnp.int32)[:, None] == mapping[None, :]).astype(jnp.bfloat16)


def pivot_sum(diag_block, quarter_rows):
    return lax.psum_scatter(
        jnp.dot(diag_block, quarter_rows, preferred_element_type=jnp.float32).astype(jnp.bfloat16),
        "row",
        scatter_dimension=0,
        tiled=True,
    ).astype(jnp.float32)


def quarter_swap(values, bit_no):
    return from_partner(values, "leaf", bit_no)


def update_swap(values, bit_no):
    return from_partner(values, "leaf", bit_no)


def parent_swap(values, bit_no):
    return from_partner(values, "leaf", bit_no)


def reduce_swap(values, bit_no):
    return from_partner(values.astype(jnp.bfloat16), "leaf", bit_no).astype(values.dtype)


def deep_tree(rhs, pivot_inverse, panel, live, parent_map):
    leaves = lax.axis_size("leaf")
    row_count = lax.axis_size("row")
    tree_depth = leaves.bit_length() - 1
    leaf_pos = lax.axis_index("leaf")
    row_pos = lax.axis_index("row")
    columns = rhs.shape[1]
    quarter = F // row_count
    parent_blocks = F // 128
    child_blocks = E // 128
    layout = []
    vec_off, piv_off, pan_off, front_base = (0, 0, 0, 0)
    for level_no in range(tree_depth + 1):
        groups = 2**level_no
        layout.append((groups, vec_off, piv_off, pan_off, front_base))
        vec_off += F // (row_count * groups)
        piv_off += F // groups
        pan_off += E // groups
        front_base += leaves // groups
    forward_parts = []
    live_masks = []
    incoming = None
    for level_no in range(tree_depth + 1):
        groups, vec_off, piv_off, pan_off, front_base = layout[level_no]
        piece_rows = F // (row_count * groups)
        panel_rows = E // (row_count * groups)
        inner_pos = leaf_pos % groups
        front_no = jnp.right_shift(leaf_pos, level_no)
        live_rows = lax.dynamic_index_in_dim(live, front_base + front_no, 0, keepdims=False) * 128
        first_row = (row_pos * groups + inner_pos) * piece_rows
        live_mask = (first_row + jnp.arange(piece_rows, dtype=jnp.int32) < live_rows)[:, None]
        live_masks.append(live_mask)
        right_side = rhs[vec_off : vec_off + piece_rows]
        if incoming is not None:
            right_side = (right_side.astype(jnp.float32) - incoming).astype(jnp.bfloat16)
        masked = jnp.where(live_mask, right_side, jnp.zeros_like(right_side))
        quarter_rows = doubling(masked[None], level_no, leaf_pos, quarter_swap).reshape(
            quarter, columns
        )
        diag_block = pivot_inverse[piv_off : piv_off + F // groups]
        if level_no < tree_depth:
            off_block = panel[pan_off : pan_off + E // groups]
            forward_value = pivot_sum(diag_block, quarter_rows)
            update_rows = lax.psum(
                jnp.dot(off_block, quarter_rows, preferred_element_type=jnp.float32), "row"
            ).astype(jnp.bfloat16)
        else:
            forward_value = pivot_sum(diag_block, quarter_rows)
        forward_parts.append(jnp.where(live_mask, forward_value, 0.0).astype(jnp.bfloat16))
        if level_no < tree_depth:
            gathered = doubling(update_rows[None], level_no + 1, leaf_pos, update_swap)
            parent_front = jnp.right_shift(leaf_pos, level_no + 1)
            assembled = jnp.zeros((parent_blocks, 128, columns), jnp.float32)
            for side_no in range(2):
                child_update = to_front(
                    gathered[side_no * groups : (side_no + 1) * groups], row_count
                )
                mapping = lax.dynamic_index_in_dim(
                    parent_map, front_base + 2 * parent_front + side_no, 0, keepdims=False
                )
                assembled = assembled + jnp.einsum(
                    "ke,eab->kab",
                    block_onehot(mapping),
                    child_update.reshape(child_blocks, 128, columns),
                    preferred_element_type=jnp.float32,
                )
            parent_groups = 2 * groups
            parent_rows = F // (row_count * parent_groups)
            parent_first = (row_pos * parent_groups + leaf_pos % parent_groups) * parent_rows
            incoming = lax.dynamic_slice_in_dim(
                assembled.reshape(F, columns), parent_first, parent_rows, 0
            )
    backward_parts = [None] * (tree_depth + 1)
    parent_value = None
    for level_no in reversed(range(tree_depth + 1)):
        groups, vec_off, piv_off, pan_off, front_base = layout[level_no]
        piece_rows = F // (row_count * groups)
        panel_rows = E // (row_count * groups)
        inner_pos = leaf_pos % groups
        front_no = jnp.right_shift(leaf_pos, level_no)
        diag_block = pivot_inverse[piv_off : piv_off + F // groups]
        own_piece = forward_parts[level_no]
        if level_no == tree_depth:
            own_rows = lax.all_gather(own_piece, "row", axis=0, tiled=True)
            partial_value = jnp.einsum(
                "ik,ia->ka", diag_block, own_rows, preferred_element_type=jnp.float32
            )
        else:
            own_rows, parent_gathered = (
                lax.all_gather(own_piece, "row", axis=0, tiled=True),
                lax.all_gather(parent_value, "row", axis=0, tiled=True),
            )
            whole_parent = doubling(parent_gathered[None], level_no + 1, leaf_pos, parent_swap)
            parent_full = to_front(whole_parent, row_count)
            mapping = lax.dynamic_index_in_dim(parent_map, front_base + front_no, 0, keepdims=False)
            taken_rows = jnp.einsum(
                "ke,kab->eab",
                block_onehot(mapping),
                parent_full.reshape(parent_blocks, 128, columns),
                preferred_element_type=jnp.float32,
            ).astype(jnp.bfloat16)
            taken_rows = lax.dynamic_index_in_dim(
                taken_rows.reshape(row_count, groups, panel_rows, columns),
                inner_pos,
                1,
                keepdims=False,
            ).reshape(row_count * panel_rows, columns)
            off_block = panel[pan_off : pan_off + E // groups]
            partial_value = jnp.einsum(
                "ik,ia->ka", diag_block, own_rows, preferred_element_type=jnp.float32
            ) - jnp.einsum("ik,ia->ka", off_block, taken_rows, preferred_element_type=jnp.float32)
        if level_no == 0:
            reduced = partial_value
        else:
            reduced = halving(
                partial_value.reshape(groups, piece_rows, columns), level_no, leaf_pos, reduce_swap
            )
        parent_value = jnp.where(live_masks[level_no], reduced, 0.0).astype(jnp.bfloat16)
        backward_parts[level_no] = parent_value
    return (jnp.concatenate(forward_parts, 0), jnp.concatenate(backward_parts, 0))


B = 128
VMEM = pl.BlockSpec(memory_space=pltpu.VMEM)
ANY = pl.BlockSpec(memory_space=pl.ANY)
BF = jnp.bfloat16
F32 = jnp.float32
MIB = 1024 * 1024


def stored(rows, columns, dtype=BF):
    return jax.ShapeDtypeStruct((rows, columns), dtype)


def kept(rows, columns, dtype=BF):
    return pltpu.VMEM((rows, columns), dtype)


def call(body, out_shape, in_specs, scratch, limit, flops, bytes_moved):
    return pl.pallas_call(
        body,
        out_shape=out_shape,
        in_specs=in_specs,
        out_specs=jax.tree.map(lambda _: VMEM, out_shape, is_leaf=lambda s: hasattr(s, "shape")),
        scratch_shapes=scratch,
        compiler_params=pltpu.CompilerParams(vmem_limit_bytes=limit),
        cost_estimate=pl.CostEstimate(flops=flops, bytes_accessed=bytes_moved, transcendentals=0),
    )


def rows_at(start, size):
    return pl.ds(pl.multiple_of(start, 16), size)


def mm(left, right):
    return jnp.dot(left, right, preferred_element_type=F32)


def row_order(row_pos, leaf_pos):
    return (row_pos, row_pos ^ (1 + leaf_pos), row_pos ^ (2 - leaf_pos), row_pos ^ 3)


def panel_kernel(
    sizes,
    live,
    pmap,
    rhs,
    panel,
    pivot,
    send_near,
    send_rest,
    keep_near,
    keep_rest,
    b_v,
    masked,
    mask,
    w_v,
    d_v,
    c_v,
    live_s,
    pmap_s,
    sems,
):
    quarter, half, parts, update_rows = sizes
    leaf_pos = lax.axis_index("leaf")
    row_pos = lax.axis_index("row")
    gets = [
        pltpu.make_async_copy(live, live_s, sems.at[0]),
        pltpu.make_async_copy(rhs, b_v, sems.at[1]),
        pltpu.make_async_copy(pmap, pmap_s, sems.at[2]),
    ]
    step = update_rows // parts
    for i in range(parts):
        rows = pl.ds(i * step, step)
        gets.append(pltpu.make_async_copy(panel.at[rows], w_v.at[rows], sems.at[3 + i]))
    get = pltpu.make_async_copy(pivot.at[pl.ds(0, 4 * quarter)], d_v, sems.at[3 + parts])
    gets.append(get)
    for get in gets:
        get.start()
    c_v[...] = jnp.zeros_like(c_v)
    gets[0].wait()
    gets[1].wait()
    value = b_v[pl.ds(0, quarter)]
    row = row_pos * quarter + lax.broadcasted_iota(jnp.int32, value.shape, 0)
    alive = row < live_s[leaf_pos] * B
    mask[...] = jnp.where(alive, 1.0, 0.0).astype(BF)
    masked[...] = jnp.where(alive, value, jnp.zeros_like(value))
    right = masked[...]
    gets[2].wait()
    for i in range(parts):
        gets[3 + i].wait()
        product = mm(w_v[pl.ds(i * step, step)], right).astype(BF)
        for e in range(step // B):
            block = pmap_s[leaf_pos, i * (step // B) + e]
            c_v[pl.ds(pl.multiple_of(block * B, B), B)] = product[e * B : (e + 1) * B]
    for near_out, rest, side in (
        (send_near, send_rest, 1 - leaf_pos),
        (keep_near, keep_rest, leaf_pos),
    ):
        near = (row_pos ^ (1 + side)) * quarter
        mine, other = side * half, (1 - side) * half
        near_out[pl.ds(0, half)] = c_v[rows_at(near + mine, half)]
        near_out[pl.ds(half, half)] = c_v[rows_at(near + other, half)]
        rest[pl.ds(0, half)] = c_v[rows_at((row_pos ^ 3) * quarter + mine, half)]
        rest[pl.ds(half, half)] = c_v[rows_at(row_pos * quarter + mine, half)]
    gets[3 + parts].wait()


def leaf_pivot_kernel(sizes, masked, d_v, pivot, after, *outs_and_scratch):
    quarter, rows = sizes
    *outs, root_d, sem = outs_and_scratch
    get = pltpu.make_async_copy(pivot.at[pl.ds(4 * quarter, rows)], root_d, sem)
    get.start()
    order = row_order(lax.axis_index("row"), lax.axis_index("leaf"))
    right = masked[...]
    for k in (3, 1, 2, 0):
        product = mm(d_v[rows_at(order[k] * quarter, quarter)], right)
        outs[k][...] = product.astype(BF)
    get.wait()


def scatter_kernel(sizes, live, pmap, w_v, after, out, live_s, pmap_s, sems):
    quarter, update_rows = sizes
    leaf_pos = lax.axis_index("leaf")
    row_pos = lax.axis_index("row")
    gets = [
        pltpu.make_async_copy(live, live_s, sems.at[0]),
        pltpu.make_async_copy(pmap, pmap_s, sems.at[1]),
    ]
    for get in gets:
        get.start()
    per_row = quarter // B
    out[...] = jnp.zeros_like(out)
    for get in gets:
        get.wait()
    column = row_pos * quarter + lax.broadcasted_iota(jnp.int32, (B, quarter), 1)
    alive = column < live_s[leaf_pos] * B
    for e in range(update_rows // B):
        value = w_v[pl.ds(e * B, B)]
        block = pmap_s[leaf_pos, e]
        away = (block // per_row) ^ row_pos
        slot = jnp.where(away == 1 + leaf_pos, 1, jnp.where(away == 2 - leaf_pos, 2, away))
        at = (slot * per_row + block % per_row) * B
        out[pl.ds(pl.multiple_of(at, B), B)] = jnp.where(alive, value, jnp.zeros_like(value))


def root_pivot_kernel(sizes, mine, yours, other_mine, other_yours, d_v, out, q_v):
    half = sizes
    leaf_pos = lax.axis_index("leaf")
    for own, other, at in ((mine, other_yours, leaf_pos), (yours, other_mine, 1 - leaf_pos)):
        value = own[...].astype(F32) + other[...].astype(F32)
        q_v[rows_at(at * half, half)] = (-value).astype(BF)
    out[...] = mm(d_v[pl.ds(0, 4 * half)], q_v[...]).astype(BF)


def root_transposed_kernel(sizes, y, d_v, out, piece, s_v):
    half = sizes
    leaf_pos = lax.axis_index("leaf")
    row_pos = lax.axis_index("row")
    piece[...] = y[rows_at(row_pos * half, half)]
    s_v[...] = mm(y[...].T, d_v[pl.ds(0, 4 * half)]).T
    out[pl.ds(0, half)] = s_v[rows_at(leaf_pos * half, half)].astype(BF)
    out[pl.ds(half, half)] = s_v[rows_at((1 - leaf_pos) * half, half)].astype(BF)


def put(target, slot, half, source, order):
    for k, side in enumerate(order):
        at = 2 * slot * half + side * half
        target[rows_at(at, half)] = source[pl.ds(k * half, half)]


def leaf_transposed_kernel(
    sizes,
    own,
    rows_y,
    rows_x,
    rows_d,
    d_v,
    mask,
    root_rows,
    panel_rows,
    root_piece,
    total,
    forward,
    y_v,
    s_v,
):
    quarter, half = sizes
    row_pos = lax.axis_index("row")
    leaf_pos = lax.axis_index("leaf")
    order = row_order(row_pos, leaf_pos)
    forward[pl.ds(0, quarter)] = own[...]
    forward[pl.ds(quarter, half)] = root_piece[...]
    for k, part in enumerate((own, rows_x, rows_y, rows_d)):
        y_v[rows_at(order[k] * quarter, quarter)] = part[...]
    value = mm(y_v[...].T, d_v[pl.ds(0, 4 * quarter)])
    value = jnp.where(mask[...].astype(F32).T > 0.0, value, 0.0)
    put(s_v, 0, half, root_rows, (leaf_pos, 1 - leaf_pos))
    total[...] = value - mm(s_v[...].T, panel_rows[pl.ds(0, quarter)])


def own_kernel(sizes, near, far, total, panel_rows, out, s_v):
    quarter, half = sizes
    leaf_pos = lax.axis_index("leaf")
    put(s_v, 0, half, near, (leaf_pos, 1 - leaf_pos))
    value = total[...] - mm(s_v[...].T, panel_rows[pl.ds(2 * quarter, quarter)])
    rows = rows_at(3 * quarter + leaf_pos * half, half)
    out[...] = value - mm(far[...].T, panel_rows[rows])


def last_kernel(sizes, near, far, total, panel_rows, root_rows, out, s_v):
    quarter, half = sizes
    leaf_pos = lax.axis_index("leaf")
    put(s_v, 0, half, near, (1 - leaf_pos, leaf_pos))
    value = total[...] - mm(s_v[...].T, panel_rows[pl.ds(quarter, quarter)])
    rows = rows_at(3 * quarter + (1 - leaf_pos) * half, half)
    value = value - mm(far[...].T, panel_rows[rows])
    out[pl.ds(0, quarter)] = value.T.astype(BF)
    out[pl.ds(quarter, half)] = root_rows[pl.ds(0, half)]


def leaf_swap(value):
    return lax.ppermute(value, "leaf", [(0, 1), (1, 0)])


def row_swap(value, phase):
    route = []
    for leaf in range(2):
        apart = (1 + leaf, 2 - leaf, 3)[phase]
        route += [(4 * leaf + r, 4 * leaf + (r ^ apart)) for r in range(4)]
    return lax.ppermute(value, ("leaf", "row"), route)


def added(left, right):
    return left.astype(F32) + right.astype(F32)


def two_levels(rhs, pivot_inverse, panel, live, parent_map):
    columns = rhs.shape[1]
    quarter = pivot_inverse.shape[1]
    half = quarter // 2
    front = 4 * quarter
    updates = parent_map.shape[1] * B
    after = lambda value, other: lax.optimization_barrier((value, other))[0]
    smem = [pltpu.SMEM(live.shape, jnp.int32), pltpu.SMEM(parent_map.shape, jnp.int32)]

    parts = 4 if updates % (4 * B) == 0 else 1
    send_near, send_rest, keep_near, keep_rest, b_v, masked, mask, w_v, d_v = call(
        functools.partial(panel_kernel, (quarter, half, parts, updates)),
        (
            kept(quarter, columns),
            kept(quarter, columns),
            kept(quarter, columns),
            kept(quarter, columns),
            kept(quarter + half, columns),
            kept(quarter, columns),
            kept(quarter, columns),
            kept(updates, quarter),
            kept(front, quarter),
        ),
        [ANY] * 5,
        [pltpu.VMEM((front, columns), BF), *smem, pltpu.SemaphoreType.DMA((4 + parts,))],
        58_700_000,
        2 * updates * quarter * columns,
        2 * updates * quarter,
    )(live, parent_map, rhs, panel, pivot_inverse)
    away_near = added(keep_near, leaf_swap(send_near)).astype(BF)
    rest = added(keep_rest, leaf_swap(send_rest))
    away_far = rest[:half].astype(BF)
    from_far = row_swap(away_far, 2)
    from_near = row_swap(away_near, 0)

    *pieces, root_d = call(
        functools.partial(leaf_pivot_kernel, (quarter, 4 * half)),
        (*(kept(quarter, columns),) * 4, kept(4 * half, quarter)),
        [VMEM, VMEM, ANY, ANY],
        [pltpu.SemaphoreType.DMA],
        49_500_000,
        2 * front * quarter * columns,
        2 * front * quarter,
    )(masked, d_v, pivot_inverse, away_near)
    from_near = after(from_near, pieces[0])
    leaf_forward = pieces[0].astype(F32)
    for phase in (0, 2, 1):
        leaf_forward = leaf_forward + row_swap(pieces[1 + phase], phase).astype(F32)
    leaf_forward = jnp.where(mask > 0, leaf_forward, 0.0).astype(BF)
    rows_y = row_swap(leaf_forward, 1)
    rows_x = row_swap(leaf_forward, 0)
    rows_d = row_swap(rows_y, 0)

    term = rest[half:] + from_far.astype(F32) - b_v[quarter:].astype(F32)
    from_near = from_near.astype(F32)
    negated_mine = (from_near[:half] + term).astype(BF)
    negated_yours = from_near[half:].astype(BF)
    other_yours = leaf_swap(negated_yours)
    other_mine = leaf_swap(negated_mine)

    partial = call(
        functools.partial(root_pivot_kernel, half),
        kept(4 * half, columns),
        [VMEM] * 5,
        [pltpu.VMEM((quarter, columns), BF)],
        16 * MIB,
        0,
        0,
    )(negated_mine, negated_yours, other_mine, other_yours, root_d)
    panel_rows = call(
        functools.partial(scatter_kernel, (quarter, updates)),
        kept(front, quarter),
        [ANY, ANY, VMEM, ANY],
        [*smem, pltpu.SemaphoreType.DMA((2,))],
        16 * MIB,
        2000000000,
        4 * front * quarter,
    )(live, parent_map, w_v, after(rows_y, rows_x))
    partial = added(partial, row_swap(partial, 1))
    got = after(row_swap(partial.astype(BF), 0), panel_rows)
    root_forward = (partial + got.astype(F32)).astype(BF)

    part, root_piece = call(
        functools.partial(root_transposed_kernel, half),
        (kept(quarter, columns), kept(half, columns)),
        [VMEM, VMEM],
        [pltpu.VMEM((quarter, columns), F32)],
        16 * MIB,
        0,
        0,
    )(root_forward, root_d)
    got = after(leaf_swap(part), rows_d)
    root_mine = added(part[:half], got[half:]).astype(BF)
    root_other = added(part[half:], got[:half]).astype(BF)
    root_rows = jnp.concatenate([root_mine, root_other], 0)

    near = row_swap(root_rows, 1)
    far = row_swap(root_mine, 2)
    total, forward = call(
        functools.partial(leaf_transposed_kernel, (quarter, half)),
        (kept(columns, quarter, F32), stored(quarter + half, columns)),
        [VMEM] * 9,
        [pltpu.VMEM((front, columns), BF), pltpu.VMEM((quarter, columns), BF)],
        16 * MIB,
        2 * front * quarter * columns,
        2 * front * quarter,
    )(leaf_forward, rows_y, rows_x, rows_d, d_v, mask, root_rows, panel_rows, root_piece)
    near = after(near, total)
    near_other = leaf_swap(near)
    far_other = leaf_swap(far)
    total = call(
        functools.partial(own_kernel, (quarter, half)),
        kept(columns, quarter, F32),
        [VMEM] * 4,
        [pltpu.VMEM((quarter, columns), BF)],
        16 * MIB,
        0,
        0,
    )(near, far, total, panel_rows)
    backward = call(
        functools.partial(last_kernel, (quarter, half)),
        stored(quarter + half, columns),
        [VMEM] * 5,
        [pltpu.VMEM((quarter, columns), BF)],
        16 * MIB,
        front * quarter * columns,
        front * quarter,
    )(near_other, far_other, total, panel_rows, root_rows)
    return forward, backward


def on_device(rhs, pivot_inverse, panel, live, parent_map):
    if lax.axis_size("leaf") == 2 and lax.axis_size("row") == 4:
        return two_levels(rhs, pivot_inverse, panel, live, parent_map)
    return deep_tree(rhs, pivot_inverse, panel, live, parent_map)


def solution(mesh):
    in_specs = (P(("leaf", "row"), "col"), P("leaf", "row"), P("leaf", "row"), P(), P())
    out_specs = (P(("leaf", "row"), "col"), P(("leaf", "row"), "col"))
    return jax.shard_map(
        on_device, mesh=mesh, in_specs=in_specs, out_specs=out_specs, check_vma=False
    )
```
